512 devices in a mesh: seq: 32 (over z, x), section: 8 (over y_lo, core), dp: 2 (over y_hi).
Axes of the slice: x: 4, y: 8 (y_hi: 2, y_lo: 4; y = y_hi * 4 + y_lo), z: 8, core: 2. Of those that a mesh axis runs over, the one named last changes fastest.
Arguments:
- queries: bfloat16 [8, 4096, 3584], P('section', 'seq', 'dp'), may hold values from -5 to 5
- key_vectors: bfloat16 [8, 4096, 3584], P('section', 'seq', 'dp'), may hold values from -5 to 5
- value_vectors: bfloat16 [8, 4096, 3584], P('section', 'seq', 'dp'), may hold values from -6 to 6
- out_grad: bfloat16 [8, 4096, 3584], P('section', 'seq', 'dp'), may hold values from -6 to 6
- doc_lengths: int32 [8], replicated, may hold values from 1 to 1536, 4096 in all
Outputs:
- query_grad: bfloat16 [8, 4096, 3584], P('section', 'seq', 'dp')
- key_grad: bfloat16 [8, 4096, 3584], P('section', 'seq', 'dp')
- value_grad: bfloat16 [8, 4096, 3584], P('section', 'seq', 'dp')
The draws below stay inside these ranges and needn't reach their ends.
Inputs may be any that keep to these rules, and one draw needn't show every extreme that they name: `doc_lengths`: the 8 lengths sum to 4096; the longest is exactly 1536.
All inputs are finite; a program needn't handle non-finite values.
Results may differ from the reference program's by a relative error of at most 0.024.
Values may be sent and summed in bfloat16 or wider, within the bound.
A program may use at most 192 MiB of HBM per device.

```python
import math
import jax
import jax.numpy as jnp
import numpy as np
from jax import lax

HEADS = 16
HEAD = 224
DOCS = 8
INNER = 3584
LENGTH = 4096
SECTIONS = 8
LONGEST = 1536


def draw_queries(key, part):
    key = jax.random.fold_in(key, 7)
    values = jnp.clip(jax.random.normal(key, (SECTIONS, LENGTH, INNER), jnp.float32), -5.0, 5.0)
    return values.astype(jnp.bfloat16)


def draw_key_vectors(key, part):
    key = jax.random.fold_in(key, 9)
    values = jnp.clip(jax.random.normal(key, (SECTIONS, LENGTH, INNER), jnp.float32), -5.0, 5.0)
    return values.astype(jnp.bfloat16)


def levels(stream_key, extent, cuts, low, high):
    def one(dim, shards_of):
        draws = jax.random.uniform(jax.random.fold_in(jax.random.fold_in(stream_key, 6), dim), (shards_of,), jnp.float32, low / len(cuts), high / len(cuts))
        return jnp.repeat(jnp.exp(draws), extent[dim] // shards_of).reshape((-1,) + (1,) * (len(extent) - dim - 1))

    level = one(*cuts[0])
    for cut in cuts[1:]:
        level = level * one(*cut)
    return level


def profile(count, total, bound, lean):
    portions = [(1 << 20) // math.isqrt(grade ** lean) + 1 for grade in range(2, count + 1)]
    spare, given = total - bound - (count - 1), [1] * (count - 1)
    while spare > 0:
        movable = [i for i in range(count - 1) if given[i] < bound]
        mass, remaining = sum([portions[i] for i in movable]), spare
        for i in movable:
            addition = min(bound - given[i], max(1, remaining * portions[i] // mass), spare)
            given[i] = given[i] + addition
            spare = spare - addition
    return np.array([bound] + given)


def ragged(key, count, total, limit, skew):
    if count == 2:
        one = jax.random.randint(key, (), max(1, total - limit), min(limit, total - 1) + 1)
        return jnp.stack([one, total - one])
    tallies = jnp.asarray(profile(count, total, limit, skew), jnp.int32)
    twos = (count - 1) // 2
    giver, receiver = tallies[1:1 + 2 * twos:2], tallies[2:2 + 2 * twos:2]
    room = jnp.minimum(giver - 1, limit - receiver)
    moved = jax.random.randint(jax.random.fold_in(key, 1), (twos,), 0, 1 << 20) % (room + 1)
    tallies = tallies.at[1:1 + 2 * twos:2].set(giver - moved).at[2:2 + 2 * twos:2].set(receiver + moved)
    return tallies[jax.random.permutation(jax.random.fold_in(key, 2), count)]


def bell_draw(own_key, shape, deviation, bound, shards=(), kind=jnp.bfloat16):
    values = deviation * jax.random.normal(own_key, shape, jnp.float32)
    if shards:
        values = values * levels(own_key, shape, shards, -0.22, 0.18)
    return jnp.clip(values, -bound, bound).astype(kind)


def setup_inputs(seed: int = 0) -> dict:
    keys = jax.random.split(jax.random.key(seed), 6)
    return {
        "queries": draw_queries(jax.random.fold_in(keys[5], 71), 0),
        "key_vectors": draw_key_vectors(jax.random.fold_in(keys[5], 71), 0),
        "value_vectors": bell_draw(keys[2], (SECTIONS, LENGTH, INNER), 1.0, 6.0, ((0, 8), (1, 32), (2, 2))),
        "out_grad": bell_draw(keys[3], (SECTIONS, LENGTH, INNER), 1.0, 6.0, ((0, 8), (1, 32), (2, 2))),
        "doc_lengths": ragged(keys[4], DOCS, LENGTH, LONGEST, 2).astype(jnp.int32),
    }


def head_grads(query_head, key_head, value_head, cot_head, allowed):
    scaling = HEAD ** -0.5
    scores = jnp.dot(query_head, key_head.T, preferred_element_type=jnp.float32) * scaling
    scores = jnp.where(allowed, scores, -jnp.inf)
    row_max = jnp.max(scores, axis=1, keepdims=True)
    exponent = jnp.exp(scores - row_max)
    weights = exponent / jnp.sum(exponent, axis=1, keepdims=True)
    rounded = weights.astype(jnp.bfloat16)
    attended = jnp.dot(rounded, value_head, preferred_element_type=jnp.float32).astype(jnp.bfloat16)
    row_dot = jnp.sum(cot_head.astype(jnp.float32) * attended.astype(jnp.float32), axis=1, keepdims=True)
    prob_grad = jnp.dot(cot_head, value_head.T, preferred_element_type=jnp.float32)
    score_grad = (weights * (prob_grad - row_dot) * scaling).astype(jnp.bfloat16)
    query_part = jnp.dot(score_grad, key_head, preferred_element_type=jnp.float32).astype(jnp.bfloat16)
    key_part = jnp.dot(score_grad.T, query_head, preferred_element_type=jnp.float32).astype(jnp.bfloat16)
    value_part = jnp.dot(rounded.T, cot_head, preferred_element_type=jnp.float32).astype(jnp.bfloat16)
    return query_part, key_part, value_part


def split_heads(matrix):
    return matrix.reshape(LENGTH, HEADS, HEAD).transpose(1, 0, 2)


def join_heads(stacked):
    return stacked.transpose(1, 0, 2).reshape(LENGTH, INNER)


def reference(queries, key_vectors, value_vectors, out_grad, doc_lengths):
    positions = jnp.arange(LENGTH, dtype=jnp.int32)
    bounds = jnp.cumsum(doc_lengths)
    doc_index = jnp.sum((positions[:, None] >= bounds[None, :]).astype(jnp.int32), axis=1)
    allowed = (doc_index[:, None] == doc_index[None, :]) & (positions[:, None] >= positions[None, :])

    def one_section(carry, members):
        query_rows, key_rows, value_rows, cot_rows = members

        def per_head(parts):
            return head_grads(parts[0], parts[1], parts[2], parts[3], allowed)

        query_part, key_part, value_part = lax.map(
            per_head, (split_heads(query_rows), split_heads(key_rows), split_heads(value_rows), split_heads(cot_rows)))
        return carry, (join_heads(query_part), join_heads(key_part), join_heads(value_part))

    begin = jnp.zeros((), jnp.float32)
    unused, (query_grad, key_grad, value_grad) = lax.scan(
        one_section, begin, (queries, key_vectors, value_vectors, out_grad))
    return (query_grad, key_grad, value_grad)
```

```python
import functools

import jax
import jax.numpy as jnp
from jax import lax
from jax.experimental import pallas as pl
from jax.experimental.pallas import tpu as pltpu
from jax.sharding import PartitionSpec as P

HEAD = 224
ZN, XN = 8, 4
SCALE = HEAD ** (-0.5)
NEG = -1e30
LOW = -1e20
TQ = 256
TK = 256
ITEMS = ((0, 3), (1, 3), (2, 3), (0, 2), (1, 2), (2, 2), (3, 0), (3, 1), (3, 2), (2, 0), (2, 1))


class Docs:
    def __init__(self, lengths):
        self.bounds = []
        total = jnp.int32(0)
        for d in range(8):
            total = total + lengths[d]
            self.bounds.append(total)

    def start(self, t):
        r = jnp.int32(0)
        for b in self.bounds[:7]:
            r = jnp.where(b <= t, b, r)
        return r

    def end(self, t):
        r = jnp.int32(4096)
        for b in reversed(self.bounds):
            r = jnp.where(b > t, b, r)
        return r

    def row_start(self, pos):
        r = jnp.zeros_like(pos)
        for b in self.bounds[:7]:
            r = jnp.where(pos >= b, b, r)
        return r

    def case(self, t):
        before = t - self.start(t - 1)
        after = self.end(t - 1) - t
        keys = after > 1024
        return keys, (before > 1024) & jnp.logical_not(keys)


def slots(docs, z):
    lk, lq = docs.case(z * 512)
    rk, rq = docs.case(z * 512 + 512)
    lm = jnp.logical_not(lk | lq)
    rm = jnp.logical_not(rk | rq)
    q_ids = (z, z + 1, jnp.where(rq, z + 1, z + 2), z)
    k_ids = (z, z - 1, jnp.where(lk, z - 1, z - 2), z)
    valid = {
        (0, 3): True,
        (1, 3): jnp.logical_not(rk),
        (2, 3): rm,
        (0, 2): lk,
        (1, 2): lk & jnp.logical_not(rk),
        (2, 2): (lk & rm) | (rq & lm),
        (3, 0): True,
        (3, 1): jnp.logical_not(lq),
        (3, 2): lm,
        (2, 0): rq,
        (2, 1): rq & jnp.logical_not(lq),
    }
    return q_ids, k_ids, valid


NT = (((1,), (1,)), ((), ()))


def for_tiles(docs, z, body):
    q_ids, k_ids, valid = slots(docs, z)
    for qs, ks in ITEMS:
        qid, kid, ok = q_ids[qs], k_ids[ks], valid[(qs, ks)]
        use = (qid < ZN) & (kid >= 0) & ok
        for qt in range(512 // TQ):
            q0 = qid * 512 + qt * TQ
            first = docs.start(q0)
            for kt in range(512 // TK):
                k0 = kid * 512 + kt * TK
                k1 = k0 + TK - 1
                hit = use & (k0 <= q0 + TQ - 1) & ((k1 >= q0) | (k1 >= first))

                @pl.when(hit)
                def _():
                    body(qs, ks, qt, kt, q0, k0)


def masked_scores(docs, k, q, q0, k0):
    s = lax.dot_general(k, q, NT, preferred_element_type=jnp.float32) * SCALE
    kpos = k0 + lax.broadcasted_iota(jnp.int32, (TK, 1), 0)
    qpos = q0 + lax.broadcasted_iota(jnp.int32, (1, TQ), 1)
    qstart = docs.row_start(qpos)
    return jnp.where((kpos <= qpos) & (kpos >= qstart), s, NEG)


def stats_kernel(len_ref, q_ref, do_ref, k_ref, v_ref, st_ref):
    z = lax.axis_index("seq") // XN
    docs = Docs(len_ref)
    st_ref[0:4, :] = jnp.full((4, 512), LOW, jnp.float32)
    st_ref[4:16, :] = jnp.zeros((12, 512), jnp.float32)

    def body(qs, ks, qt, kt, q0, k0):
        rows, cols = pl.ds(qt * TQ, TQ), pl.ds(kt * TK, TK)
        q, do = q_ref[qs, rows, :], do_ref[qs, rows, :]
        k, v = k_ref[ks, cols, :], v_ref[ks, cols, :]
        s = masked_scores(docs, k, q, q0, k0)
        dp = lax.dot_general(v, do, NT, preferred_element_type=jnp.float32)
        old = st_ref[qs : qs + 1, rows]
        new = jnp.maximum(old, jnp.max(s, axis=0, keepdims=True))
        p = jnp.exp(s - new)
        alpha = jnp.exp(old - new)
        st_ref[qs : qs + 1, rows] = new
        st_ref[4 + qs : 5 + qs, rows] = st_ref[4 + qs : 5 + qs, rows] * alpha + jnp.sum(p, axis=0, keepdims=True)
        st_ref[8 + qs : 9 + qs, rows] = st_ref[8 + qs : 9 + qs, rows] * alpha + jnp.sum(p * dp, axis=0, keepdims=True)

    for_tiles(docs, z, body)


def combine_stats(docs, z, mine, up1, up2, down1, down2):
    lk, lq = docs.case(z * 512)
    rk, rq = docs.case(z * 512 + 512)
    lm = jnp.logical_not(lk | lq)
    rm = jnp.logical_not(rk | rq)
    bk, bq = docs.case(z * 512 - 512)
    bm = jnp.logical_not(bk | bq) & (z >= 2)

    def part(ref, slot, use=None):
        m, l, d = ref[slot : slot + 1, :], ref[4 + slot : 5 + slot, :], ref[8 + slot : 9 + slot, :]
        if use is not None:
            m = jnp.where(use, m, LOW)
            l = jnp.where(use, l, 0.0)
            d = jnp.where(use, d, 0.0)
        return m, l, d

    groups = (
        (part(mine, 0), part(down1, 1, z >= 1), part(down2, 2, bm)),
        (part(mine, 1), part(up1, 0, z + 1 < ZN), part(down1, 2, lm & (z >= 1))),
        (part(mine, 2), part(up2, 0, rm & (z + 2 < ZN)), part(up1, 1, rm & (z + 1 < ZN)), part(up1, 3, rq & (z + 1 < ZN))),
        (part(mine, 3), part(down1, 2, lq & (z >= 1))),
    )
    out = []
    for parts in groups:
        m = functools.reduce(jnp.maximum, [p[0] for p in parts])
        l = sum(p[1] * jnp.exp(p[0] - m) for p in parts)
        d = sum(p[2] * jnp.exp(p[0] - m) for p in parts)
        inv = jnp.where(l > 0.0, 1.0 / jnp.where(l > 0.0, l, 1.0), 0.0)
        out.append((m, inv, d * inv))
    return out


def grads_kernel(len_ref, q_ref, do_ref, k_ref, v_ref, mine, up1, up2, down1, down2,
                 dq_ref, dk_ref, dv_ref, stat, kt_ref, dqt, dk_acc, dv_acc):
    z = lax.axis_index("seq") // XN
    docs = Docs(len_ref)
    for qs, (m, inv, d) in enumerate(combine_stats(docs, z, mine, up1, up2, down1, down2)):
        stat[qs : qs + 1, :] = m
        stat[4 + qs : 5 + qs, :] = inv
        stat[8 + qs : 9 + qs, :] = d
    for i in range(4):
        kt_ref[i] = k_ref[i].T
    dqt[...] = jnp.zeros_like(dqt)
    dk_acc[...] = jnp.zeros_like(dk_acc)
    dv_acc[...] = jnp.zeros_like(dv_acc)

    def body(qs, ks, qt, kt, q0, k0):
        rows, cols = pl.ds(qt * TQ, TQ), pl.ds(kt * TK, TK)
        q, do = q_ref[qs, rows, :], do_ref[qs, rows, :]
        k, v = k_ref[ks, cols, :], v_ref[ks, cols, :]
        s = masked_scores(docs, k, q, q0, k0)
        dp = lax.dot_general(v, do, NT, preferred_element_type=jnp.float32)
        p = jnp.exp(s - stat[qs : qs + 1, rows]) * stat[4 + qs : 5 + qs, rows]
        ds = (p * (dp - stat[8 + qs : 9 + qs, rows])).astype(jnp.bfloat16)
        dv_acc[ks, cols, :] += jnp.dot(p.astype(jnp.bfloat16), do, preferred_element_type=jnp.float32)
        dk_acc[ks, cols, :] += jnp.dot(ds, q, preferred_element_type=jnp.float32)
        dqt[qs, :, rows] += jnp.dot(kt_ref[ks, :, cols], ds, preferred_element_type=jnp.float32)

    for_tiles(docs, z, body)
    for i in range(4):
        dq_ref[i] = (dqt[i] * SCALE).T.astype(jnp.bfloat16)
        dk_ref[i] = (dk_acc[i] * SCALE).astype(jnp.bfloat16)
        dv_ref[i] = dv_acc[i].astype(jnp.bfloat16)


VM = pl.BlockSpec(memory_space=pltpu.VMEM)
SM = pl.BlockSpec(memory_space=pltpu.SMEM)
BIG = pltpu.CompilerParams(vmem_limit_bytes=48 * 1024 * 1024)


def shards(queries, key_vectors, value_vectors, out_grad, doc_lengths):
    rows, width = queries.shape[1], queries.shape[2]
    idx = lax.axis_index("seq")
    z = idx // XN
    docs = Docs(doc_lengths)
    x_groups = [[XN * a + b for b in range(XN)] for a in range(ZN)]
    n = ZN * XN

    def move(value, dz):
        return lax.ppermute(value, "seq", [(i, (i + XN * dz) % n) for i in range(n)])

    stacked = jnp.concatenate([queries, out_grad, key_vectors, value_vectors], axis=0)
    shaped = stacked.reshape(4, rows, XN, 2, HEAD).transpose(2, 3, 0, 1, 4)
    got = lax.all_to_all(shaped, "seq", split_axis=0, concat_axis=0, axis_index_groups=x_groups, tiled=True)
    got = got.transpose(1, 2, 0, 3, 4).reshape(2, 4, XN * rows, HEAD)
    a_q, a_k = got[0, 0:2], got[0, 2:4]
    b_q, b_k = got[1, 0:2], got[1, 2:4]
    lk, lq = docs.case(z * 512)
    rk, rq = docs.case(z * 512 + 512)
    back1 = move(a_q, -1)
    fore1 = move(b_k, 1)
    back2 = move(jnp.where(lq, b_q, back1), -1)
    fore2 = move(jnp.where(rk, a_k, fore1), 1)
    qs = jnp.stack([a_q[0], back1[0], back2[0], b_q[0]])
    dos = jnp.stack([a_q[1], back1[1], back2[1], b_q[1]])
    ks = jnp.stack([b_k[0], fore1[0], fore2[0], a_k[0]])
    vs = jnp.stack([b_k[1], fore1[1], fore2[1], a_k[1]])
    mine = pl.pallas_call(
        stats_kernel,
        out_shape=jax.ShapeDtypeStruct((16, 512), jnp.float32),
        in_specs=[SM] + [VM] * 4,
        out_specs=VM,
        compiler_params=BIG,
    )(doc_lengths, qs, dos, ks, vs)
    up1, up2 = move(mine, -1), move(mine, -2)
    down1, down2 = move(mine, 1), move(mine, 2)
    block = jax.ShapeDtypeStruct((4, 512, HEAD), jnp.bfloat16)
    dq, dk, dv = pl.pallas_call(
        grads_kernel,
        out_shape=(block, block, block),
        in_specs=[SM] + [VM] * 9,
        out_specs=(VM, VM, VM),
        scratch_shapes=[
            pltpu.VMEM((16, 512), jnp.float32),
            pltpu.VMEM((4, HEAD, 512), jnp.bfloat16),
            pltpu.VMEM((4, HEAD, 512), jnp.float32),
            pltpu.VMEM((4, 512, HEAD), jnp.float32),
            pltpu.VMEM((4, 512, HEAD), jnp.float32),
        ],
        compiler_params=BIG,
    )(doc_lengths, qs, dos, ks, vs, mine, up1, up2, down1, down2)
    kv = jnp.stack([dk, dv])
    f32 = jnp.float32

    def plus(base, term, use):
        return (base.astype(f32) + jnp.where(use, term.astype(f32), 0.0)).astype(jnp.bfloat16)

    lm = jnp.logical_not(lk | lq)
    rm = jnp.logical_not(rk | rq)
    q2 = move(dq[2], 1)
    k2 = move(kv[:, 2], -1)
    q_first = plus(dq[1], q2, lm & (z >= 1))
    q_b = plus(dq[3], q2, lq & (z >= 1))
    k_first = plus(kv[:, 1], k2, rm & (z < ZN - 1))
    k_a = plus(kv[:, 3], k2, rk & (z < ZN - 1))
    q_a = plus(dq[0], move(q_first, 1), z >= 1)
    k_b = plus(kv[:, 0], move(k_first, -1), z < ZN - 1)
    out = jnp.stack([jnp.stack([q_a, k_a[0], k_a[1]]), jnp.stack([q_b, k_b[0], k_b[1]])])
    out = out.reshape(2, 3, XN, rows, HEAD).transpose(2, 0, 1, 3, 4)
    home = lax.all_to_all(out, "seq", split_axis=0, concat_axis=0, axis_index_groups=x_groups, tiled=True)
    home = home.transpose(2, 3, 0, 1, 4).reshape(3, 1, rows, width)
    return home[0], home[1], home[2]


def solution(mesh):
    spec = P("section", "seq", "dp")
    return jax.shard_map(
        shards,
        mesh=mesh,
        in_specs=(spec, spec, spec, spec, P()),
        out_specs=(spec, spec, spec),
        check_vma=False,
    )
```

```python
import functools

import jax
import jax.numpy as jnp
from jax import lax
from jax.experimental import pallas as pl
from jax.experimental.pallas import tpu as pltpu
from jax.sharding import PartitionSpec as P

HEAD = 224
ZN, XN = 8, 4
SCALE = HEAD ** (-0.5)
NEG = -1e30
LOW = -1e20
TQ = 256
TK = 256
ITEMS = ((0, 3), (1, 3), (2, 3), (0, 2), (1, 2), (2, 2), (3, 0), (3, 1), (3, 2), (2, 0), (2, 1))


class Docs:
    def __init__(self, lengths):
        self.bounds = []
        total = jnp.int32(0)
        for d in range(8):
            total = total + lengths[d]
            self.bounds.append(total)

    def start(self, t):
        r = jnp.int32(0)
        for b in self.bounds[:7]:
            r = jnp.where(b <= t, b, r)
        return r

    def end(self, t):
        r = jnp.int32(4096)
        for b in reversed(self.bounds):
            r = jnp.where(b > t, b, r)
        return r

    def row_start(self, pos):
        r = jnp.zeros_like(pos)
        for b in self.bounds[:7]:
            r = jnp.where(pos >= b, b, r)
        return r

    def case(self, t):
        before = t - self.start(t - 1)
        after = self.end(t - 1) - t
        keys = after > 1024
        return keys, (before > 1024) & jnp.logical_not(keys)


def slots(docs, z):
    lk, lq = docs.case(z * 512)
    rk, rq = docs.case(z * 512 + 512)
    lm = jnp.logical_not(lk | lq)
    rm = jnp.logical_not(rk | rq)
    q_ids = (z, z + 1, jnp.where(rq, z + 1, z + 2), z)
    k_ids = (z, z - 1, jnp.where(lk, z - 1, z - 2), z)
    valid = {
        (0, 3): True,
        (1, 3): jnp.logical_not(rk),
        (2, 3): rm,
        (0, 2): lk,
        (1, 2): lk & jnp.logical_not(rk),
        (2, 2): (lk & rm) | (rq & lm),
        (3, 0): True,
        (3, 1): jnp.logical_not(lq),
        (3, 2): lm,
        (2, 0): rq,
        (2, 1): rq & jnp.logical_not(lq),
    }
    return q_ids, k_ids, valid


NT = (((1,), (1,)), ((), ()))


def for_tiles(docs, z, body):
    q_ids, k_ids, valid = slots(docs, z)
    for qs, ks in ITEMS:
        qid, kid, ok = q_ids[qs], k_ids[ks], valid[(qs, ks)]
        use = (qid < ZN) & (kid >= 0) & ok
        for qt in range(512 // TQ):
            q0 = qid * 512 + qt * TQ
            first = docs.start(q0)
            for kt in range(512 // TK):
                k0 = kid * 512 + kt * TK
                k1 = k0 + TK - 1
                hit = use & (k0 <= q0 + TQ - 1) & ((k1 >= q0) | (k1 >= first))

                @pl.when(hit)
                def _():
                    body(qs, ks, qt, kt, q0, k0)


def masked_scores(docs, k, q, q0, k0):
    s = lax.dot_general(k, q, NT, preferred_element_type=jnp.float32) * SCALE
    kpos = k0 + lax.broadcasted_iota(jnp.int32, (TK, 1), 0)
    qpos = q0 + lax.broadcasted_iota(jnp.int32, (1, TQ), 1)
    qstart = docs.row_start(qpos)
    return jnp.where((kpos <= qpos) & (kpos >= qstart), s, NEG)


def stats_kernel(len_ref, q_ref, do_ref, k_ref, v_ref, st_ref):
    z = lax.axis_index("seq") // XN
    docs = Docs(len_ref)
    st_ref[0:4, :] = jnp.full((4, 512), LOW, jnp.float32)
    st_ref[4:16, :] = jnp.zeros((12, 512), jnp.float32)

    def body(qs, ks, qt, kt, q0, k0):
        rows, cols = pl.ds(qt * TQ, TQ), pl.ds(kt * TK, TK)
        q, do = q_ref[qs, rows, :], do_ref[qs, rows, :]
        k, v = k_ref[ks, cols, :], v_ref[ks, cols, :]
        s = masked_scores(docs, k, q, q0, k0)
        dp = lax.dot_general(v, do, NT, preferred_element_type=jnp.float32)
        old = st_ref[qs : qs + 1, rows]
        new = jnp.maximum(old, jnp.max(s, axis=0, keepdims=True))
        p = jnp.exp(s - new)
        alpha = jnp.exp(old - new)
        st_ref[qs : qs + 1, rows] = new
        st_ref[4 + qs : 5 + qs, rows] = st_ref[4 + qs : 5 + qs, rows] * alpha + jnp.sum(p, axis=0, keepdims=True)
        st_ref[8 + qs : 9 + qs, rows] = st_ref[8 + qs : 9 + qs, rows] * alpha + jnp.sum(p * dp, axis=0, keepdims=True)

    for_tiles(docs, z, body)


def combine_stats(docs, z, mine, up1, up2, down1, down2):
    lk, lq = docs.case(z * 512)
    rk, rq = docs.case(z * 512 + 512)
    lm = jnp.logical_not(lk | lq)
    rm = jnp.logical_not(rk | rq)
    bk, bq = docs.case(z * 512 - 512)
    bm = jnp.logical_not(bk | bq) & (z >= 2)

    def part(ref, slot, use=None):
        m, l, d = ref[slot : slot + 1, :], ref[4 + slot : 5 + slot, :], ref[8 + slot : 9 + slot, :]
        if use is not None:
            m = jnp.where(use, m, LOW)
            l = jnp.where(use, l, 0.0)
            d = jnp.where(use, d, 0.0)
        return m, l, d

    groups = (
        (part(mine, 0), part(down1, 1, z >= 1), part(down2, 2, bm)),
        (part(mine, 1), part(up1, 0, z + 1 < ZN), part(down1, 2, lm & (z >= 1))),
        (part(mine, 2), part(up2, 0, rm & (z + 2 < ZN)), part(up1, 1, rm & (z + 1 < ZN)), part(up1, 3, rq & (z + 1 < ZN))),
        (part(mine, 3), part(down1, 2, lq & (z >= 1))),
    )
    out = []
    for parts in groups:
        m = functools.reduce(jnp.maximum, [p[0] for p in parts])
        l = sum(p[1] * jnp.exp(p[0] - m) for p in parts)
        d = sum(p[2] * jnp.exp(p[0] - m) for p in parts)
        inv = jnp.where(l > 0.0, 1.0 / jnp.where(l > 0.0, l, 1.0), 0.0)
        out.append((m, inv, d * inv))
    return out


def grads_kernel(len_ref, q_ref, do_ref, k_ref, v_ref, mine, up1, up2, down1, down2,
                 qp_ref, kp_ref, stat, kt_ref, dqt, dk_acc, dv_acc):
    z = lax.axis_index("seq") // XN
    docs = Docs(len_ref)
    for qs, (m, inv, d) in enumerate(combine_stats(docs, z, mine, up1, up2, down1, down2)):
        stat[qs : qs + 1, :] = m
        stat[4 + qs : 5 + qs, :] = inv
        stat[8 + qs : 9 + qs, :] = d
    for i in range(4):
        kt_ref[i] = k_ref[i].T
    dqt[...] = jnp.zeros_like(dqt)
    dk_acc[...] = jnp.zeros_like(dk_acc)
    dv_acc[...] = jnp.zeros_like(dv_acc)

    def body(qs, ks, qt, kt, q0, k0):
        rows, cols = pl.ds(qt * TQ, TQ), pl.ds(kt * TK, TK)
        q, do = q_ref[qs, rows, :], do_ref[qs, rows, :]
        k, v = k_ref[ks, cols, :], v_ref[ks, cols, :]
        s = masked_scores(docs, k, q, q0, k0)
        dp = lax.dot_general(v, do, NT, preferred_element_type=jnp.float32)
        p = jnp.exp(s - stat[qs : qs + 1, rows]) * stat[4 + qs : 5 + qs, rows]
        ds = (p * (dp - stat[8 + qs : 9 + qs, rows])).astype(jnp.bfloat16)
        dv_acc[ks, cols, :] += jnp.dot(p.astype(jnp.bfloat16), do, preferred_element_type=jnp.float32)
        dk_acc[ks, cols, :] += jnp.dot(ds, q, preferred_element_type=jnp.float32)
        dqt[qs, :, rows] += jnp.dot(kt_ref[ks, :, cols], ds, preferred_element_type=jnp.float32)

    for_tiles(docs, z, body)
    for i in range(4):
        dq = (dqt[i] * SCALE).T.astype(jnp.bfloat16)
        dk = (dk_acc[i] * SCALE).astype(jnp.bfloat16)
        dv = dv_acc[i].astype(jnp.bfloat16)
        for c in range(XN):
            r = c * 128
            qp_ref[i, c] = jnp.concatenate([dq[r + 32 * j : r + 32 * j + 32] for j in range(4)], axis=1)
            kp_ref[i, c] = pack_pair(dk[r : r + 128], dv[r : r + 128])


def copy_to(src, dst, send, recv, device):
    return pltpu.make_async_remote_copy(
        src_ref=src,
        dst_ref=dst,
        send_sem=send,
        recv_sem=recv,
        device_id={"seq": device},
        device_id_type=pl.DeviceIdType.MESH,
    )


def greet(devices):
    barrier = pltpu.get_barrier_semaphore()
    for device in devices:
        pl.semaphore_signal(barrier, inc=1, device_id={"seq": device}, device_id_type=pl.DeviceIdType.MESH)
    pl.semaphore_wait(barrier, len(devices))


def window(ref, off):
    low = off // 128 * 128
    high = -(-(off + HEAD) // 128) * 128
    return ref[:, low:high][:, off - low : off - low + HEAD]


def pack_pair(first, second):
    return jnp.concatenate([first[:64], second[:64], first[64:], second[64:]], axis=1)


def place():
    me = lax.axis_index("seq")
    z, x = me // XN, me % XN
    up = lax.rem(z + 1, ZN) * XN + x
    down = lax.rem(z + ZN - 1, ZN) * XN + x
    peer = [z * XN + lax.rem(x + d, XN) for d in range(XN)]
    return z, x, up, down, peer


TYPES = (("q", 0), ("k", 1), ("q", 1), ("k", 0))


def gather_kernel(len_ref, q_in, k_in, v_in, do_in, q_out, do_out, k_out, v_out,
                  packed, own, q1, k1, qsel, ksel, q2, k2,
                  x_send, x_recv, z_send, z_recv):
    z, x, up, down, peer = place()
    docs = Docs(len_ref)
    lk, lq = docs.case(z * 512)
    rk, rq = docs.case(z * 512 + 512)
    arrays = {"q": (q_in, do_in), "k": (k_in, v_in)}

    def pack(t):
        kind, head = TYPES[t]
        a, b = arrays[kind]
        for xp in range(XN):
            off = (2 * xp + head) * HEAD
            packed[t, xp] = pack_pair(window(a, off), window(b, off))

    def x_copy(t, d):
        to = lax.rem(x + d, XN)
        return copy_to(packed.at[t, to], own.at[t, x], x_send.at[t, d - 1], x_recv.at[t, d - 1], peer[d])

    def z_copy(i, c):
        src, dst, to = ((own.at[0, c], q1.at[c], down), (own.at[1, c], k1.at[c], up),
                        (qsel.at[c], q2.at[c], down), (ksel.at[c], k2.at[c], up))[i]
        return copy_to(src, dst, z_send.at[i, c], z_recv.at[i, c], to)

    def unpack(value, slot, c, first, second):
        top, low = pl.ds(c * 128, 64), pl.ds(c * 128 + 64, 64)
        first[slot, top, :] = value[:, 0:HEAD]
        second[slot, top, :] = value[:, HEAD : 2 * HEAD]
        first[slot, low, :] = value[:, 2 * HEAD : 3 * HEAD]
        second[slot, low, :] = value[:, 3 * HEAD : 4 * HEAD]

    pack(0)
    pack(1)
    greet(peer[1:] + [up, down])
    for t in (0, 1):
        own[t, x] = packed[t, x]
        for d in (2, 1, 3):
            x_copy(t, d).start()
    z_copy(0, x).start()
    z_copy(1, x).start()
    for t in (2, 3):
        pack(t)
        own[t, x] = packed[t, x]
        for d in (2, 1, 3):
            x_copy(t, d).start()

    def source(d):
        return lax.rem(x + d, XN)

    def got_x(t, d):
        back = XN - d
        copy_to(packed.at[t, x], own.at[t, source(d)], x_send.at[t, back - 1], x_recv.at[t, back - 1], peer[d]).wait_recv()

    for d in (1, 3, 2):
        c = source(d)
        for t in (0, 1):
            got_x(t, d)
            z_copy(t, c).start()
    for d in (0, 1, 3, 2):
        c = source(d)
        if d:
            got_x(2, d)
            got_x(3, d)
        z_copy(0, c).wait_recv()
        qsel[c] = jnp.where(lq, own[2, c], q1[c])
        z_copy(2, c).start()
        z_copy(1, c).wait_recv()
        ksel[c] = jnp.where(rk, own[3, c], k1[c])
        z_copy(3, c).start()
        unpack(own[0, c], 0, c, q_out, do_out)
        unpack(own[1, c], 0, c, k_out, v_out)
        unpack(own[2, c], 3, c, q_out, do_out)
        unpack(own[3, c], 3, c, k_out, v_out)
        unpack(q1[c], 1, c, q_out, do_out)
        unpack(k1[c], 1, c, k_out, v_out)
    for d in (0, 1, 3, 2):
        c = source(d)
        z_copy(2, c).wait_recv()
        unpack(q2[c], 2, c, q_out, do_out)
        z_copy(3, c).wait_recv()
        unpack(k2[c], 2, c, k_out, v_out)
    for t in range(4):
        for d in (1, 2, 3):
            x_copy(t, d).wait_send()
        for c in range(XN):
            z_copy(t, c).wait_send()


def share_kernel(mine, up1, up2, down1, down2, send, recv):
    z, x, up, down, _ = place()
    upper = lax.rem(z + 2, ZN) * XN + x
    lower = lax.rem(z + ZN - 2, ZN) * XN + x
    greet([up, upper, down, lower])
    copies = [copy_to(mine, ref, send.at[i], recv.at[i], to)
              for i, (ref, to) in enumerate(((up1, down), (up2, lower), (down1, up), (down2, upper)))]
    for copy in copies:
        copy.start()
    for copy in copies:
        copy.wait()


def scatter_kernel(len_ref, qp, kp, dq_out, dk_out, dv_out,
                   rq2, rk2, rq1, rk1, qs, ks, qfin, kfin, qhome, khome,
                   z_send, z_recv, x_send, x_recv):
    z, x, up, down, peer = place()
    docs = Docs(len_ref)
    lk, lq = docs.case(z * 512)
    rk, rq = docs.case(z * 512 + 512)
    low, top = z >= 1, z < ZN - 1
    lm = jnp.logical_not(lk | lq) & low
    rm = jnp.logical_not(rk | rq) & top
    lq, rk = lq & low, rk & top

    def z_copy(i, c):
        src, dst, to = ((qp.at[2, c], rq2.at[c], up), (kp.at[2, c], rk2.at[c], down),
                        (qs.at[c], rq1.at[c], up), (ks.at[c], rk1.at[c], down))[i]
        return copy_to(src, dst, z_send.at[i, c], z_recv.at[i, c], to)

    def plus(a, b, use):
        return (a.astype(jnp.float32) + jnp.where(use, b.astype(jnp.float32), 0.0)).astype(jnp.bfloat16)

    def dest(d):
        return lax.rem(x + d, XN)

    def x_copy(kind, head, d):
        src, dst = ((qfin, qhome), (kfin, khome))[kind]
        i = 2 * kind + head
        return copy_to(src.at[head, dest(d)], dst.at[head, x], x_send.at[i, d - 1], x_recv.at[i, d - 1], peer[d])

    def send_home(kind, head, d, value):
        src, dst = ((qfin, qhome), (kfin, khome))[kind]
        if d:
            src[head, dest(d)] = value
            x_copy(kind, head, d).start()
        else:
            dst[head, x] = value

    order = (2, 1, 3, 0)
    greet(peer[1:] + [up, down])
    for d in order:
        z_copy(1, dest(d)).start()
        z_copy(0, dest(d)).start()
    for d in order:
        c = dest(d)
        z_copy(1, c).wait_recv()
        back = rk2[c]
        ks[c] = plus(kp[1, c], back, rm)
        z_copy(3, c).start()
        z_copy(0, c).wait_recv()
        fore = rq2[c]
        qs[c] = plus(qp[1, c], fore, lm)
        z_copy(2, c).start()
        send_home(1, 0, d, plus(kp[3, c], back, rk))
        send_home(0, 1, d, plus(qp[3, c], fore, lq))
    for d in order:
        c = dest(d)
        z_copy(3, c).wait_recv()
        send_home(1, 1, d, plus(kp[0, c], rk1[c], top))
        z_copy(2, c).wait_recv()
        send_home(0, 0, d, plus(qp[0, c], rq1[c], low))
    for i in range(4):
        for d in (1, 2, 3):
            x_copy(i // 2, i % 2, d).wait_recv()
    for a, out, n in ((0, dq_out, 4), (0, dk_out, 2), (1, dv_out, 2)):
        home = qhome if n == 4 else khome
        step = 128 // n
        for part in range(n):
            lanes = (part if n == 4 else 2 * part + a) * HEAD
            pieces = []
            for xs in range(XN):
                for head in range(2):
                    pieces.append(home[head, xs][:, lanes : lanes + HEAD])
            out[part * step : (part + 1) * step, :] = jnp.concatenate(pieces, axis=1)
    for i in range(4):
        for c in range(XN):
            z_copy(i, c).wait_send()
        for d in (1, 2, 3):
            x_copy(i // 2, i % 2, d).wait_send()


VM = pl.BlockSpec(memory_space=pltpu.VMEM)
SM = pl.BlockSpec(memory_space=pltpu.SMEM)
LIMIT = 48 * 1024 * 1024
BIG = pltpu.CompilerParams(vmem_limit_bytes=LIMIT)
DMA = pltpu.SemaphoreType.DMA


def remote(number):
    return pltpu.CompilerParams(vmem_limit_bytes=LIMIT, collective_id=number, has_side_effects=True)


def buf(*shape, dtype=jnp.bfloat16):
    return pltpu.VMEM(shape, dtype)


def out(*shape, dtype=jnp.bfloat16):
    return jax.ShapeDtypeStruct(shape, dtype)


def shards(queries, key_vectors, value_vectors, out_grad, doc_lengths):
    rows, width = queries.shape[1], queries.shape[2]
    chunk = (XN, 64, 4 * HEAD)
    small = (XN, 32, 4 * HEAD)
    block = out(4, 512, HEAD)
    qs, dos, ks, vs = pl.pallas_call(
        gather_kernel,
        out_shape=(block,) * 4,
        in_specs=[SM] + [VM] * 4,
        out_specs=(VM,) * 4,
        scratch_shapes=[buf(4, *chunk), buf(4, *chunk)] + [buf(*chunk)] * 6
        + [DMA((4, 3)), DMA((4, 3)), DMA((4, 4)), DMA((4, 4))],
        compiler_params=remote(0),
    )(doc_lengths, queries[0], key_vectors[0], value_vectors[0], out_grad[0])
    stat = out(16, 512, dtype=jnp.float32)
    mine = pl.pallas_call(
        stats_kernel,
        out_shape=stat,
        in_specs=[SM] + [VM] * 4,
        out_specs=VM,
        compiler_params=BIG,
    )(doc_lengths, qs, dos, ks, vs)
    others = pl.pallas_call(
        share_kernel,
        out_shape=(stat,) * 4,
        in_specs=[VM],
        out_specs=(VM,) * 4,
        scratch_shapes=[DMA((4,)), DMA((4,))],
        compiler_params=remote(1),
    )(mine)
    qp, kp = pl.pallas_call(
        grads_kernel,
        out_shape=(out(4, *small), out(4, *chunk)),
        in_specs=[SM] + [VM] * 9,
        out_specs=(VM, VM),
        scratch_shapes=[
            buf(16, 512, dtype=jnp.float32),
            buf(4, HEAD, 512),
            buf(4, HEAD, 512, dtype=jnp.float32),
            buf(4, 512, HEAD, dtype=jnp.float32),
            buf(4, 512, HEAD, dtype=jnp.float32),
        ],
        compiler_params=BIG,
    )(doc_lengths, qs, dos, ks, vs, mine, *others)
    full = out(rows, width)
    grads = pl.pallas_call(
        scatter_kernel,
        out_shape=(full,) * 3,
        in_specs=[SM, VM, VM],
        out_specs=(VM,) * 3,
        scratch_shapes=[buf(*small), buf(*chunk), buf(*small), buf(*chunk), buf(*small), buf(*chunk),
                        buf(2, *small), buf(2, *chunk), buf(2, *small), buf(2, *chunk),
                        DMA((4, 4)), DMA((4, 4)), DMA((4, 3)), DMA((4, 3))],
        compiler_params=remote(2),
    )(doc_lengths, qp, kp)
    return tuple(g[None] for g in grads)


def solution(mesh):
    spec = P("section", "seq", "dp")
    return jax.shard_map(
        shards,
        mesh=mesh,
        in_specs=(spec, spec, spec, spec, P()),
        out_specs=(spec, spec, spec),
        check_vma=False,
    )
```

```python
import functools

import jax
import jax.numpy as jnp
from jax import lax
from jax.experimental import pallas as pl
from jax.experimental.pallas import tpu as pltpu
from jax.sharding import PartitionSpec as P

HEAD = 224
ZN, XN = 8, 4
SCALE = HEAD ** (-0.5)
NEG = -1e30
LOW = -1e20
TILE = 256
GROUP = 4
ITEMS = ((0, 3), (1, 3), (2, 3), (0, 2), (1, 2), (2, 2), (3, 0), (3, 1), (3, 2), (2, 0), (2, 1))


class Docs:
    def __init__(self, lengths):
        self.bounds = []
        total = jnp.int32(0)
        for d in range(8):
            total = total + lengths[d]
            self.bounds.append(total)

    def start(self, t):
        r = jnp.int32(0)
        for b in self.bounds[:7]:
            r = jnp.where(b <= t, b, r)
        return r

    def end(self, t):
        r = jnp.int32(4096)
        for b in reversed(self.bounds):
            r = jnp.where(b > t, b, r)
        return r

    def row_start(self, pos):
        r = jnp.zeros_like(pos)
        for b in self.bounds[:7]:
            r = jnp.where(pos >= b, b, r)
        return r

    def case(self, t):
        before = t - self.start(t - 1)
        after = self.end(t - 1) - t
        keys = after > 1024
        return keys, (before > 1024) & jnp.logical_not(keys)


def slots(docs, z):
    lk, lq = docs.case(z * 512)
    rk, rq = docs.case(z * 512 + 512)
    lm = jnp.logical_not(lk | lq)
    rm = jnp.logical_not(rk | rq)
    q_ids = (z, z + 1, jnp.where(rq, z + 1, z + 2), z)
    k_ids = (z, z - 1, jnp.where(lk, z - 1, z - 2), z)
    valid = {
        (0, 3): True,
        (1, 3): jnp.logical_not(rk),
        (2, 3): rm,
        (0, 2): lk,
        (1, 2): lk & jnp.logical_not(rk),
        (2, 2): (lk & rm) | (rq & lm),
        (3, 0): True,
        (3, 1): jnp.logical_not(lq),
        (3, 2): lm,
        (2, 0): rq,
        (2, 1): rq & jnp.logical_not(lq),
    }
    return q_ids, k_ids, valid


NT = (((1,), (1,)), ((), ()))


def list_tiles(docs, z, todo):
    q_ids, k_ids, valid = slots(docs, z)
    firsts = [[docs.start(q_ids[qs] * 512 + qt * TILE) for qt in range(2)] for qs in range(4)]
    count = jnp.int32(0)
    for qs, ks in ITEMS:
        qid, kid, ok = q_ids[qs], k_ids[ks], valid[(qs, ks)]
        use = (qid < ZN) & (kid >= 0) & ok
        for qt in range(2):
            q0 = qid * 512 + qt * TILE
            for kt in range(2):
                k0 = kid * 512 + kt * TILE
                k1 = k0 + TILE - 1
                hit = use & (k0 <= q0 + TILE - 1) & ((k1 >= q0) | (k1 >= firsts[qs][qt]))
                todo[0, count] = 2 * qs + qt
                todo[1, count] = 2 * ks + kt
                todo[2, count] = q0
                todo[3, count] = k0
                count = count + jnp.where(hit, 1, 0)
    for i in range(GROUP - 1):
        todo[0, count + i] = 0
        todo[1, count + i] = 0
        todo[2, count + i] = 0
        todo[3, count + i] = 1 << 20
    return count


def for_groups(count, todo, body):
    @pl.loop(0, (count + GROUP - 1) // GROUP)
    def _(g):
        body([tuple(todo[j, g * GROUP + i] for j in range(4)) for i in range(GROUP)])


def tile_rows(ref, i):
    return ref[pl.ds(pl.multiple_of(i * TILE, TILE), TILE), :]


def raw_scores(k, q):
    return lax.dot_general(k, q, NT, preferred_element_type=jnp.float32)


def masked(docs, s, q0, k0):
    kpos = k0 + lax.broadcasted_iota(jnp.int32, (TILE, 1), 0)
    qpos = q0 + lax.broadcasted_iota(jnp.int32, (1, TILE), 1)
    qstart = docs.row_start(qpos)
    return jnp.where((kpos <= qpos) & (kpos >= qstart), s * SCALE, NEG)


def stats_kernel(len_ref, q_ref, do_ref, k_ref, v_ref, st_ref, todo):
    z = lax.axis_index("seq") // XN
    docs = Docs(len_ref)
    st_ref[:, 0:1, :] = jnp.full((8, 1, TILE), LOW, jnp.float32)
    st_ref[:, 1:4, :] = jnp.zeros((8, 3, TILE), jnp.float32)

    def body(tiles):
        raw = []
        for qi, ki, q0, k0 in tiles:
            s = raw_scores(tile_rows(k_ref, ki), tile_rows(q_ref, qi))
            raw.append((s, raw_scores(tile_rows(v_ref, ki), tile_rows(do_ref, qi))))
        for (qi, ki, q0, k0), (s, dp) in zip(tiles, raw):
            s = masked(docs, s, q0, k0)
            old = st_ref[qi, 0:1, :]
            new = jnp.maximum(old, jnp.max(s, axis=0, keepdims=True))
            p = jnp.exp(s - new)
            alpha = jnp.exp(old - new)
            st_ref[qi, 0:1, :] = new
            st_ref[qi, 1:2, :] = st_ref[qi, 1:2, :] * alpha + jnp.sum(p, axis=0, keepdims=True)
            st_ref[qi, 2:3, :] = st_ref[qi, 2:3, :] * alpha + jnp.sum(p * dp, axis=0, keepdims=True)

    for_groups(list_tiles(docs, z, todo), todo, body)


def combine_stats(docs, z, mine, up1, up2, down1, down2):
    lk, lq = docs.case(z * 512)
    rk, rq = docs.case(z * 512 + 512)
    lm = jnp.logical_not(lk | lq)
    rm = jnp.logical_not(rk | rq)
    bk, bq = docs.case(z * 512 - 512)
    bm = jnp.logical_not(bk | bq) & (z >= 2)

    def part(ref, slot, use=None):
        m, l, d = (ref[2 * slot : 2 * slot + 2, r : r + 1, :] for r in range(3))
        if use is not None:
            m = jnp.where(use, m, LOW)
            l = jnp.where(use, l, 0.0)
            d = jnp.where(use, d, 0.0)
        return m, l, d

    groups = (
        (part(mine, 0), part(down1, 1, z >= 1), part(down2, 2, bm)),
        (part(mine, 1), part(up1, 0, z + 1 < ZN), part(down1, 2, lm & (z >= 1))),
        (part(mine, 2), part(up2, 0, rm & (z + 2 < ZN)), part(up1, 1, rm & (z + 1 < ZN)), part(up1, 3, rq & (z + 1 < ZN))),
        (part(mine, 3), part(down1, 2, lq & (z >= 1))),
    )
    out = []
    for parts in groups:
        m = functools.reduce(jnp.maximum, [p[0] for p in parts])
        l = sum(p[1] * jnp.exp(p[0] - m) for p in parts)
        d = sum(p[2] * jnp.exp(p[0] - m) for p in parts)
        inv = jnp.where(l > 0.0, 1.0 / jnp.where(l > 0.0, l, 1.0), 0.0)
        out.append((m, inv, d * inv))
    return out


def grads_kernel(len_ref, q_ref, do_ref, k_ref, v_ref, mine, up1, up2, down1, down2,
                 qp_ref, kp_ref, stat, todo, kt_ref, dqt, dk_acc, dv_acc):
    z = lax.axis_index("seq") // XN
    docs = Docs(len_ref)
    for qs, values in enumerate(combine_stats(docs, z, mine, up1, up2, down1, down2)):
        for r, value in enumerate(values):
            stat[2 * qs : 2 * qs + 2, r : r + 1, :] = value
    for i in range(8):
        kt_ref[i] = k_ref[i * TILE : (i + 1) * TILE, :].T
    dqt[...] = jnp.zeros_like(dqt)
    dk_acc[...] = jnp.zeros_like(dk_acc)
    dv_acc[...] = jnp.zeros_like(dv_acc)

    def body(tiles):
        raw = []
        for qi, ki, q0, k0 in tiles:
            s = raw_scores(tile_rows(k_ref, ki), tile_rows(q_ref, qi))
            raw.append((s, raw_scores(tile_rows(v_ref, ki), tile_rows(do_ref, qi))))
        weights = []
        for (qi, ki, q0, k0), (s, dp) in zip(tiles, raw):
            p = jnp.exp(masked(docs, s, q0, k0) - stat[qi, 0:1, :]) * stat[qi, 1:2, :]
            weights.append((p.astype(jnp.bfloat16), (p * (dp - stat[qi, 2:3, :])).astype(jnp.bfloat16)))
        terms = []
        for (qi, ki, q0, k0), (p, ds) in zip(tiles, weights):
            terms.append((
                jnp.dot(p, tile_rows(do_ref, qi), preferred_element_type=jnp.float32),
                jnp.dot(ds, tile_rows(q_ref, qi), preferred_element_type=jnp.float32),
                jnp.dot(kt_ref[ki], ds, preferred_element_type=jnp.float32),
            ))
        for (qi, ki, q0, k0), (dv, dk, dq) in zip(tiles, terms):
            dv_acc[ki] += dv
            dk_acc[ki] += dk
            dqt[qi] += dq

    for_groups(list_tiles(docs, z, todo), todo, body)
    for i in range(8):
        dq = (dqt[i] * SCALE).T.astype(jnp.bfloat16)
        dk = (dk_acc[i] * SCALE).astype(jnp.bfloat16)
        dv = dv_acc[i].astype(jnp.bfloat16)
        for half in range(2):
            r, c = half * 128, 2 * (i % 2) + half
            qp_ref[i // 2, c] = jnp.concatenate([dq[r + 32 * j : r + 32 * j + 32] for j in range(4)], axis=1)
            kp_ref[i // 2, c] = pack_pair(dk[r : r + 128], dv[r : r + 128])


def copy_to(src, dst, send, recv, device):
    return pltpu.make_async_remote_copy(
        src_ref=src,
        dst_ref=dst,
        send_sem=send,
        recv_sem=recv,
        device_id={"seq": device},
        device_id_type=pl.DeviceIdType.MESH,
    )


def meet(devices):
    for device in devices:
        pl.semaphore_signal(
            pltpu.get_barrier_semaphore(), inc=1, device_id={"seq": device}, device_id_type=pl.DeviceIdType.MESH
        )


def greet(devices):
    meet(devices)
    pl.semaphore_wait(pltpu.get_barrier_semaphore(), len(devices))


def window(ref, off):
    low = off // 128 * 128
    high = -(-(off + HEAD) // 128) * 128
    return ref[:, low:high][:, off - low : off - low + HEAD]


def pack_pair(first, second):
    return jnp.concatenate([first[:64], second[:64], first[64:], second[64:]], axis=1)


def place():
    me = lax.axis_index("seq")
    z, x = me // XN, me % XN
    up = lax.rem(z + 1, ZN) * XN + x
    down = lax.rem(z + ZN - 1, ZN) * XN + x
    peer = [z * XN + lax.rem(x + d, XN) for d in range(XN)]
    return z, x, up, down, peer


TYPES = (("q", 0), ("k", 1), ("q", 1), ("k", 0))


def gather_kernel(len_ref, raw, q_out, do_out, k_out, v_out,
                  packed, own, q1, k1, qsel, ksel, q2, k2,
                  x_send, x_recv, z_send, z_recv):
    z, x, up, down, peer = place()
    low, top = z > 0, z < ZN - 1
    meet(peer[1:])
    pl.when(low)(lambda: meet([down]))
    pl.when(top)(lambda: meet([up]))
    docs = Docs(len_ref)
    lk, lq = docs.case(z * 512)
    rk, rq = docs.case(z * 512 + 512)

    def pack(t, xp):
        kind, head = TYPES[t]
        i = 0 if kind == "q" else 2
        off = (2 * xp + head) * HEAD
        packed[t, xp] = pack_pair(window(raw.at[i], off), window(raw.at[i + 1], off))

    def x_copy(t, d):
        to = lax.rem(x + d, XN)
        return copy_to(packed.at[t, to], own.at[t, x], x_send.at[t, d - 1], x_recv.at[t, d - 1], peer[d])

    def z_copy(i, c):
        src, dst, to = ((own.at[0, c], q1.at[c], down), (own.at[1, c], k1.at[c], up),
                        (qsel.at[c], q2.at[c], down), (ksel.at[c], k2.at[c], up))[i]
        return copy_to(src, dst, z_send.at[i, c], z_recv.at[i, c], to)

    def z_start(i, c):
        pl.when((low, top)[i % 2])(lambda: z_copy(i, c).start())

    def z_got(i, c):
        pl.when((top, low)[i % 2])(lambda: z_copy(i, c).wait_recv())

    def unpack(value, slot, c, first, second):
        row = slot * 512 + c * 128
        upper = pl.ds(pl.multiple_of(row, 64), 64)
        lower = pl.ds(pl.multiple_of(row + 64, 64), 64)
        first[upper, :] = value[:, 0:HEAD]
        second[upper, :] = value[:, HEAD : 2 * HEAD]
        first[lower, :] = value[:, 2 * HEAD : 3 * HEAD]
        second[lower, :] = value[:, 3 * HEAD : 4 * HEAD]

    def source(d):
        return lax.rem(x + d, XN)

    def got_x(t, d):
        back = XN - d
        copy_to(packed.at[t, x], own.at[t, source(d)], x_send.at[t, back - 1], x_recv.at[t, back - 1], peer[d]).wait_recv()

    def second(i, c):
        z_got(i - 2, c)
        if i == 2:
            qsel[c] = jnp.where(lq, own[2, c], q1[c])
        else:
            ksel[c] = jnp.where(rk, own[3, c], k1[c])
        z_start(i, c)

    def first(t, d):
        got_x(t, d)
        z_start(t, source(d))

    def unpack_own(t, c):
        unpack(own[t, c], *((0, c, q_out, do_out), (0, c, k_out, v_out), (3, c, q_out, do_out), (3, c, k_out, v_out))[t])

    for xp in range(XN):
        pack(0, xp)
    own[0, x] = packed[0, x]
    pl.semaphore_wait(pltpu.get_barrier_semaphore(), 3 + jnp.where(low, 1, 0) + jnp.where(top, 1, 0))
    for d in (1, 3):
        x_copy(0, d).start()
    z_start(0, x)
    for xp in range(XN):
        pack(1, xp)
    own[1, x] = packed[1, x]
    for d in (1, 3):
        x_copy(1, d).start()
    z_start(1, x)
    for t in (0, 1):
        x_copy(t, 2).start()
    for t in (2, 3):
        for xp in range(XN):
            pack(t, xp)
        own[t, x] = packed[t, x]
    second(2, x)
    second(3, x)
    unpack_own(0, x)
    unpack_own(1, x)
    first(0, 1)
    first(0, 3)
    first(1, 1)
    first(1, 3)
    for d in (1, 3):
        x_copy(2, d).start()
        x_copy(3, d).start()
    unpack_own(2, x)
    unpack_own(3, x)
    for t in (0, 1):
        unpack_own(t, source(1))
        unpack_own(t, source(3))
    first(0, 2)
    first(1, 2)
    x_copy(2, 2).start()
    x_copy(3, 2).start()
    unpack(q1[x], 1, x, q_out, do_out)
    unpack(k1[x], 1, x, k_out, v_out)
    for t in (0, 1):
        unpack_own(t, source(2))
    for d in (1, 3, 2):
        c = source(d)
        for t in (2, 3):
            got_x(t, d)
            second(t, c)
        unpack(q1[c], 1, c, q_out, do_out)
        unpack(k1[c], 1, c, k_out, v_out)
        unpack_own(2, c)
        unpack_own(3, c)
    for d in (0, 1, 3, 2):
        c = source(d)
        z_got(2, c)
        unpack(q2[c], 2, c, q_out, do_out)
        z_got(3, c)
        unpack(k2[c], 2, c, k_out, v_out)
    for t in range(4):
        for d in (1, 2, 3):
            x_copy(t, d).wait_send()
    for t in range(4):
        for c in range(XN):
            pl.when((low, top)[t % 2])(z_copy(t, c).wait_send)


def share_kernel(mine, up1, up2, down1, down2, send, recv):
    z, x, up, down, _ = place()
    upper = lax.rem(z + 2, ZN) * XN + x
    lower = lax.rem(z + ZN - 2, ZN) * XN + x
    greet([up, upper, down, lower])
    copies = []
    for i, (ref, tiles, to) in enumerate(((up1, (0, 8), down), (down1, (2, 4), up), (up2, (0, 2), lower), (down2, (4, 2), upper))):
        part = pl.ds(*tiles)
        copies.append(copy_to(mine.at[part], ref.at[part], send.at[i], recv.at[i], to))
    for copy in copies:
        copy.start()
    for copy in copies:
        copy.wait()


def scatter_kernel(len_ref, qp, kp, qhome, khome,
                   rq2, rk2, rq1, rk1, qs, ks, qfin, kfin,
                   z_send, z_recv, x_send, x_recv):
    z, x, up, down, peer = place()
    docs = Docs(len_ref)
    lk, lq = docs.case(z * 512)
    rk, rq = docs.case(z * 512 + 512)
    low, top = z >= 1, z < ZN - 1
    lm = jnp.logical_not(lk | lq) & low
    rm = jnp.logical_not(rk | rq) & top
    lq, rk = lq & low, rk & top

    def z_start(i, c):
        pl.when((top, low)[i % 2])(lambda: z_copy(i, c).start())

    def z_got(i, c):
        pl.when((low, top)[i % 2])(lambda: z_copy(i, c).wait_recv())

    def z_copy(i, c):
        src, dst, to = ((qp.at[2, c], rq2.at[c], up), (kp.at[2, c], rk2.at[c], down),
                        (qs.at[c], rq1.at[c], up), (ks.at[c], rk1.at[c], down))[i]
        return copy_to(src, dst, z_send.at[i, c], z_recv.at[i, c], to)

    def plus(a, b, use):
        return (a.astype(jnp.float32) + jnp.where(use, b.astype(jnp.float32), 0.0)).astype(jnp.bfloat16)

    def dest(d):
        return lax.rem(x + d, XN)

    def x_copy(kind, head, d):
        src, dst = ((qfin, qhome), (kfin, khome))[kind]
        i = 2 * kind + head
        return copy_to(src.at[head, dest(d)], dst.at[head, x], x_send.at[i, d - 1], x_recv.at[i, d - 1], peer[d])

    def send_home(kind, head, d, value):
        src, dst = ((qfin, qhome), (kfin, khome))[kind]
        if d:
            src[head, dest(d)] = value
            x_copy(kind, head, d).start()
        else:
            dst[head, x] = value

    order = (2, 1, 3, 0)
    meet(peer[1:])
    pl.when(low)(lambda: meet([down]))
    pl.when(top)(lambda: meet([up]))
    pl.semaphore_wait(pltpu.get_barrier_semaphore(), 3 + jnp.where(low, 1, 0) + jnp.where(top, 1, 0))
    def second(d):
        z_start(1, dest(d))
        z_start(0, dest(d))

    second(order[0])
    second(order[1])
    for n, d in enumerate(order):
        c = dest(d)
        z_got(1, c)
        if n + 2 < XN:
            second(order[n + 2])
        back = rk2[c]
        ks[c] = plus(kp[1, c], back, rm)
        z_start(3, c)
        z_got(0, c)
        fore = rq2[c]
        qs[c] = plus(qp[1, c], fore, lm)
        z_start(2, c)
        send_home(1, 0, d, plus(kp[3, c], back, rk))
        send_home(0, 1, d, plus(qp[3, c], fore, lq))
    for d in order:
        c = dest(d)
        z_got(3, c)
        send_home(1, 1, d, plus(kp[0, c], rk1[c], top))
        z_got(2, c)
        send_home(0, 0, d, plus(qp[0, c], rq1[c], low))
    for i in range(4):
        for d in (1, 2, 3):
            x_copy(i // 2, i % 2, d).wait_recv()
    for i in range(4):
        for c in range(XN):
            pl.when((top, low)[i % 2])(z_copy(i, c).wait_send)
        for d in (1, 2, 3):
            x_copy(i // 2, i % 2, d).wait_send()


def unpack_kernel(qhome, khome, dq_out, dk_out, dv_out):
    for a, out, n in ((0, dq_out, 4), (0, dk_out, 2), (1, dv_out, 2)):
        home = qhome if n == 4 else khome
        step = 128 // n
        for part in range(n):
            lanes = (part if n == 4 else 2 * part + a) * HEAD
            pieces = []
            for xs in range(XN):
                for head in range(2):
                    pieces.append(home[head, xs][:, lanes : lanes + HEAD])
            out[part * step : (part + 1) * step, :] = jnp.concatenate(pieces, axis=1)


VM = pl.BlockSpec(memory_space=pltpu.VMEM)
SM = pl.BlockSpec(memory_space=pltpu.SMEM)
LIMIT = 26 * 1024 * 1024
BIG = pltpu.CompilerParams(vmem_limit_bytes=LIMIT)
HB = pl.BlockSpec(memory_space=pltpu.HBM)
DMA = pltpu.SemaphoreType.DMA


def remote(number, limit=26):
    return pltpu.CompilerParams(vmem_limit_bytes=limit * 1024 * 1024, collective_id=number, has_side_effects=True)


def buf(*shape, dtype=jnp.bfloat16):
    return pltpu.VMEM(shape, dtype)


def out(*shape, dtype=jnp.bfloat16):
    return jax.ShapeDtypeStruct(shape, dtype)


def shards(queries, key_vectors, value_vectors, out_grad, doc_lengths):
    rows, width = queries.shape[1], queries.shape[2]
    chunk = (XN, 64, 4 * HEAD)
    small = (XN, 32, 4 * HEAD)
    block = out(2048, HEAD)
    qs, dos, ks, vs = pl.pallas_call(
        gather_kernel,
        out_shape=(block,) * 4,
        name="gather",
        in_specs=[SM, VM],
        out_specs=(VM,) * 4,
        scratch_shapes=[buf(4, *chunk), buf(4, *chunk)] + [buf(*chunk)] * 6
        + [DMA((4, 3)), DMA((4, 3)), DMA((4, 4)), DMA((4, 4))],
        compiler_params=remote(0),
    )(doc_lengths, jnp.concatenate([queries, out_grad, key_vectors, value_vectors]))
    stat = out(8, 4, TILE, dtype=jnp.float32)
    todo = pltpu.SMEM((4, 64), jnp.int32)
    mine = pl.pallas_call(
        stats_kernel,
        name="stats",
        out_shape=stat,
        in_specs=[SM] + [VM] * 4,
        out_specs=VM,
        scratch_shapes=[todo],
        compiler_params=BIG,
    )(doc_lengths, qs, dos, ks, vs)
    others = pl.pallas_call(
        share_kernel,
        name="share",
        out_shape=(stat,) * 4,
        in_specs=[VM],
        out_specs=(VM,) * 4,
        scratch_shapes=[DMA((4,)), DMA((4,))],
        compiler_params=remote(1),
    )(mine)
    qp, kp = pl.pallas_call(
        grads_kernel,
        name="grads",
        out_shape=(out(4, *small), out(4, *chunk)),
        in_specs=[SM] + [VM] * 9,
        out_specs=(VM, VM),
        scratch_shapes=[
            buf(8, 4, TILE, dtype=jnp.float32),
            todo,
            buf(8, HEAD, TILE),
            buf(8, HEAD, TILE, dtype=jnp.float32),
            buf(8, TILE, HEAD, dtype=jnp.float32),
            buf(8, TILE, HEAD, dtype=jnp.float32),
        ],
        compiler_params=BIG,
    )(doc_lengths, qs, dos, ks, vs, mine, *others)
    full = out(rows, width)
    home = pl.pallas_call(
        scatter_kernel,
        name="scatter",
        out_shape=(out(2, *small), out(2, *chunk)),
        in_specs=[SM, VM, VM],
        out_specs=(VM,) * 2,
        scratch_shapes=[buf(*small), buf(*chunk), buf(*small), buf(*chunk), buf(*small), buf(*chunk),
                        buf(2, *small), buf(2, *chunk),
                        DMA((4, 4)), DMA((4, 4)), DMA((4, 3)), DMA((4, 3))],
        compiler_params=remote(2),
    )(doc_lengths, qp, kp)
    full = out(rows, width)
    grads = pl.pallas_call(
        unpack_kernel,
        name="unpack",
        out_shape=(full,) * 3,
        in_specs=[VM, VM],
        out_specs=(VM,) * 3,
        compiler_params=BIG,
    )(*home)
    return tuple(g[None] for g in grads)


def solution(mesh):
    spec = P("section", "seq", "dp")
    return jax.shard_map(
        shards,
        mesh=mesh,
        in_specs=(spec, spec, spec, spec, P()),
        out_specs=(spec, spec, spec),
        check_vma=False,
    )
```

```python
import functools

import jax
import jax.numpy as jnp
from jax import lax
from jax.experimental import pallas as pl
from jax.experimental.pallas import tpu as pltpu
from jax.sharding import PartitionSpec as P

HEAD = 224
ZN, XN = 8, 4
SCALE = HEAD ** (-0.5)
NEG = -1e30
LOW = -1e20
TILE = 256
GROUP = 4
ITEMS = ((0, 3), (1, 3), (2, 3), (0, 2), (1, 2), (2, 2), (3, 0), (3, 1), (3, 2), (2, 0), (2, 1))

LATE = tuple(item for item in ITEMS if 2 in item)
OFF = tuple(item for item in ITEMS if item not in ((0, 3), (3, 0)))


class Docs:
    def __init__(self, lengths):
        self.bounds = []
        total = jnp.int32(0)
        for d in range(8):
            total = total + lengths[d]
            self.bounds.append(total)

    def start(self, t):
        r = jnp.int32(0)
        for b in self.bounds[:7]:
            r = jnp.where(b <= t, b, r)
        return r

    def end(self, t):
        r = jnp.int32(4096)
        for b in reversed(self.bounds):
            r = jnp.where(b > t, b, r)
        return r

    def row_start(self, pos):
        r = jnp.zeros_like(pos)
        for b in self.bounds[:7]:
            r = jnp.where(pos >= b, b, r)
        return r

    def case(self, t):
        before = t - self.start(t - 1)
        after = self.end(t - 1) - t
        keys = after > 1024
        return keys, (before > 1024) & jnp.logical_not(keys)


def slots(docs, z):
    lk, lq = docs.case(z * 512)
    rk, rq = docs.case(z * 512 + 512)
    lm = jnp.logical_not(lk | lq)
    rm = jnp.logical_not(rk | rq)
    q_ids = (z, z + 1, jnp.where(rq, z + 1, z + 2), z)
    k_ids = (z, z - 1, jnp.where(lk, z - 1, z - 2), z)
    valid = {
        (0, 3): True,
        (1, 3): jnp.logical_not(rk),
        (2, 3): rm,
        (0, 2): lk,
        (1, 2): lk & jnp.logical_not(rk),
        (2, 2): (lk & rm) | (rq & lm),
        (3, 0): True,
        (3, 1): jnp.logical_not(lq),
        (3, 2): lm,
        (2, 0): rq,
        (2, 1): rq & jnp.logical_not(lq),
    }
    return q_ids, k_ids, valid


NT = (((1,), (1,)), ((), ()))


def list_tiles(docs, z, todo, items):
    q_ids, k_ids, valid = slots(docs, z)
    firsts = [[docs.start(q_ids[qs] * 512 + qt * TILE) for qt in range(2)] for qs in range(4)]
    count = jnp.int32(0)
    for qs, ks in items:
        qid, kid, ok = q_ids[qs], k_ids[ks], valid[(qs, ks)]
        use = (qid < ZN) & (kid >= 0) & ok
        for qt in range(2):
            q0 = qid * 512 + qt * TILE
            for kt in range(2):
                k0 = kid * 512 + kt * TILE
                k1 = k0 + TILE - 1
                hit = use & (k0 <= q0 + TILE - 1) & ((k1 >= q0) | (k1 >= firsts[qs][qt]))
                todo[0, count] = 2 * qs + qt
                todo[1, count] = 2 * ks + kt
                todo[2, count] = q0
                todo[3, count] = k0
                count = count + jnp.where(hit, 1, 0)
    for i in range(GROUP - 1):
        todo[0, count + i] = 0
        todo[1, count + i] = 0
        todo[2, count + i] = 0
        todo[3, count + i] = 1 << 20
    return count


def for_groups(count, todo, body):
    @pl.loop(0, (count + GROUP - 1) // GROUP)
    def _(g):
        body([tuple(todo[j, g * GROUP + i] for j in range(4)) for i in range(GROUP)])


def tile_rows(ref, i):
    return ref[pl.ds(pl.multiple_of(i * TILE, TILE), TILE), :]


def raw_scores(k, q):
    return lax.dot_general(k, q, NT, preferred_element_type=jnp.float32)


def masked(docs, s, q0, k0):
    kpos = k0 + lax.broadcasted_iota(jnp.int32, (TILE, 1), 0)
    qpos = q0 + lax.broadcasted_iota(jnp.int32, (1, TILE), 1)
    qstart = docs.row_start(qpos)
    return jnp.where((kpos <= qpos) & (kpos >= qstart), s * SCALE, NEG)


FAR = 1 << 20


def diagonal_tiles(z):
    a, b = z * 512, z * 512 + TILE
    return [
        (0, a, [(6, a)]),
        (1, b, [(6, a), (7, b)]),
        (6, a, [(0, a)]),
        (7, b, [(0, a), (1, b)]),
    ]


def near_tiles(docs, z):
    _, lq = docs.case(z * 512)
    rk, _ = docs.case(z * 512 + 512)
    a, b = z * 512, z * 512 + TILE
    fore = jnp.where(jnp.logical_not(rk) & (z < ZN - 1), a, FAR)
    back = jnp.where(jnp.logical_not(lq) & (z > 0), a - 512, FAR)
    tiles = diagonal_tiles(z)
    for i in (2, 3):
        tiles[i][2].extend([(2, back), (3, back + TILE)])
    for i in range(2):
        tiles.append((2 + i, a + 512 + i * TILE, [(6, fore), (7, fore + TILE)]))
    return tiles


def near_stats(docs, z, q_ref, do_ref, k_ref, v_ref, st_ref):
    for qi, q0, keys in near_tiles(docs, z):
        raw = []
        for ki, k0 in keys:
            s = raw_scores(tile_rows(k_ref, ki), tile_rows(q_ref, qi))
            raw.append((masked(docs, s, q0, k0), raw_scores(tile_rows(v_ref, ki), tile_rows(do_ref, qi))))
        m = jnp.full((1, TILE), LOW, jnp.float32)
        for s, dp in raw:
            m = jnp.maximum(m, jnp.max(s, axis=0, keepdims=True))
        l = jnp.zeros((1, TILE), jnp.float32)
        d = jnp.zeros((1, TILE), jnp.float32)
        for s, dp in raw:
            p = jnp.exp(s - m)
            l = l + jnp.sum(p, axis=0, keepdims=True)
            d = d + jnp.sum(p * dp, axis=0, keepdims=True)
        st_ref[qi, 0:1, :] = m
        st_ref[qi, 1:2, :] = l
        st_ref[qi, 2:3, :] = d
    for qi in (4, 5):
        st_ref[qi, 0:1, :] = jnp.full((1, TILE), LOW, jnp.float32)
        st_ref[qi, 1:3, :] = jnp.zeros((2, TILE), jnp.float32)


def stats_kernel(len_ref, q_ref, do_ref, k_ref, v_ref, near, st_ref, todo):
    z = lax.axis_index("seq") // XN
    docs = Docs(len_ref)
    st_ref[...] = near[...]

    def body(tiles):
        raw = []
        for qi, ki, q0, k0 in tiles:
            s = raw_scores(tile_rows(k_ref, ki), tile_rows(q_ref, qi))
            raw.append((s, raw_scores(tile_rows(v_ref, ki), tile_rows(do_ref, qi))))
        for (qi, ki, q0, k0), (s, dp) in zip(tiles, raw):
            s = masked(docs, s, q0, k0)
            old = st_ref[qi, 0:1, :]
            new = jnp.maximum(old, jnp.max(s, axis=0, keepdims=True))
            p = jnp.exp(s - new)
            alpha = jnp.exp(old - new)
            st_ref[qi, 0:1, :] = new
            st_ref[qi, 1:2, :] = st_ref[qi, 1:2, :] * alpha + jnp.sum(p, axis=0, keepdims=True)
            st_ref[qi, 2:3, :] = st_ref[qi, 2:3, :] * alpha + jnp.sum(p * dp, axis=0, keepdims=True)

    for_groups(list_tiles(docs, z, todo, LATE), todo, body)


def combine_stats(docs, z, mine, up1, up2, down1, down2):
    lk, lq = docs.case(z * 512)
    rk, rq = docs.case(z * 512 + 512)
    lm = jnp.logical_not(lk | lq)
    rm = jnp.logical_not(rk | rq)
    bk, bq = docs.case(z * 512 - 512)
    bm = jnp.logical_not(bk | bq) & (z >= 2)

    def part(ref, slot, use=None):
        m, l, d = (ref[2 * slot : 2 * slot + 2, r : r + 1, :] for r in range(3))
        if use is not None:
            m = jnp.where(use, m, LOW)
            l = jnp.where(use, l, 0.0)
            d = jnp.where(use, d, 0.0)
        return m, l, d

    groups = (
        (part(mine, 0), part(down1, 1, z >= 1), part(down2, 2, bm)),
        (part(mine, 1), part(up1, 0, z + 1 < ZN), part(down1, 2, lm & (z >= 1))),
        (part(mine, 2), part(up2, 0, rm & (z + 2 < ZN)), part(up1, 1, rm & (z + 1 < ZN)), part(up1, 3, rq & (z + 1 < ZN))),
        (part(mine, 3), part(down1, 2, lq & (z >= 1))),
    )
    out = []
    for parts in groups:
        m = functools.reduce(jnp.maximum, [p[0] for p in parts])
        l = sum(p[1] * jnp.exp(p[0] - m) for p in parts)
        d = sum(p[2] * jnp.exp(p[0] - m) for p in parts)
        inv = jnp.where(l > 0.0, 1.0 / jnp.where(l > 0.0, l, 1.0), 0.0)
        out.append((m, inv, d * inv))
    return out


def tile_grads(docs, tiles, q_ref, do_ref, k_ref, v_ref, stat, kt_ref):
    raw = []
    for qi, ki, q0, k0 in tiles:
        s = raw_scores(tile_rows(k_ref, ki), tile_rows(q_ref, qi))
        raw.append((s, raw_scores(tile_rows(v_ref, ki), tile_rows(do_ref, qi))))
    weights = []
    for (qi, ki, q0, k0), (s, dp) in zip(tiles, raw):
        p = jnp.exp(masked(docs, s, q0, k0) - stat[qi, 0:1, :]) * stat[qi, 1:2, :]
        weights.append((p.astype(jnp.bfloat16), (p * (dp - stat[qi, 2:3, :])).astype(jnp.bfloat16)))
    terms = []
    for (qi, ki, q0, k0), (p, ds) in zip(tiles, weights):
        terms.append((
            jnp.dot(p, tile_rows(do_ref, qi), preferred_element_type=jnp.float32),
            jnp.dot(ds, tile_rows(q_ref, qi), preferred_element_type=jnp.float32),
            jnp.dot(kt_ref[ki], ds, preferred_element_type=jnp.float32),
        ))
    return terms


def pack_pair(first, second):
    return jnp.concatenate([first[:64], second[:64], first[64:], second[64:]], axis=1)


def pack_query(dqt, q_out, half):
    dq = (dqt * SCALE).T.astype(jnp.bfloat16)
    for i in range(2):
        r = i * 128
        q_out[2 * half + i] = jnp.concatenate([dq[r + 32 * j : r + 32 * j + 32] for j in range(4)], axis=1)


def pack_keys(dk, dv, k_out, half):
    dk = (dk * SCALE).astype(jnp.bfloat16)
    dv = dv.astype(jnp.bfloat16)
    for i in range(2):
        r = i * 128
        k_out[2 * half + i] = pack_pair(dk[r : r + 128], dv[r : r + 128])


def pack_grads(dqt, dk, dv, q_out, k_out, half):
    pack_query(dqt, q_out, half)
    pack_keys(dk, dv, k_out, half)


def grads_kernel(len_ref, q_ref, do_ref, k_ref, v_ref, mine, up1, up2, down1, down2,
                 qp_ref, kp_ref, stat, dqt, dk_acc, dv_acc, todo, kt_ref):
    z = lax.axis_index("seq") // XN
    docs = Docs(len_ref)
    for qs, values in enumerate(combine_stats(docs, z, mine, up1, up2, down1, down2)):
        for r, value in enumerate(values):
            stat[2 * qs : 2 * qs + 2, r : r + 1, :] = value
    for i in range(8):
        kt_ref[i] = k_ref[i * TILE : (i + 1) * TILE, :].T
    dqt[...] = jnp.zeros_like(dqt)
    dk_acc[...] = jnp.zeros_like(dk_acc)
    dv_acc[...] = jnp.zeros_like(dv_acc)

    def body(tiles):
        for (qi, ki, q0, k0), (dv, dk, dq) in zip(tiles, tile_grads(docs, tiles, q_ref, do_ref, k_ref, v_ref, stat, kt_ref)):
            dv_acc[ki] += dv
            dk_acc[ki] += dk
            dqt[qi] += dq

    for_groups(list_tiles(docs, z, todo, OFF), todo, body)
    for i in range(2, 6):
        pack_grads(dqt[i], dk_acc[i], dv_acc[i], qp_ref.at[i // 2 - 1], kp_ref.at[i // 2 - 1], i % 2)


def copy_to(src, dst, send, recv, device):
    return pltpu.make_async_remote_copy(
        src_ref=src,
        dst_ref=dst,
        send_sem=send,
        recv_sem=recv,
        device_id={"seq": device},
        device_id_type=pl.DeviceIdType.MESH,
    )


def meet(devices):
    for device in devices:
        pl.semaphore_signal(
            pltpu.get_barrier_semaphore(), inc=1, device_id={"seq": device}, device_id_type=pl.DeviceIdType.MESH
        )


def greet(devices):
    meet(devices)
    pl.semaphore_wait(pltpu.get_barrier_semaphore(), len(devices))


def window(ref, off):
    low = off // 128 * 128
    high = -(-(off + HEAD) // 128) * 128
    return ref[:, low:high][:, off - low : off - low + HEAD]


def place():
    me = lax.axis_index("seq")
    z, x = me // XN, me % XN
    up = lax.rem(z + 1, ZN) * XN + x
    down = lax.rem(z + ZN - 1, ZN) * XN + x
    peer = [z * XN + lax.rem(x + d, XN) for d in range(XN)]
    return z, x, up, down, peer


TYPES = (("q", 0), ("k", 1), ("q", 1), ("k", 0))


def gather_kernel(len_ref, raw, q_out, do_out, k_out, v_out, near,
                  packed, own, q1, k1, qsel, ksel, q2, k2,
                  x_send, x_recv, z_send, z_recv):
    z, x, up, down, peer = place()
    low, top = z > 0, z < ZN - 1
    meet(peer[1:])
    pl.when(low)(lambda: meet([down]))
    pl.when(top)(lambda: meet([up]))
    docs = Docs(len_ref)
    lk, lq = docs.case(z * 512)
    rk, rq = docs.case(z * 512 + 512)

    def pack(t, xp):
        kind, head = TYPES[t]
        i = 0 if kind == "q" else 2
        off = (2 * xp + head) * HEAD
        packed[t, xp] = pack_pair(window(raw.at[i], off), window(raw.at[i + 1], off))

    def x_copy(t, d):
        to = lax.rem(x + d, XN)
        return copy_to(packed.at[t, to], own.at[t, x], x_send.at[t, d - 1], x_recv.at[t, d - 1], peer[d])

    def z_copy(i, c):
        src, dst, to = ((own.at[0, c], q1.at[c], down), (own.at[1, c], k1.at[c], up),
                        (qsel.at[c], q2.at[c], down), (ksel.at[c], k2.at[c], up))[i]
        return copy_to(src, dst, z_send.at[i, c], z_recv.at[i, c], to)

    def z_start(i, c):
        pl.when((low, top)[i % 2])(lambda: z_copy(i, c).start())

    def z_got(i, c):
        pl.when((top, low)[i % 2])(lambda: z_copy(i, c).wait_recv())

    def unpack(value, slot, c, first, second):
        row = slot * 512 + c * 128
        upper = pl.ds(pl.multiple_of(row, 64), 64)
        lower = pl.ds(pl.multiple_of(row + 64, 64), 64)
        first[upper, :] = value[:, 0:HEAD]
        second[upper, :] = value[:, HEAD : 2 * HEAD]
        first[lower, :] = value[:, 2 * HEAD : 3 * HEAD]
        second[lower, :] = value[:, 3 * HEAD : 4 * HEAD]

    def source(d):
        return lax.rem(x + d, XN)

    def got_x(t, d):
        back = XN - d
        copy_to(packed.at[t, x], own.at[t, source(d)], x_send.at[t, back - 1], x_recv.at[t, back - 1], peer[d]).wait_recv()

    def second(i, c):
        z_got(i - 2, c)
        if i == 2:
            qsel[c] = jnp.where(lq, own[2, c], q1[c])
        else:
            ksel[c] = jnp.where(rk, own[3, c], k1[c])
        z_start(i, c)

    def first(t, d):
        got_x(t, d)
        z_start(t, source(d))

    def unpack_own(t, c):
        unpack(own[t, c], *((0, c, q_out, do_out), (0, c, k_out, v_out), (3, c, q_out, do_out), (3, c, k_out, v_out))[t])

    for xp in range(XN):
        pack(0, xp)
    own[0, x] = packed[0, x]
    pl.semaphore_wait(pltpu.get_barrier_semaphore(), 3 + jnp.where(low, 1, 0) + jnp.where(top, 1, 0))
    for d in (1, 3):
        x_copy(0, d).start()
    z_start(0, x)
    for xp in range(XN):
        pack(1, xp)
    own[1, x] = packed[1, x]
    for d in (1, 3):
        x_copy(1, d).start()
    z_start(1, x)
    for t in (0, 1):
        x_copy(t, 2).start()
    for t in (2, 3):
        for xp in range(XN):
            pack(t, xp)
        own[t, x] = packed[t, x]
    second(2, x)
    second(3, x)
    unpack_own(0, x)
    unpack_own(1, x)
    first(0, 1)
    first(0, 3)
    first(1, 1)
    first(1, 3)
    for d in (1, 3):
        x_copy(2, d).start()
        x_copy(3, d).start()
    unpack_own(2, x)
    unpack_own(3, x)
    for t in (0, 1):
        unpack_own(t, source(1))
        unpack_own(t, source(3))
    first(0, 2)
    first(1, 2)
    x_copy(2, 2).start()
    x_copy(3, 2).start()
    unpack(q1[x], 1, x, q_out, do_out)
    unpack(k1[x], 1, x, k_out, v_out)
    for t in (0, 1):
        unpack_own(t, source(2))
    for d in (1, 3, 2):
        c = source(d)
        for t in (2, 3):
            got_x(t, d)
            second(t, c)
        unpack(q1[c], 1, c, q_out, do_out)
        unpack(k1[c], 1, c, k_out, v_out)
        unpack_own(2, c)
        unpack_own(3, c)
    @pl.when(jnp.logical_not(top))
    def _():
        q_out[512:1024, :] = jnp.zeros((512, HEAD), jnp.bfloat16)
        do_out[512:1024, :] = jnp.zeros((512, HEAD), jnp.bfloat16)

    @pl.when(jnp.logical_not(low))
    def _():
        k_out[512:1024, :] = jnp.zeros((512, HEAD), jnp.bfloat16)
        v_out[512:1024, :] = jnp.zeros((512, HEAD), jnp.bfloat16)

    near_stats(docs, z, q_out, do_out, k_out, v_out, near)
    for d in (0, 1, 3, 2):
        c = source(d)
        z_got(2, c)
        unpack(q2[c], 2, c, q_out, do_out)
        z_got(3, c)
        unpack(k2[c], 2, c, k_out, v_out)
    for t in range(4):
        for d in (1, 2, 3):
            x_copy(t, d).wait_send()
    for t in range(4):
        for c in range(XN):
            pl.when((low, top)[t % 2])(z_copy(t, c).wait_send)


def share_kernel(mine, up1, up2, down1, down2, send, recv):
    z, x, up, down, _ = place()
    upper = lax.rem(z + 2, ZN) * XN + x
    lower = lax.rem(z + ZN - 2, ZN) * XN + x
    greet([up, upper, down, lower])
    copies = []
    for i, (ref, tiles, to) in enumerate(((up1, (0, 8), down), (down1, (2, 4), up), (up2, (0, 2), lower), (down2, (4, 2), upper))):
        part = pl.ds(*tiles)
        copies.append(copy_to(mine.at[part], ref.at[part], send.at[i], recv.at[i], to))
    for copy in copies:
        copy.start()
    for copy in copies:
        copy.wait()


def scatter_kernel(len_ref, q_ref, do_ref, k_ref, v_ref, stat, dqt, dk_acc, dv_acc, qp, kp, qhome, khome,
                   kt_ref, ownq, ownk, rq2, rk2, rq1, rk1, qs, ks, qfin, kfin,
                   z_send, z_recv, x_send, x_recv):
    z, x, up, down, peer = place()
    docs = Docs(len_ref)
    lk, lq = docs.case(z * 512)
    rk, rq = docs.case(z * 512 + 512)
    low, top = z >= 1, z < ZN - 1
    lm = jnp.logical_not(lk | lq) & low
    rm = jnp.logical_not(rk | rq) & top
    lq, rk = lq & low, rk & top

    def z_start(i, c):
        pl.when((top, low)[i % 2])(lambda: z_copy(i, c).start())

    def z_got(i, c):
        pl.when((low, top)[i % 2])(lambda: z_copy(i, c).wait_recv())

    def z_copy(i, c):
        src, dst, to = ((qp.at[1, c], rq2.at[c], up), (kp.at[1, c], rk2.at[c], down),
                        (qs.at[c], rq1.at[c], up), (ks.at[c], rk1.at[c], down))[i]
        return copy_to(src, dst, z_send.at[i, c], z_recv.at[i, c], to)

    def plus(a, b, use):
        return (a.astype(jnp.float32) + jnp.where(use, b.astype(jnp.float32), 0.0)).astype(jnp.bfloat16)

    def dest(d):
        return lax.rem(x + d, XN)

    def x_copy(kind, head, d):
        src, dst = ((qfin, qhome), (kfin, khome))[kind]
        i = 2 * kind + head
        return copy_to(src.at[head, dest(d)], dst.at[head, x], x_send.at[i, d - 1], x_recv.at[i, d - 1], peer[d])

    def send_home(kind, head, d, value):
        src, dst = ((qfin, qhome), (kfin, khome))[kind]
        if d:
            src[head, dest(d)] = value
            x_copy(kind, head, d).start()
        else:
            dst[head, x] = value

    order = (2, 1, 3, 0)
    meet(peer[1:])
    pl.when(low)(lambda: meet([down]))
    pl.when(top)(lambda: meet([up]))
    pl.semaphore_wait(pltpu.get_barrier_semaphore(), 3 + jnp.where(low, 1, 0) + jnp.where(top, 1, 0))
    def second(d):
        z_start(1, dest(d))
        z_start(0, dest(d))

    second(order[0])
    second(order[1])
    own = (0, 1, 6, 7)
    for i in own:
        kt_ref[i] = tile_rows(k_ref, i).T
    for head, tiles in enumerate((diagonal_tiles(z)[:2], diagonal_tiles(z)[2:])):
        pairs = [(qi, ki, q0, k0) for qi, q0, keys in tiles for ki, k0 in keys]
        terms = tile_grads(docs, pairs, q_ref, do_ref, k_ref, v_ref, stat, kt_ref)
        for half in range(2):
            qi, ki = pairs[2 * half][0], pairs[2 * half][1]
            dq = dqt[qi] + sum(t[2] for p, t in zip(pairs, terms) if p[0] == qi)
            pack_query(dq, ownq.at[head], half)
            dk = dk_acc[ki] + sum(t[1] for p, t in zip(pairs, terms) if p[1] == ki)
            dv = dv_acc[ki] + sum(t[0] for p, t in zip(pairs, terms) if p[1] == ki)
            pack_keys(dk, dv, ownk.at[head], half)
    for n, d in enumerate(order):
        c = dest(d)
        z_got(1, c)
        if n + 2 < XN:
            second(order[n + 2])
        back = rk2[c]
        ks[c] = plus(kp[0, c], back, rm)
        z_start(3, c)
        z_got(0, c)
        fore = rq2[c]
        qs[c] = plus(qp[0, c], fore, lm)
        z_start(2, c)
        send_home(1, 0, d, plus(ownk[0, c], back, rk))
        send_home(0, 1, d, plus(ownq[1, c], fore, lq))
    for d in order:
        c = dest(d)
        z_got(3, c)
        send_home(1, 1, d, plus(ownk[1, c], rk1[c], top))
        z_got(2, c)
        send_home(0, 0, d, plus(ownq[0, c], rq1[c], low))
    for i in range(4):
        for d in (1, 2, 3):
            x_copy(i // 2, i % 2, d).wait_recv()
    for i in range(4):
        for c in range(XN):
            pl.when((top, low)[i % 2])(z_copy(i, c).wait_send)
        for d in (1, 2, 3):
            x_copy(i // 2, i % 2, d).wait_send()


def unpack_kernel(qhome, khome, dq_out, dk_out, dv_out):
    for a, out, n in ((0, dq_out, 4), (0, dk_out, 2), (1, dv_out, 2)):
        home = qhome if n == 4 else khome
        step = 128 // n
        for part in range(n):
            lanes = (part if n == 4 else 2 * part + a) * HEAD
            pieces = []
            for xs in range(XN):
                for head in range(2):
                    pieces.append(home[head, xs][:, lanes : lanes + HEAD])
            out[part * step : (part + 1) * step, :] = jnp.concatenate(pieces, axis=1)


VM = pl.BlockSpec(memory_space=pltpu.VMEM)
SM = pl.BlockSpec(memory_space=pltpu.SMEM)
LIMIT = 26 * 1024 * 1024
BIG = pltpu.CompilerParams(vmem_limit_bytes=LIMIT)
HB = pl.BlockSpec(memory_space=pltpu.HBM)
DMA = pltpu.SemaphoreType.DMA


def remote(number, limit=26):
    return pltpu.CompilerParams(vmem_limit_bytes=limit * 1024 * 1024, collective_id=number, has_side_effects=True)


def buf(*shape, dtype=jnp.bfloat16):
    return pltpu.VMEM(shape, dtype)


def out(*shape, dtype=jnp.bfloat16):
    return jax.ShapeDtypeStruct(shape, dtype)


def shards(queries, key_vectors, value_vectors, out_grad, doc_lengths):
    rows, width = queries.shape[1], queries.shape[2]
    chunk = (XN, 64, 4 * HEAD)
    small = (XN, 32, 4 * HEAD)
    block = out(2048, HEAD)
    stat = out(8, 4, TILE, dtype=jnp.float32)
    todo = pltpu.SMEM((4, 64), jnp.int32)
    qs, dos, ks, vs, near = pl.pallas_call(
        gather_kernel,
        out_shape=(block,) * 4 + (stat,),
        name="gather",
        in_specs=[SM, VM],
        out_specs=(VM,) * 5,
        scratch_shapes=[buf(4, *chunk), buf(4, *chunk)] + [buf(*chunk)] * 6
        + [DMA((4, 3)), DMA((4, 3)), DMA((4, 4)), DMA((4, 4))],
        compiler_params=remote(0),
    )(doc_lengths, jnp.concatenate([queries, out_grad, key_vectors, value_vectors]))
    mine = pl.pallas_call(
        stats_kernel,
        name="stats",
        out_shape=stat,
        in_specs=[SM] + [VM] * 5,
        out_specs=VM,
        scratch_shapes=[todo],
        compiler_params=BIG,
    )(doc_lengths, qs, dos, ks, vs, near)
    others = pl.pallas_call(
        share_kernel,
        name="share",
        out_shape=(stat,) * 4,
        in_specs=[VM],
        out_specs=(VM,) * 4,
        scratch_shapes=[DMA((4,)), DMA((4,))],
        compiler_params=remote(1),
    )(mine)
    acc = out(8, TILE, HEAD, dtype=jnp.float32)
    qp, kp, *partial = pl.pallas_call(
        grads_kernel,
        name="grads",
        out_shape=(out(2, *small), out(2, *chunk), stat, out(8, HEAD, TILE, dtype=jnp.float32), acc, acc),
        in_specs=[SM] + [VM] * 9,
        out_specs=(VM,) * 6,
        scratch_shapes=[todo, buf(8, HEAD, TILE)],
        compiler_params=BIG,
    )(doc_lengths, qs, dos, ks, vs, mine, *others)
    home = pl.pallas_call(
        scatter_kernel,
        name="scatter",
        out_shape=(out(2, *small), out(2, *chunk)),
        in_specs=[SM] + [VM] * 10,
        out_specs=(VM,) * 2,
        scratch_shapes=[buf(8, HEAD, TILE), buf(2, *small), buf(2, *chunk),
                        buf(*small), buf(*chunk), buf(*small), buf(*chunk), buf(*small), buf(*chunk),
                        buf(2, *small), buf(2, *chunk),
                        DMA((4, 4)), DMA((4, 4)), DMA((4, 3)), DMA((4, 3))],
        compiler_params=remote(2),
    )(doc_lengths, qs, dos, ks, vs, *partial, qp, kp)
    full = out(rows, width)
    grads = pl.pallas_call(
        unpack_kernel,
        name="unpack",
        out_shape=(full,) * 3,
        in_specs=[VM, VM],
        out_specs=(VM,) * 3,
        compiler_params=BIG,
    )(*home)
    return tuple(g[None] for g in grads)


def solution(mesh):
    spec = P("section", "seq", "dp")
    return jax.shard_map(
        shards,
        mesh=mesh,
        in_specs=(spec, spec, spec, spec, P()),
        out_specs=(spec, spec, spec),
        check_vma=False,
    )
```

```python
import functools

import jax
import jax.numpy as jnp
from jax import lax
from jax.experimental import pallas as pl
from jax.experimental.pallas import tpu as pltpu
from jax.sharding import PartitionSpec as P

HEAD = 224
ZN, XN = 8, 4
SCALE = HEAD ** (-0.5)
NEG = -1e30
LOW = -1e20
TILE = 256
GROUP = 4
ITEMS = ((0, 3), (1, 3), (2, 3), (0, 2), (1, 2), (2, 2), (3, 0), (3, 1), (3, 2), (2, 0), (2, 1))

LATE = tuple(item for item in ITEMS if 2 in item)


class Docs:
    def __init__(self, lengths):
        self.bounds = []
        total = jnp.int32(0)
        for d in range(8):
            total = total + lengths[d]
            self.bounds.append(total)

    def start(self, t):
        r = jnp.int32(0)
        for b in self.bounds[:7]:
            r = jnp.where(b <= t, b, r)
        return r

    def end(self, t):
        r = jnp.int32(4096)
        for b in reversed(self.bounds):
            r = jnp.where(b > t, b, r)
        return r

    def row_start(self, pos):
        r = jnp.zeros_like(pos)
        for b in self.bounds[:7]:
            r = jnp.where(pos >= b, b, r)
        return r

    def case(self, t):
        before = t - self.start(t - 1)
        after = self.end(t - 1) - t
        keys = after > 1024
        return keys, (before > 1024) & jnp.logical_not(keys)


def slots(docs, z):
    lk, lq = docs.case(z * 512)
    rk, rq = docs.case(z * 512 + 512)
    lm = jnp.logical_not(lk | lq)
    rm = jnp.logical_not(rk | rq)
    q_ids = (z, z + 1, jnp.where(rq, z + 1, z + 2), z)
    k_ids = (z, z - 1, jnp.where(lk, z - 1, z - 2), z)
    valid = {
        (0, 3): True,
        (1, 3): jnp.logical_not(rk),
        (2, 3): rm,
        (0, 2): lk,
        (1, 2): lk & jnp.logical_not(rk),
        (2, 2): (lk & rm) | (rq & lm),
        (3, 0): True,
        (3, 1): jnp.logical_not(lq),
        (3, 2): lm,
        (2, 0): rq,
        (2, 1): rq & jnp.logical_not(lq),
    }
    return q_ids, k_ids, valid


NT = (((1,), (1,)), ((), ()))


def list_tiles(docs, z, todo, items):
    q_ids, k_ids, valid = slots(docs, z)
    firsts = [[docs.start(q_ids[qs] * 512 + qt * TILE) for qt in range(2)] for qs in range(4)]
    count = jnp.int32(0)
    for qs, ks in items:
        qid, kid, ok = q_ids[qs], k_ids[ks], valid[(qs, ks)]
        use = (qid < ZN) & (kid >= 0) & ok
        for qt in range(2):
            q0 = qid * 512 + qt * TILE
            for kt in range(2):
                k0 = kid * 512 + kt * TILE
                k1 = k0 + TILE - 1
                hit = use & (k0 <= q0 + TILE - 1) & ((k1 >= q0) | (k1 >= firsts[qs][qt]))
                todo[0, count] = 2 * qs + qt
                todo[1, count] = 2 * ks + kt
                todo[2, count] = q0
                todo[3, count] = k0
                count = count + jnp.where(hit, 1, 0)
    for i in range(GROUP - 1):
        todo[0, count + i] = 0
        todo[1, count + i] = 0
        todo[2, count + i] = 0
        todo[3, count + i] = 1 << 20
    return count


def for_groups(count, todo, body):
    @pl.loop(0, (count + GROUP - 1) // GROUP)
    def _(g):
        body([tuple(todo[j, g * GROUP + i] for j in range(4)) for i in range(GROUP)])


def tile_rows(ref, i):
    return ref[pl.ds(pl.multiple_of(i * TILE, TILE), TILE), :]


def raw_scores(k, q):
    return lax.dot_general(k, q, NT, preferred_element_type=jnp.float32)


def masked(docs, s, q0, k0):
    kpos = k0 + lax.broadcasted_iota(jnp.int32, (TILE, 1), 0)
    qpos = q0 + lax.broadcasted_iota(jnp.int32, (1, TILE), 1)
    qstart = docs.row_start(qpos)
    return jnp.where((kpos <= qpos) & (kpos >= qstart), s * SCALE, NEG)


FAR = 1 << 20


def diagonal_tiles(z):
    a, b = z * 512, z * 512 + TILE
    return [
        (0, a, [(6, a)]),
        (1, b, [(6, a), (7, b)]),
        (6, a, [(0, a)]),
        (7, b, [(0, a), (1, b)]),
    ]


def near_tiles(docs, z):
    _, lq = docs.case(z * 512)
    rk, _ = docs.case(z * 512 + 512)
    a, b = z * 512, z * 512 + TILE
    fore = jnp.where(jnp.logical_not(rk) & (z < ZN - 1), a, FAR)
    back = jnp.where(jnp.logical_not(lq) & (z > 0), a - 512, FAR)
    tiles = diagonal_tiles(z)
    for i in (2, 3):
        tiles[i][2].extend([(2, back), (3, back + TILE)])
    for i in range(2):
        tiles.append((2 + i, a + 512 + i * TILE, [(6, fore), (7, fore + TILE)]))
    return tiles


def near_stats(docs, z, q_ref, do_ref, k_ref, v_ref, st_ref):
    for qi, q0, keys in near_tiles(docs, z):
        raw = []
        for ki, k0 in keys:
            s = raw_scores(tile_rows(k_ref, ki), tile_rows(q_ref, qi))
            raw.append((masked(docs, s, q0, k0), raw_scores(tile_rows(v_ref, ki), tile_rows(do_ref, qi))))
        m = jnp.full((1, TILE), LOW, jnp.float32)
        for s, dp in raw:
            m = jnp.maximum(m, jnp.max(s, axis=0, keepdims=True))
        l = jnp.zeros((1, TILE), jnp.float32)
        d = jnp.zeros((1, TILE), jnp.float32)
        for s, dp in raw:
            p = jnp.exp(s - m)
            l = l + jnp.sum(p, axis=0, keepdims=True)
            d = d + jnp.sum(p * dp, axis=0, keepdims=True)
        st_ref[qi, 0:1, :] = m
        st_ref[qi, 1:2, :] = l
        st_ref[qi, 2:3, :] = d
    for qi in (4, 5):
        st_ref[qi, 0:1, :] = jnp.full((1, TILE), LOW, jnp.float32)
        st_ref[qi, 1:3, :] = jnp.zeros((2, TILE), jnp.float32)


def stats_kernel(len_ref, q_ref, do_ref, k_ref, v_ref, near, st_ref, todo):
    z = lax.axis_index("seq") // XN
    docs = Docs(len_ref)
    st_ref[...] = near[...]

    def body(tiles):
        raw = []
        for qi, ki, q0, k0 in tiles:
            s = raw_scores(tile_rows(k_ref, ki), tile_rows(q_ref, qi))
            raw.append((s, raw_scores(tile_rows(v_ref, ki), tile_rows(do_ref, qi))))
        for (qi, ki, q0, k0), (s, dp) in zip(tiles, raw):
            s = masked(docs, s, q0, k0)
            old = st_ref[qi, 0:1, :]
            new = jnp.maximum(old, jnp.max(s, axis=0, keepdims=True))
            p = jnp.exp(s - new)
            alpha = jnp.exp(old - new)
            st_ref[qi, 0:1, :] = new
            st_ref[qi, 1:2, :] = st_ref[qi, 1:2, :] * alpha + jnp.sum(p, axis=0, keepdims=True)
            st_ref[qi, 2:3, :] = st_ref[qi, 2:3, :] * alpha + jnp.sum(p * dp, axis=0, keepdims=True)

    for_groups(list_tiles(docs, z, todo, LATE), todo, body)


def combine_stats(docs, z, mine, up1, up2, down1, down2):
    lk, lq = docs.case(z * 512)
    rk, rq = docs.case(z * 512 + 512)
    lm = jnp.logical_not(lk | lq)
    rm = jnp.logical_not(rk | rq)
    bk, bq = docs.case(z * 512 - 512)
    bm = jnp.logical_not(bk | bq) & (z >= 2)

    def part(ref, slot, use=None):
        m, l, d = (ref[2 * slot : 2 * slot + 2, r : r + 1, :] for r in range(3))
        if use is not None:
            m = jnp.where(use, m, LOW)
            l = jnp.where(use, l, 0.0)
            d = jnp.where(use, d, 0.0)
        return m, l, d

    groups = (
        (part(mine, 0), part(down1, 1, z >= 1), part(down2, 2, bm)),
        (part(mine, 1), part(up1, 0, z + 1 < ZN), part(down1, 2, lm & (z >= 1))),
        (part(mine, 2), part(up2, 0, rm & (z + 2 < ZN)), part(up1, 1, rm & (z + 1 < ZN)), part(up1, 3, rq & (z + 1 < ZN))),
        (part(mine, 3), part(down1, 2, lq & (z >= 1))),
    )
    out = []
    for parts in groups:
        m = functools.reduce(jnp.maximum, [p[0] for p in parts])
        l = sum(p[1] * jnp.exp(p[0] - m) for p in parts)
        d = sum(p[2] * jnp.exp(p[0] - m) for p in parts)
        inv = jnp.where(l > 0.0, 1.0 / jnp.where(l > 0.0, l, 1.0), 0.0)
        out.append((m, inv, d * inv))
    return out


def tile_grads(docs, tiles, q_ref, do_ref, k_ref, v_ref, stat, kt_ref):
    raw = []
    for qi, ki, q0, k0 in tiles:
        s = raw_scores(tile_rows(k_ref, ki), tile_rows(q_ref, qi))
        raw.append((s, raw_scores(tile_rows(v_ref, ki), tile_rows(do_ref, qi))))
    weights = []
    for (qi, ki, q0, k0), (s, dp) in zip(tiles, raw):
        p = jnp.exp(masked(docs, s, q0, k0) - stat[qi, 0:1, :]) * stat[qi, 1:2, :]
        weights.append((p.astype(jnp.bfloat16), (p * (dp - stat[qi, 2:3, :])).astype(jnp.bfloat16)))
    terms = []
    for (qi, ki, q0, k0), (p, ds) in zip(tiles, weights):
        terms.append((
            jnp.dot(p, tile_rows(do_ref, qi), preferred_element_type=jnp.float32),
            jnp.dot(ds, tile_rows(q_ref, qi), preferred_element_type=jnp.float32),
            jnp.dot(kt_ref[ki], ds, preferred_element_type=jnp.float32),
        ))
    return terms


def pack_pair(first, second):
    return jnp.concatenate([first[:64], second[:64], first[64:], second[64:]], axis=1)


def pack_query(dqt, q_out, half):
    dq = (dqt * SCALE).T.astype(jnp.bfloat16)
    for i in range(2):
        r = i * 128
        q_out[2 * half + i] = jnp.concatenate([dq[r + 32 * j : r + 32 * j + 32] for j in range(4)], axis=1)


def pack_keys(dk, dv, k_out, half):
    dk = (dk * SCALE).astype(jnp.bfloat16)
    dv = dv.astype(jnp.bfloat16)
    for i in range(2):
        r = i * 128
        k_out[2 * half + i] = pack_pair(dk[r : r + 128], dv[r : r + 128])


def grads_kernel(len_ref, q_ref, do_ref, k_ref, v_ref, mine, up1, up2, down1, down2,
                 qp_ref, kp_ref, stat, dqt, dk_acc, dv_acc, todo, kt_ref):
    z = lax.axis_index("seq") // XN
    docs = Docs(len_ref)
    for qs, values in enumerate(combine_stats(docs, z, mine, up1, up2, down1, down2)):
        for r, value in enumerate(values):
            stat[2 * qs : 2 * qs + 2, r : r + 1, :] = value
    for i in range(8):
        kt_ref[i] = k_ref[i * TILE : (i + 1) * TILE, :].T
    dqt[...] = jnp.zeros_like(dqt)
    dk_acc[...] = jnp.zeros_like(dk_acc)
    dv_acc[...] = jnp.zeros_like(dv_acc)

    def body(tiles):
        for (qi, ki, q0, k0), (dv, dk, dq) in zip(tiles, tile_grads(docs, tiles, q_ref, do_ref, k_ref, v_ref, stat, kt_ref)):
            dv_acc[ki] += dv
            dk_acc[ki] += dk
            dqt[qi] += dq

    for_groups(list_tiles(docs, z, todo, LATE), todo, body)
    for half in range(2):
        pack_query(dqt[4 + half], qp_ref, half)
        pack_keys(dk_acc[4 + half], dv_acc[4 + half], kp_ref, half)


def copy_to(src, dst, send, recv, device):
    return pltpu.make_async_remote_copy(
        src_ref=src,
        dst_ref=dst,
        send_sem=send,
        recv_sem=recv,
        device_id={"seq": device},
        device_id_type=pl.DeviceIdType.MESH,
    )


def meet(devices):
    for device in devices:
        pl.semaphore_signal(
            pltpu.get_barrier_semaphore(), inc=1, device_id={"seq": device}, device_id_type=pl.DeviceIdType.MESH
        )


def greet(devices):
    meet(devices)
    pl.semaphore_wait(pltpu.get_barrier_semaphore(), len(devices))


def window(ref, off):
    low = off // 128 * 128
    high = -(-(off + HEAD) // 128) * 128
    return ref[:, low:high][:, off - low : off - low + HEAD]


def place():
    me = lax.axis_index("seq")
    z, x = me // XN, me % XN
    up = lax.rem(z + 1, ZN) * XN + x
    down = lax.rem(z + ZN - 1, ZN) * XN + x
    peer = [z * XN + lax.rem(x + d, XN) for d in range(XN)]
    return z, x, up, down, peer


TYPES = (("q", 0), ("k", 1), ("q", 1), ("k", 0))


def gather_kernel(len_ref, raw, q_out, do_out, k_out, v_out, near,
                  packed, own, q1, k1, qsel, ksel, q2, k2,
                  x_send, x_recv, z_send, z_recv):
    z, x, up, down, peer = place()
    low, top = z > 0, z < ZN - 1
    meet(peer[1:])
    pl.when(low)(lambda: meet([down]))
    pl.when(top)(lambda: meet([up]))
    docs = Docs(len_ref)
    lk, lq = docs.case(z * 512)
    rk, rq = docs.case(z * 512 + 512)

    def pack(t, xp):
        kind, head = TYPES[t]
        i = 0 if kind == "q" else 2
        off = (2 * xp + head) * HEAD
        packed[t, xp] = pack_pair(window(raw.at[i], off), window(raw.at[i + 1], off))

    def x_copy(t, d):
        to = lax.rem(x + d, XN)
        return copy_to(packed.at[t, to], own.at[t, x], x_send.at[t, d - 1], x_recv.at[t, d - 1], peer[d])

    def z_copy(i, c):
        src, dst, to = ((own.at[0, c], q1.at[c], down), (own.at[1, c], k1.at[c], up),
                        (qsel.at[c], q2.at[c], down), (ksel.at[c], k2.at[c], up))[i]
        return copy_to(src, dst, z_send.at[i, c], z_recv.at[i, c], to)

    def z_start(i, c):
        pl.when((low, top)[i % 2])(lambda: z_copy(i, c).start())

    def z_got(i, c):
        pl.when((top, low)[i % 2])(lambda: z_copy(i, c).wait_recv())

    def unpack(value, slot, c, first, second):
        row = slot * 512 + c * 128
        upper = pl.ds(pl.multiple_of(row, 64), 64)
        lower = pl.ds(pl.multiple_of(row + 64, 64), 64)
        first[upper, :] = value[:, 0:HEAD]
        second[upper, :] = value[:, HEAD : 2 * HEAD]
        first[lower, :] = value[:, 2 * HEAD : 3 * HEAD]
        second[lower, :] = value[:, 3 * HEAD : 4 * HEAD]

    def source(d):
        return lax.rem(x + d, XN)

    def got_x(t, d):
        back = XN - d
        copy_to(packed.at[t, x], own.at[t, source(d)], x_send.at[t, back - 1], x_recv.at[t, back - 1], peer[d]).wait_recv()

    def second(i, c):
        z_got(i - 2, c)
        if i == 2:
            qsel[c] = jnp.where(lq, own[2, c], q1[c])
        else:
            ksel[c] = jnp.where(rk, own[3, c], k1[c])
        z_start(i, c)

    def first(t, d):
        got_x(t, d)
        z_start(t, source(d))

    def unpack_own(t, c):
        unpack(own[t, c], *((0, c, q_out, do_out), (0, c, k_out, v_out), (3, c, q_out, do_out), (3, c, k_out, v_out))[t])

    for xp in range(XN):
        pack(0, xp)
    own[0, x] = packed[0, x]
    pl.semaphore_wait(pltpu.get_barrier_semaphore(), 3 + jnp.where(low, 1, 0) + jnp.where(top, 1, 0))
    for d in (1, 3):
        x_copy(0, d).start()
    z_start(0, x)
    for xp in range(XN):
        pack(1, xp)
    own[1, x] = packed[1, x]
    for d in (1, 3):
        x_copy(1, d).start()
    z_start(1, x)
    for t in (0, 1):
        x_copy(t, 2).start()
    for t in (2, 3):
        for xp in range(XN):
            pack(t, xp)
        own[t, x] = packed[t, x]
    second(2, x)
    second(3, x)
    unpack_own(0, x)
    unpack_own(1, x)
    first(0, 1)
    first(0, 3)
    first(1, 1)
    first(1, 3)
    for d in (1, 3):
        x_copy(2, d).start()
        x_copy(3, d).start()
    unpack_own(2, x)
    unpack_own(3, x)
    for t in (0, 1):
        unpack_own(t, source(1))
        unpack_own(t, source(3))
    first(0, 2)
    first(1, 2)
    x_copy(2, 2).start()
    x_copy(3, 2).start()
    unpack(q1[x], 1, x, q_out, do_out)
    unpack(k1[x], 1, x, k_out, v_out)
    for t in (0, 1):
        unpack_own(t, source(2))
    for d in (1, 3, 2):
        c = source(d)
        for t in (2, 3):
            got_x(t, d)
            second(t, c)
        unpack(q1[c], 1, c, q_out, do_out)
        unpack(k1[c], 1, c, k_out, v_out)
        unpack_own(2, c)
        unpack_own(3, c)
    @pl.when(jnp.logical_not(top))
    def _():
        q_out[512:1024, :] = jnp.zeros((512, HEAD), jnp.bfloat16)
        do_out[512:1024, :] = jnp.zeros((512, HEAD), jnp.bfloat16)

    @pl.when(jnp.logical_not(low))
    def _():
        k_out[512:1024, :] = jnp.zeros((512, HEAD), jnp.bfloat16)
        v_out[512:1024, :] = jnp.zeros((512, HEAD), jnp.bfloat16)

    near_stats(docs, z, q_out, do_out, k_out, v_out, near)
    for d in (0, 1, 3, 2):
        c = source(d)
        z_got(2, c)
        unpack(q2[c], 2, c, q_out, do_out)
        z_got(3, c)
        unpack(k2[c], 2, c, k_out, v_out)
    for t in range(4):
        for d in (1, 2, 3):
            x_copy(t, d).wait_send()
    for t in range(4):
        for c in range(XN):
            pl.when((low, top)[t % 2])(z_copy(t, c).wait_send)


def share_kernel(mine, up1, up2, down1, down2, send, recv):
    z, x, up, down, _ = place()
    upper = lax.rem(z + 2, ZN) * XN + x
    lower = lax.rem(z + ZN - 2, ZN) * XN + x
    greet([up, upper, down, lower])
    copies = []
    for i, (ref, tiles, to) in enumerate(((up1, (0, 8), down), (down1, (2, 4), up), (up2, (0, 2), lower), (down2, (4, 2), upper))):
        part = pl.ds(*tiles)
        copies.append(copy_to(mine.at[part], ref.at[part], send.at[i], recv.at[i], to))
    for copy in copies:
        copy.start()
    for copy in copies:
        copy.wait()


def scatter_kernel(len_ref, q_ref, do_ref, k_ref, v_ref, stat, dqt, dk_acc, dv_acc, qp, kp, qhome, khome,
                   kt_ref, ownq, ownk, q1p, k1p, rq2, rk2, rq1, rk1, qs, ks, qfin, kfin,
                   z_send, z_recv, x_send, x_recv):
    z, x, up, down, peer = place()
    docs = Docs(len_ref)
    lk, lq = docs.case(z * 512)
    rk, rq = docs.case(z * 512 + 512)
    low, top = z >= 1, z < ZN - 1
    lm = jnp.logical_not(lk | lq) & low
    rm = jnp.logical_not(rk | rq) & top
    lq, rk = lq & low, rk & top

    def z_start(i, c):
        pl.when((top, low)[i % 2])(lambda: z_copy(i, c).start())

    def z_got(i, c):
        pl.when((low, top)[i % 2])(lambda: z_copy(i, c).wait_recv())

    def z_copy(i, c):
        src, dst, to = ((qp.at[c], rq2.at[c], up), (kp.at[c], rk2.at[c], down),
                        (qs.at[c], rq1.at[c], up), (ks.at[c], rk1.at[c], down))[i]
        return copy_to(src, dst, z_send.at[i, c], z_recv.at[i, c], to)

    def plus(a, b, use):
        return (a.astype(jnp.float32) + jnp.where(use, b.astype(jnp.float32), 0.0)).astype(jnp.bfloat16)

    def dest(d):
        return lax.rem(x + d, XN)

    def x_copy(kind, head, d):
        src, dst = ((qfin, qhome), (kfin, khome))[kind]
        i = 2 * kind + head
        return copy_to(src.at[head, dest(d)], dst.at[head, x], x_send.at[i, d - 1], x_recv.at[i, d - 1], peer[d])

    def send_home(kind, head, d, value):
        src, dst = ((qfin, qhome), (kfin, khome))[kind]
        if d:
            src[head, dest(d)] = value
            x_copy(kind, head, d).start()
        else:
            dst[head, x] = value

    order = (2, 1, 3, 0)
    meet(peer[1:])
    pl.when(low)(lambda: meet([down]))
    pl.when(top)(lambda: meet([up]))
    pl.semaphore_wait(pltpu.get_barrier_semaphore(), 3 + jnp.where(low, 1, 0) + jnp.where(top, 1, 0))
    def second(d):
        z_start(1, dest(d))
        z_start(0, dest(d))

    for d in order:
        z_start(1, dest(d))
    for d in order:
        z_start(0, dest(d))

    def near_grads(head):
        tiles = [tile for tile in near_tiles(docs, z) if (tile[0] >= 6) == bool(head)]
        for ki in (range(4), (6, 7))[1 - head]:
            kt_ref[ki] = tile_rows(k_ref, ki).T
        pairs = [(qi, ki, q0, k0) for qi, q0, keys in tiles for ki, k0 in keys]
        terms = tile_grads(docs, pairs, q_ref, do_ref, k_ref, v_ref, stat, kt_ref)
        for qi in sorted({p[0] for p in pairs}):
            dq = dqt[qi] + sum(t[2] for p, t in zip(pairs, terms) if p[0] == qi)
            pack_query(dq, (ownq.at[0], q1p, None, ownq.at[1])[qi // 2], qi % 2)
        for ki in sorted({p[1] for p in pairs}):
            dk = dk_acc[ki] + sum(t[1] for p, t in zip(pairs, terms) if p[1] == ki)
            dv = dv_acc[ki] + sum(t[0] for p, t in zip(pairs, terms) if p[1] == ki)
            pack_keys(dk, dv, (ownk.at[1], k1p, None, ownk.at[0])[ki // 2], ki % 2)

    def key_home(d):
        c = dest(d)
        z_got(1, c)
        send_home(1, 0, d, plus(ownk[0, c], rk2[c], rk))

    near_grads(0)
    for d in order:
        c = dest(d)
        z_got(0, c)
        qs[c] = plus(q1p[c], rq2[c], lm)
        z_start(2, c)
    key_home(order[0])
    key_home(order[1])
    near_grads(1)
    for n, d in enumerate(order):
        c = dest(d)
        if n >= 2:
            key_home(d)
        ks[c] = plus(k1p[c], rk2[c], rm)
        z_start(3, c)
        send_home(0, 1, d, plus(ownq[1, c], rq2[c], lq))
    for d in order:
        c = dest(d)
        z_got(2, c)
        send_home(0, 0, d, plus(ownq[0, c], rq1[c], low))
    for d in order:
        c = dest(d)
        z_got(3, c)
        send_home(1, 1, d, plus(ownk[1, c], rk1[c], top))
    for i in range(4):
        for d in (1, 2, 3):
            x_copy(i // 2, i % 2, d).wait_recv()
    for i in range(4):
        for c in range(XN):
            pl.when((top, low)[i % 2])(z_copy(i, c).wait_send)
        for d in (1, 2, 3):
            x_copy(i // 2, i % 2, d).wait_send()


def unpack_kernel(qhome, khome, dq_out, dk_out, dv_out):
    for a, out, n in ((0, dq_out, 4), (0, dk_out, 2), (1, dv_out, 2)):
        home = qhome if n == 4 else khome
        step = 128 // n
        for part in range(n):
            lanes = (part if n == 4 else 2 * part + a) * HEAD
            pieces = []
            for xs in range(XN):
                for head in range(2):
                    pieces.append(home[head, xs][:, lanes : lanes + HEAD])
            out[part * step : (part + 1) * step, :] = jnp.concatenate(pieces, axis=1)


VM = pl.BlockSpec(memory_space=pltpu.VMEM)
SM = pl.BlockSpec(memory_space=pltpu.SMEM)
LIMIT = 26 * 1024 * 1024
BIG = pltpu.CompilerParams(vmem_limit_bytes=LIMIT)
HB = pl.BlockSpec(memory_space=pltpu.HBM)
DMA = pltpu.SemaphoreType.DMA


def remote(number, limit=26):
    return pltpu.CompilerParams(vmem_limit_bytes=limit * 1024 * 1024, collective_id=number, has_side_effects=True)


def buf(*shape, dtype=jnp.bfloat16):
    return pltpu.VMEM(shape, dtype)


def out(*shape, dtype=jnp.bfloat16):
    return jax.ShapeDtypeStruct(shape, dtype)


def shards(queries, key_vectors, value_vectors, out_grad, doc_lengths):
    rows, width = queries.shape[1], queries.shape[2]
    chunk = (XN, 64, 4 * HEAD)
    small = (XN, 32, 4 * HEAD)
    block = out(2048, HEAD)
    stat = out(8, 4, TILE, dtype=jnp.float32)
    todo = pltpu.SMEM((4, 64), jnp.int32)
    qs, dos, ks, vs, near = pl.pallas_call(
        gather_kernel,
        out_shape=(block,) * 4 + (stat,),
        name="gather",
        in_specs=[SM, VM],
        out_specs=(VM,) * 5,
        scratch_shapes=[buf(4, *chunk), buf(4, *chunk)] + [buf(*chunk)] * 6
        + [DMA((4, 3)), DMA((4, 3)), DMA((4, 4)), DMA((4, 4))],
        compiler_params=remote(0),
    )(doc_lengths, jnp.concatenate([queries, out_grad, key_vectors, value_vectors]))
    mine = pl.pallas_call(
        stats_kernel,
        name="stats",
        out_shape=stat,
        in_specs=[SM] + [VM] * 5,
        out_specs=VM,
        scratch_shapes=[todo],
        compiler_params=BIG,
    )(doc_lengths, qs, dos, ks, vs, near)
    others = pl.pallas_call(
        share_kernel,
        name="share",
        out_shape=(stat,) * 4,
        in_specs=[VM],
        out_specs=(VM,) * 4,
        scratch_shapes=[DMA((4,)), DMA((4,))],
        compiler_params=remote(1),
    )(mine)
    acc = out(8, TILE, HEAD, dtype=jnp.float32)
    qp, kp, *partial = pl.pallas_call(
        grads_kernel,
        name="grads",
        out_shape=(out(*small), out(*chunk), stat, out(8, HEAD, TILE, dtype=jnp.float32), acc, acc),
        in_specs=[SM] + [VM] * 9,
        out_specs=(VM,) * 6,
        scratch_shapes=[todo, buf(8, HEAD, TILE)],
        compiler_params=BIG,
    )(doc_lengths, qs, dos, ks, vs, mine, *others)
    home = pl.pallas_call(
        scatter_kernel,
        name="scatter",
        out_shape=(out(2, *small), out(2, *chunk)),
        in_specs=[SM] + [VM] * 10,
        out_specs=(VM,) * 2,
        scratch_shapes=[buf(8, HEAD, TILE), buf(2, *small), buf(2, *chunk), buf(*small), buf(*chunk),
                        buf(*small), buf(*chunk), buf(*small), buf(*chunk), buf(*small), buf(*chunk),
                        buf(2, *small), buf(2, *chunk),
                        DMA((4, 4)), DMA((4, 4)), DMA((4, 3)), DMA((4, 3))],
        compiler_params=remote(2),
    )(doc_lengths, qs, dos, ks, vs, *partial, qp, kp)
    full = out(rows, width)
    grads = pl.pallas_call(
        unpack_kernel,
        name="unpack",
        out_shape=(full,) * 3,
        in_specs=[VM, VM],
        out_specs=(VM,) * 3,
        compiler_params=BIG,
    )(*home)
    return tuple(g[None] for g in grads)


def solution(mesh):
    spec = P("section", "seq", "dp")
    return jax.shard_map(
        shards,
        mesh=mesh,
        in_specs=(spec, spec, spec, spec, P()),
        out_specs=(spec, spec, spec),
        check_vma=False,
    )
```

```python
import functools
import math

import jax
import jax.numpy as jnp
from jax import lax
from jax.experimental import pallas as pl
from jax.experimental.pallas import tpu as pltpu
from jax.sharding import PartitionSpec as P

HEAD = 224
ZN, XN = 8, 4
SCALE = HEAD ** (-0.5)
NEG = -1e30
LOG2E = math.log2(math.e)
LOW = -1e20
TILE = 256
GROUP = 4
ITEMS = ((0, 3), (1, 3), (2, 3), (0, 2), (1, 2), (2, 2), (3, 0), (3, 1), (3, 2), (2, 0), (2, 1))

LATE = tuple(item for item in ITEMS if 2 in item)


class Docs:
    def __init__(self, lengths):
        self.bounds = []
        total = jnp.int32(0)
        for d in range(8):
            total = total + lengths[d]
            self.bounds.append(total)

    def start(self, t):
        r = jnp.int32(0)
        for b in self.bounds[:7]:
            r = jnp.where(b <= t, b, r)
        return r

    def end(self, t):
        r = jnp.int32(4096)
        for b in reversed(self.bounds):
            r = jnp.where(b > t, b, r)
        return r

    def row_start(self, pos):
        r = jnp.zeros_like(pos)
        for b in self.bounds[:7]:
            r = jnp.where(pos >= b, b, r)
        return r

    def case(self, t):
        before = t - self.start(t - 1)
        after = self.end(t - 1) - t
        keys = after > 1024
        return keys, (before > 1024) & jnp.logical_not(keys)


def slots(docs, z):
    lk, lq = docs.case(z * 512)
    rk, rq = docs.case(z * 512 + 512)
    lm = jnp.logical_not(lk | lq)
    rm = jnp.logical_not(rk | rq)
    q_ids = (z, z + 1, jnp.where(rq, z + 1, z + 2), z)
    k_ids = (z, z - 1, jnp.where(lk, z - 1, z - 2), z)
    valid = {
        (0, 3): True,
        (1, 3): jnp.logical_not(rk),
        (2, 3): rm,
        (0, 2): lk,
        (1, 2): lk & jnp.logical_not(rk),
        (2, 2): (lk & rm) | (rq & lm),
        (3, 0): True,
        (3, 1): jnp.logical_not(lq),
        (3, 2): lm,
        (2, 0): rq,
        (2, 1): rq & jnp.logical_not(lq),
    }
    return q_ids, k_ids, valid


NT = (((1,), (1,)), ((), ()))


def list_tiles(docs, z, todo, items):
    q_ids, k_ids, valid = slots(docs, z)
    firsts = [[docs.start(q_ids[qs] * 512 + qt * TILE) for qt in range(2)] for qs in range(4)]
    count = jnp.int32(0)
    for qs, ks in items:
        qid, kid, ok = q_ids[qs], k_ids[ks], valid[(qs, ks)]
        use = (qid < ZN) & (kid >= 0) & ok
        for qt in range(2):
            q0 = qid * 512 + qt * TILE
            for kt in range(2):
                k0 = kid * 512 + kt * TILE
                k1 = k0 + TILE - 1
                hit = use & (k0 <= q0 + TILE - 1) & ((k1 >= q0) | (k1 >= firsts[qs][qt]))
                todo[0, count] = 2 * qs + qt
                todo[1, count] = 2 * ks + kt
                todo[2, count] = q0
                todo[3, count] = k0
                count = count + jnp.where(hit, 1, 0)
    for i in range(GROUP - 1):
        todo[0, count + i] = 0
        todo[1, count + i] = 0
        todo[2, count + i] = 0
        todo[3, count + i] = -(1 << 20)
    return count


def for_groups(count, todo, body):
    @pl.loop(0, (count + GROUP - 1) // GROUP)
    def _(g):
        body([tuple(todo[j, g * GROUP + i] for j in range(4)) for i in range(GROUP)])


def tile_rows(ref, i):
    return ref[pl.ds(pl.multiple_of(i * TILE, TILE), TILE), :]


def raw_scores(k, q):
    return lax.dot_general(k, q, NT, preferred_element_type=jnp.float32)


def masked(docs, s, q0, k0):
    row = lax.broadcasted_iota(jnp.int32, (TILE, TILE), 0)
    qpos = q0 + lax.broadcasted_iota(jnp.int32, (1, TILE), 1)
    allowed = row >= docs.row_start(qpos) - k0
    if q0 is k0:
        allowed = allowed & (row <= lax.broadcasted_iota(jnp.int32, (1, TILE), 1))
    return jnp.where(allowed, s * (SCALE * LOG2E), NEG)


FAR = -(1 << 20)


def diagonal_tiles(z):
    a, b = z * 512, z * 512 + TILE
    return [
        (0, a, [(6, a)]),
        (1, b, [(6, a), (7, b)]),
        (6, a, [(0, a)]),
        (7, b, [(0, a), (1, b)]),
    ]


def near_tiles(docs, z):
    _, lq = docs.case(z * 512)
    rk, _ = docs.case(z * 512 + 512)
    a, b = z * 512, z * 512 + TILE
    fore = jnp.where(jnp.logical_not(rk) & (z < ZN - 1), a, FAR)
    back = jnp.where(jnp.logical_not(lq) & (z > 0), a - 512, FAR)
    tiles = diagonal_tiles(z)
    for i in (2, 3):
        tiles[i][2].extend([(2, back), (3, back + TILE)])
    for i in range(2):
        tiles.append((2 + i, a + 512 + i * TILE, [(6, fore), (7, fore + TILE)]))
    return tiles


def part_stats(docs, q, do, q0, keys):
    raw = [(masked(docs, raw_scores(k, q), q0, k0), raw_scores(v, do)) for k, v, k0 in keys]
    m = jnp.full((1, TILE), LOW, jnp.float32)
    for s, dp in raw:
        m = jnp.maximum(m, jnp.max(s, axis=0, keepdims=True))
    l = jnp.zeros((1, TILE), jnp.float32)
    d = jnp.zeros((1, TILE), jnp.float32)
    for s, dp in raw:
        p = jnp.exp2(s - m)
        l = l + jnp.sum(p, axis=0, keepdims=True)
        d = d + jnp.sum(p * dp, axis=0, keepdims=True)
    return m, l, d


def put_stats(st_ref, qi, values):
    for r, value in enumerate(values):
        st_ref[qi, r : r + 1, :] = value


def add_stats(st_ref, qi, part, use):
    old = [st_ref[qi, r : r + 1, :] for r in range(3)]
    m = jnp.maximum(old[0], jnp.where(use, part[0], LOW))
    a, b = jnp.exp2(old[0] - m), jnp.where(use, jnp.exp2(part[0] - m), 0.0)
    put_stats(st_ref, qi, (m, old[1] * a + part[1] * b, old[2] * a + part[2] * b))


def near_stats(docs, z, q_ref, do_ref, k_ref, v_ref, st_ref):
    for qi, q0, keys in near_tiles(docs, z):
        tiles = [(tile_rows(k_ref, ki), tile_rows(v_ref, ki), k0) for ki, k0 in keys]
        put_stats(st_ref, qi, part_stats(docs, tile_rows(q_ref, qi), tile_rows(do_ref, qi), q0, tiles))


def late_stats(docs, z, q_ref, do_ref, k_ref, v_ref, st_ref):
    lk, lq = docs.case(z * 512)
    rk, rq = docs.case(z * 512 + 512)
    lm, rm = jnp.logical_not(lk | lq), jnp.logical_not(rk | rq)
    q_ids, k_ids, _ = slots(docs, z)
    here, q2, k2 = z * 512, q_ids[2] * 512, k_ids[2] * 512
    q_ok, k_ok = q_ids[2] < ZN, k_ids[2] >= 0

    def start(use, pos, j):
        return jnp.where(use, pos, FAR) + j * TILE

    def pick(ref, use, one, other):
        return jnp.where(use, tile_rows(ref, one), tile_rows(ref, other))

    own = jnp.logical_not(rk) & q_ok
    both = ((lk & rm) | (rq & lm)) & q_ok & k_ok
    cross = (lk & jnp.logical_not(rk) & (z < ZN - 1) & k_ok) | (rq & jnp.logical_not(lq) & (z > 0) & q_ok)
    for i in range(2):
        keys = [(pick(k_ref, rq, j, 6 + j), pick(v_ref, rq, j, 6 + j), start(own, here, j)) for j in range(2)]
        keys += [(tile_rows(k_ref, 4 + j), tile_rows(v_ref, 4 + j), start(both, k2, j)) for j in range(2)]
        put_stats(st_ref, 4 + i, part_stats(docs, tile_rows(q_ref, 4 + i), tile_rows(do_ref, 4 + i), q2 + i * TILE, keys))
    for i in range(2):
        keys = [(tile_rows(k_ref, 4 + j), tile_rows(v_ref, 4 + j), start(jnp.logical_not(lq) & k_ok, k2, j)) for j in range(2)]
        part = part_stats(docs, pick(q_ref, lk, i, 6 + i), pick(do_ref, lk, i, 6 + i), here + i * TILE, keys)
        add_stats(st_ref, i, part, lk)
        add_stats(st_ref, 6 + i, part, lm)
    for i in range(2):
        keys = [(pick(k_ref, lk, 4 + j, 2 + j), pick(v_ref, lk, 4 + j, 2 + j), start(cross, jnp.where(lk, k2, here - 512), j))
                for j in range(2)]
        part = part_stats(docs, pick(q_ref, lk, 2 + i, 4 + i), pick(do_ref, lk, 2 + i, 4 + i),
                          jnp.where(lk, here + 512, q2) + i * TILE, keys)
        add_stats(st_ref, 2 + i, part, lk)
        add_stats(st_ref, 4 + i, part, jnp.logical_not(lk))


def combine_stats(docs, z, mine, up1, up2, down1, down2):
    lk, lq = docs.case(z * 512)
    rk, rq = docs.case(z * 512 + 512)
    lm = jnp.logical_not(lk | lq)
    rm = jnp.logical_not(rk | rq)
    bk, bq = docs.case(z * 512 - 512)
    bm = jnp.logical_not(bk | bq) & (z >= 2)

    def part(ref, slot, use=None):
        m, l, d = (ref[2 * slot : 2 * slot + 2, r : r + 1, :] for r in range(3))
        if use is not None:
            m = jnp.where(use, m, LOW)
            l = jnp.where(use, l, 0.0)
            d = jnp.where(use, d, 0.0)
        return m, l, d

    groups = (
        (part(mine, 0), part(down1, 1, z >= 1), part(down2, 2, bm)),
        (part(mine, 1), part(up1, 0, z + 1 < ZN), part(down1, 2, lm & (z >= 1))),
        (part(mine, 2), part(up2, 0, rm & (z + 2 < ZN)), part(up1, 1, rm & (z + 1 < ZN)), part(up1, 3, rq & (z + 1 < ZN))),
        (part(mine, 3), part(down1, 2, lq & (z >= 1))),
    )
    out = []
    for parts in groups:
        m = functools.reduce(jnp.maximum, [p[0] for p in parts])
        l = sum(p[1] * jnp.exp2(p[0] - m) for p in parts)
        d = sum(p[2] * jnp.exp2(p[0] - m) for p in parts)
        some = l > 0.0
        l = jnp.where(some, l, 1.0)
        out.append((jnp.where(some, m + jnp.log2(l), -NEG), d / l))
    return out


def tile_grads(docs, tiles, q_ref, do_ref, k_ref, v_ref, stat, kt_ref):
    raw = []
    for qi, ki, q0, k0 in tiles:
        s = raw_scores(tile_rows(k_ref, ki), tile_rows(q_ref, qi))
        raw.append((s, raw_scores(tile_rows(v_ref, ki), tile_rows(do_ref, qi))))
    weights = []
    for (qi, ki, q0, k0), (s, dp) in zip(tiles, raw):
        p = jnp.exp2(masked(docs, s, q0, k0) - stat[qi, 0:1, :])
        weights.append((p.astype(jnp.bfloat16), (p * (dp - stat[qi, 1:2, :])).astype(jnp.bfloat16)))
    terms = []
    for (qi, ki, q0, k0), (p, ds) in zip(tiles, weights):
        terms.append((
            jnp.dot(p, tile_rows(do_ref, qi), preferred_element_type=jnp.float32),
            jnp.dot(ds, tile_rows(q_ref, qi), preferred_element_type=jnp.float32),
            jnp.dot(kt_ref[ki], ds, preferred_element_type=jnp.float32),
        ))
    return terms


def pack_pair(first, second):
    return jnp.concatenate([first[:64], second[:64], first[64:], second[64:]], axis=1)


def pack_query(dqt, q_out, half):
    dq = (dqt * SCALE).T.astype(jnp.bfloat16)
    for i in range(2):
        r = i * 128
        q_out[2 * half + i] = jnp.concatenate([dq[r + 32 * j : r + 32 * j + 32] for j in range(4)], axis=1)


def pack_keys(dk, dv, k_out, half):
    dk = (dk * SCALE).astype(jnp.bfloat16)
    dv = dv.astype(jnp.bfloat16)
    for i in range(2):
        r = i * 128
        k_out[2 * half + i] = pack_pair(dk[r : r + 128], dv[r : r + 128])


def grads_kernel(len_ref, q_ref, do_ref, k_ref, v_ref, stat, qp_ref, kp_ref, dqt, dk_acc, dv_acc, todo, kt_ref):
    z = lax.axis_index("seq") // XN
    docs = Docs(len_ref)
    for i in range(8):
        kt_ref[i] = k_ref[i * TILE : (i + 1) * TILE, :].T
    dqt[...] = jnp.zeros_like(dqt)
    dk_acc[...] = jnp.zeros_like(dk_acc)
    dv_acc[...] = jnp.zeros_like(dv_acc)

    def body(tiles):
        for (qi, ki, q0, k0), (dv, dk, dq) in zip(tiles, tile_grads(docs, tiles, q_ref, do_ref, k_ref, v_ref, stat, kt_ref)):
            dv_acc[ki] += dv
            dk_acc[ki] += dk
            dqt[qi] += dq

    for_groups(list_tiles(docs, z, todo, LATE), todo, body)
    for half in range(2):
        pack_query(dqt[4 + half], qp_ref, half)
        pack_keys(dk_acc[4 + half], dv_acc[4 + half], kp_ref, half)


def copy_to(src, dst, send, recv, device):
    return pltpu.make_async_remote_copy(
        src_ref=src,
        dst_ref=dst,
        send_sem=send,
        recv_sem=recv,
        device_id={"seq": device},
        device_id_type=pl.DeviceIdType.MESH,
    )


def meet(devices):
    for device in devices:
        pl.semaphore_signal(
            pltpu.get_barrier_semaphore(), inc=1, device_id={"seq": device}, device_id_type=pl.DeviceIdType.MESH
        )


def greet(devices):
    meet(devices)
    pl.semaphore_wait(pltpu.get_barrier_semaphore(), len(devices))


def window(ref, off):
    low = off // 128 * 128
    high = -(-(off + HEAD) // 128) * 128
    return ref[:, low:high][:, off - low : off - low + HEAD]


def place():
    me = lax.axis_index("seq")
    z, x = me // XN, me % XN
    up = lax.rem(z + 1, ZN) * XN + x
    down = lax.rem(z + ZN - 1, ZN) * XN + x
    peer = [z * XN + lax.rem(x + d, XN) for d in range(XN)]
    return z, x, up, down, peer


TYPES = (("q", 0), ("k", 1), ("q", 1), ("k", 0))


def gather_kernel(len_ref, raw, q_out, do_out, k_out, v_out, stat,
                  packed, own, q1, k1, qsel, ksel, q2, k2, mine, up1, up2, down1, down2,
                  x_send, x_recv, z_send, z_recv, s_send, s_recv):
    z, x, up, down, peer = place()
    low, top = z > 0, z < ZN - 1
    below, above = z > 1, z < ZN - 2
    upper = lax.rem(z + 2, ZN) * XN + x
    lower = lax.rem(z + ZN - 2, ZN) * XN + x
    meet(peer[1:])
    expected = jnp.int32(3)
    for use, to in ((low, down), (top, up), (below, lower), (above, upper)):
        pl.when(use)(functools.partial(meet, [to]))
        expected = expected + jnp.where(use, 1, 0)

    @pl.when(jnp.logical_not(top))
    def _():
        q1[...] = jnp.zeros_like(q1)
        q2[...] = jnp.zeros_like(q2)

    @pl.when(jnp.logical_not(low))
    def _():
        k1[...] = jnp.zeros_like(k1)
        k2[...] = jnp.zeros_like(k2)

    docs = Docs(len_ref)
    lk, lq = docs.case(z * 512)
    rk, rq = docs.case(z * 512 + 512)

    def pack(t, xp):
        kind, head = TYPES[t]
        i = 0 if kind == "q" else 2
        off = (2 * xp + head) * HEAD
        packed[t, xp] = pack_pair(window(raw.at[i], off), window(raw.at[i + 1], off))

    def x_copy(t, d):
        to = lax.rem(x + d, XN)
        return copy_to(packed.at[t, to], own.at[t, x], x_send.at[t, d - 1], x_recv.at[t, d - 1], peer[d])

    def z_copy(i, c):
        src, dst, to = ((own.at[0, c], q1.at[c], down), (own.at[1, c], k1.at[c], up),
                        (qsel.at[c], q2.at[c], down), (ksel.at[c], k2.at[c], up))[i]
        return copy_to(src, dst, z_send.at[i, c], z_recv.at[i, c], to)

    def z_start(i, c):
        pl.when((low, top)[i % 2])(lambda: z_copy(i, c).start())

    def z_got(i, c):
        pl.when((top, low)[i % 2])(lambda: z_copy(i, c).wait_recv())

    def unpack(value, slot, c, first, second):
        row = slot * 512 + c * 128
        upper = pl.ds(pl.multiple_of(row, 64), 64)
        lower = pl.ds(pl.multiple_of(row + 64, 64), 64)
        first[upper, :] = value[:, 0:HEAD]
        second[upper, :] = value[:, HEAD : 2 * HEAD]
        first[lower, :] = value[:, 2 * HEAD : 3 * HEAD]
        second[lower, :] = value[:, 3 * HEAD : 4 * HEAD]

    def source(d):
        return lax.rem(x + d, XN)

    def got_x(t, d):
        back = XN - d
        copy_to(packed.at[t, x], own.at[t, source(d)], x_send.at[t, back - 1], x_recv.at[t, back - 1], peer[d]).wait_recv()

    def second(i, c):
        z_got(i - 2, c)
        if i == 2:
            qsel[c] = jnp.where(lq, own[2, c], q1[c])
        else:
            ksel[c] = jnp.where(rk, own[3, c], k1[c])
        z_start(i, c)

    def first(t, d):
        got_x(t, d)
        z_start(t, source(d))

    def unpack_own(t, c):
        unpack(own[t, c], *((0, c, q_out, do_out), (0, c, k_out, v_out), (3, c, q_out, do_out), (3, c, k_out, v_out))[t])

    for xp in range(XN):
        pack(0, xp)
    own[0, x] = packed[0, x]
    pl.semaphore_wait(pltpu.get_barrier_semaphore(), expected)
    for d in (1, 3):
        x_copy(0, d).start()
    z_start(0, x)
    for xp in range(XN):
        pack(1, xp)
    own[1, x] = packed[1, x]
    for d in (1, 3):
        x_copy(1, d).start()
    z_start(1, x)
    for t in (0, 1):
        x_copy(t, 2).start()
    for t in (2, 3):
        for xp in range(XN):
            pack(t, xp)
        own[t, x] = packed[t, x]
    second(2, x)
    second(3, x)
    unpack_own(0, x)
    unpack_own(1, x)
    first(0, 1)
    first(0, 3)
    first(1, 1)
    first(1, 3)
    for d in (1, 3):
        x_copy(2, d).start()
        x_copy(3, d).start()
    unpack_own(2, x)
    unpack_own(3, x)
    for t in (0, 1):
        unpack_own(t, source(1))
        unpack_own(t, source(3))
    first(0, 2)
    first(1, 2)
    x_copy(2, 2).start()
    x_copy(3, 2).start()
    unpack(q1[x], 1, x, q_out, do_out)
    unpack(k1[x], 1, x, k_out, v_out)
    for t in (0, 1):
        unpack_own(t, source(2))
    for d in (1, 3, 2):
        c = source(d)
        for t in (2, 3):
            got_x(t, d)
            second(t, c)
        unpack(q1[c], 1, c, q_out, do_out)
        unpack(k1[c], 1, c, k_out, v_out)
        unpack_own(2, c)
        unpack_own(3, c)
    near_stats(docs, z, q_out, do_out, k_out, v_out, mine)
    for d in (0, 1, 3, 2):
        c = source(d)
        z_got(2, c)
        unpack(q2[c], 2, c, q_out, do_out)
        z_got(3, c)
        unpack(k2[c], 2, c, k_out, v_out)
    late_stats(docs, z, q_out, do_out, k_out, v_out, mine)
    shares = []
    for i, (ref, tiles, to, sent, got) in enumerate((
        (up1, (0, 8), down, low, top),
        (down1, (2, 4), up, top, low),
        (up2, (0, 2), lower, below, above),
        (down2, (4, 2), upper, above, below),
    )):
        part = pl.ds(*tiles)
        shares.append((copy_to(mine.at[part], ref.at[part], s_send.at[i], s_recv.at[i], to), sent, got))
    for copy, sent, got in shares:
        pl.when(sent)(copy.start)
    for copy, sent, got in shares:
        pl.when(got)(copy.wait_recv)
    for qs, values in enumerate(combine_stats(docs, z, mine, up1, up2, down1, down2)):
        for r, value in enumerate(values):
            stat[2 * qs : 2 * qs + 2, r : r + 1, :] = value
    for copy, sent, got in shares:
        pl.when(sent)(copy.wait_send)
    for t in range(4):
        for d in (1, 2, 3):
            x_copy(t, d).wait_send()
    for t in range(4):
        for c in range(XN):
            pl.when((low, top)[t % 2])(z_copy(t, c).wait_send)


def scatter_kernel(len_ref, q_ref, do_ref, k_ref, v_ref, stat, dqt, dk_acc, dv_acc, qp, kp, qhome, khome,
                   kt_ref, ownq, ownk, q1p, k1p, rq2, rk2, rq1, rk1, qs, ks, qfin, kfin,
                   z_send, z_recv, x_send, x_recv):
    z, x, up, down, peer = place()
    docs = Docs(len_ref)
    lk, lq = docs.case(z * 512)
    rk, rq = docs.case(z * 512 + 512)
    low, top = z >= 1, z < ZN - 1
    lm = jnp.logical_not(lk | lq) & low
    rm = jnp.logical_not(rk | rq) & top
    lq, rk = lq & low, rk & top

    def z_start(i, c):
        pl.when((top, low)[i % 2])(lambda: z_copy(i, c).start())

    def z_got(i, c):
        pl.when((low, top)[i % 2])(lambda: z_copy(i, c).wait_recv())

    def z_copy(i, c):
        src, dst, to = ((qp.at[c], rq2.at[c], up), (kp.at[c], rk2.at[c], down),
                        (qs.at[c], rq1.at[c], up), (ks.at[c], rk1.at[c], down))[i]
        return copy_to(src, dst, z_send.at[i, c], z_recv.at[i, c], to)

    def plus(a, b, use):
        return (a.astype(jnp.float32) + jnp.where(use, b.astype(jnp.float32), 0.0)).astype(jnp.bfloat16)

    def dest(d):
        return lax.rem(x + d, XN)

    def x_copy(kind, head, d):
        src, dst = ((qfin, qhome), (kfin, khome))[kind]
        i = 2 * kind + head
        return copy_to(src.at[head, dest(d)], dst.at[head, x], x_send.at[i, d - 1], x_recv.at[i, d - 1], peer[d])

    def send_home(kind, head, d, value):
        src, dst = ((qfin, qhome), (kfin, khome))[kind]
        if d:
            src[head, dest(d)] = value
            x_copy(kind, head, d).start()
        else:
            dst[head, x] = value

    order = (2, 1, 3, 0)
    meet(peer[1:])
    pl.when(low)(lambda: meet([down]))
    pl.when(top)(lambda: meet([up]))
    pl.semaphore_wait(pltpu.get_barrier_semaphore(), 3 + jnp.where(low, 1, 0) + jnp.where(top, 1, 0))
    def second(d):
        z_start(1, dest(d))
        z_start(0, dest(d))

    for d in order:
        z_start(1, dest(d))
    for d in order:
        z_start(0, dest(d))

    def near_grads(head):
        tiles = [tile for tile in near_tiles(docs, z) if (tile[0] >= 6) == bool(head)]
        for ki in (range(4), (6, 7))[1 - head]:
            kt_ref[ki] = tile_rows(k_ref, ki).T
        pairs = [(qi, ki, q0, k0) for qi, q0, keys in tiles for ki, k0 in keys]
        terms = tile_grads(docs, pairs, q_ref, do_ref, k_ref, v_ref, stat, kt_ref)
        for qi in sorted({p[0] for p in pairs}):
            dq = dqt[qi] + sum(t[2] for p, t in zip(pairs, terms) if p[0] == qi)
            pack_query(dq, (ownq.at[0], q1p, None, ownq.at[1])[qi // 2], qi % 2)
        for ki in sorted({p[1] for p in pairs}):
            dk = dk_acc[ki] + sum(t[1] for p, t in zip(pairs, terms) if p[1] == ki)
            dv = dv_acc[ki] + sum(t[0] for p, t in zip(pairs, terms) if p[1] == ki)
            pack_keys(dk, dv, (ownk.at[1], k1p, None, ownk.at[0])[ki // 2], ki % 2)

    def key_home(d):
        c = dest(d)
        z_got(1, c)
        send_home(1, 0, d, plus(ownk[0, c], rk2[c], rk))

    near_grads(0)
    for d in order:
        c = dest(d)
        z_got(0, c)
        qs[c] = plus(q1p[c], rq2[c], lm)
        z_start(2, c)
    key_home(order[0])
    key_home(order[1])
    near_grads(1)
    for n, d in enumerate(order):
        c = dest(d)
        if n >= 2:
            key_home(d)
        ks[c] = plus(k1p[c], rk2[c], rm)
        z_start(3, c)
        send_home(0, 1, d, plus(ownq[1, c], rq2[c], lq))
    for d in order:
        c = dest(d)
        z_got(2, c)
        send_home(0, 0, d, plus(ownq[0, c], rq1[c], low))
    for d in order:
        c = dest(d)
        z_got(3, c)
        send_home(1, 1, d, plus(ownk[1, c], rk1[c], top))
    for i in range(4):
        for d in (1, 2, 3):
            x_copy(i // 2, i % 2, d).wait_recv()
    for i in range(4):
        for c in range(XN):
            pl.when((top, low)[i % 2])(z_copy(i, c).wait_send)
        for d in (1, 2, 3):
            x_copy(i // 2, i % 2, d).wait_send()


def unpack_kernel(qhome, khome, dq_out, dk_out, dv_out):
    for a, out, n in ((0, dq_out, 4), (0, dk_out, 2), (1, dv_out, 2)):
        home = qhome if n == 4 else khome
        step = 128 // n
        for part in range(n):
            lanes = (part if n == 4 else 2 * part + a) * HEAD
            pieces = []
            for xs in range(XN):
                for head in range(2):
                    pieces.append(home[head, xs][:, lanes : lanes + HEAD])
            out[part * step : (part + 1) * step, :] = jnp.concatenate(pieces, axis=1)


VM = pl.BlockSpec(memory_space=pltpu.VMEM)
SM = pl.BlockSpec(memory_space=pltpu.SMEM)
LIMIT = 26 * 1024 * 1024
BIG = pltpu.CompilerParams(vmem_limit_bytes=LIMIT)
HB = pl.BlockSpec(memory_space=pltpu.HBM)
DMA = pltpu.SemaphoreType.DMA


def remote(number, limit=26):
    return pltpu.CompilerParams(vmem_limit_bytes=limit * 1024 * 1024, collective_id=number, has_side_effects=True)


def buf(*shape, dtype=jnp.bfloat16):
    return pltpu.VMEM(shape, dtype)


def out(*shape, dtype=jnp.bfloat16):
    return jax.ShapeDtypeStruct(shape, dtype)


def shards(queries, key_vectors, value_vectors, out_grad, doc_lengths):
    rows, width = queries.shape[1], queries.shape[2]
    chunk = (XN, 64, 4 * HEAD)
    small = (XN, 32, 4 * HEAD)
    block = out(2048, HEAD)
    stat = out(8, 4, TILE, dtype=jnp.float32)
    todo = pltpu.SMEM((4, 64), jnp.int32)
    qs, dos, ks, vs, stats = pl.pallas_call(
        gather_kernel,
        out_shape=(block,) * 4 + (stat,),
        name="gather",
        in_specs=[SM, VM],
        out_specs=(VM,) * 5,
        scratch_shapes=[buf(4, *chunk), buf(4, *chunk)] + [buf(*chunk)] * 6
        + [buf(8, 4, TILE, dtype=jnp.float32)] * 5
        + [DMA((4, 3)), DMA((4, 3)), DMA((4, 4)), DMA((4, 4)), DMA((4,)), DMA((4,))],
        compiler_params=remote(0),
    )(doc_lengths, jnp.concatenate([queries, out_grad, key_vectors, value_vectors]))
    acc = out(8, TILE, HEAD, dtype=jnp.float32)
    qp, kp, *partial = pl.pallas_call(
        grads_kernel,
        name="grads",
        out_shape=(out(*small), out(*chunk), out(8, HEAD, TILE, dtype=jnp.float32), acc, acc),
        in_specs=[SM] + [VM] * 5,
        out_specs=(VM,) * 5,
        scratch_shapes=[todo, buf(8, HEAD, TILE)],
        compiler_params=BIG,
    )(doc_lengths, qs, dos, ks, vs, stats)
    home = pl.pallas_call(
        scatter_kernel,
        name="scatter",
        out_shape=(out(2, *small), out(2, *chunk)),
        in_specs=[SM] + [VM] * 10,
        out_specs=(VM,) * 2,
        scratch_shapes=[buf(8, HEAD, TILE), buf(2, *small), buf(2, *chunk), buf(*small), buf(*chunk),
                        buf(*small), buf(*chunk), buf(*small), buf(*chunk), buf(*small), buf(*chunk),
                        buf(2, *small), buf(2, *chunk),
                        DMA((4, 4)), DMA((4, 4)), DMA((4, 3)), DMA((4, 3))],
        compiler_params=remote(2),
    )(doc_lengths, qs, dos, ks, vs, stats, *partial, qp, kp)
    full = out(rows, width)
    grads = pl.pallas_call(
        unpack_kernel,
        name="unpack",
        out_shape=(full,) * 3,
        in_specs=[VM, VM],
        out_specs=(VM,) * 3,
        compiler_params=BIG,
    )(*home)
    return tuple(g[None] for g in grads)


def solution(mesh):
    spec = P("section", "seq", "dp")
    return jax.shard_map(
        shards,
        mesh=mesh,
        in_specs=(spec, spec, spec, spec, P()),
        out_specs=(spec, spec, spec),
        check_vma=False,
    )
```

```python
import functools
import math

import jax
import jax.numpy as jnp
from jax import lax
from jax.experimental import pallas as pl
from jax.experimental.pallas import tpu as pltpu
from jax.sharding import PartitionSpec as P

HEAD = 224
ZN, XN = 8, 4
SCALE = HEAD ** (-0.5)
NEG = -1e30
LOG2E = math.log2(math.e)
LOW = -1e20
TILE = 256
GROUP = 4
ITEMS = ((0, 3), (1, 3), (2, 3), (0, 2), (1, 2), (2, 2), (3, 0), (3, 1), (3, 2), (2, 0), (2, 1))

LATE = tuple(item for item in ITEMS if 2 in item)


class Docs:
    def __init__(self, lengths):
        self.bounds = []
        total = jnp.int32(0)
        for d in range(8):
            total = total + lengths[d]
            self.bounds.append(total)

    def start(self, t):
        r = jnp.int32(0)
        for b in self.bounds[:7]:
            r = jnp.where(b <= t, b, r)
        return r

    def end(self, t):
        r = jnp.int32(4096)
        for b in reversed(self.bounds):
            r = jnp.where(b > t, b, r)
        return r

    def row_start(self, pos):
        r = jnp.zeros_like(pos)
        for b in self.bounds[:7]:
            r = jnp.where(pos >= b, b, r)
        return r

    def case(self, t):
        before = t - self.start(t - 1)
        after = self.end(t - 1) - t
        keys = after > 1024
        return keys, (before > 1024) & jnp.logical_not(keys)


def slots(docs, z):
    lk, lq = docs.case(z * 512)
    rk, rq = docs.case(z * 512 + 512)
    lm = jnp.logical_not(lk | lq)
    rm = jnp.logical_not(rk | rq)
    q_ids = (z, z + 1, jnp.where(rq, z + 1, z + 2), z)
    k_ids = (z, z - 1, jnp.where(lk, z - 1, z - 2), z)
    valid = {
        (0, 3): True,
        (1, 3): jnp.logical_not(rk),
        (2, 3): rm,
        (0, 2): lk,
        (1, 2): lk & jnp.logical_not(rk),
        (2, 2): (lk & rm) | (rq & lm),
        (3, 0): True,
        (3, 1): jnp.logical_not(lq),
        (3, 2): lm,
        (2, 0): rq,
        (2, 1): rq & jnp.logical_not(lq),
    }
    return q_ids, k_ids, valid


NT = (((1,), (1,)), ((), ()))


def list_tiles(docs, z, todo, items):
    q_ids, k_ids, valid = slots(docs, z)
    firsts = [[docs.start(q_ids[qs] * 512 + qt * TILE) for qt in range(2)] for qs in range(4)]
    count = jnp.int32(0)
    for qs, ks in items:
        qid, kid, ok = q_ids[qs], k_ids[ks], valid[(qs, ks)]
        use = (qid < ZN) & (kid >= 0) & ok
        for qt in range(2):
            q0 = qid * 512 + qt * TILE
            for kt in range(2):
                k0 = kid * 512 + kt * TILE
                k1 = k0 + TILE - 1
                hit = use & (k0 <= q0 + TILE - 1) & ((k1 >= q0) | (k1 >= firsts[qs][qt]))
                todo[0, count] = 2 * qs + qt
                todo[1, count] = 2 * ks + kt
                todo[2, count] = q0
                todo[3, count] = k0
                count = count + jnp.where(hit, 1, 0)
    for i in range(GROUP - 1):
        todo[0, count + i] = 0
        todo[1, count + i] = 0
        todo[2, count + i] = 0
        todo[3, count + i] = -(1 << 20)
    return count


def for_groups(count, todo, body):
    @pl.loop(0, (count + GROUP - 1) // GROUP)
    def _(g):
        body([tuple(todo[j, g * GROUP + i] for j in range(4)) for i in range(GROUP)])


def tile_rows(ref, i):
    return ref[pl.ds(pl.multiple_of(i * TILE, TILE), TILE), :]


def raw_scores(k, q):
    return lax.dot_general(k, q, NT, preferred_element_type=jnp.float32)


def masked(docs, s, q0, k0, near=False):
    row = lax.broadcasted_iota(jnp.int32, (TILE, TILE), 0)
    qpos = q0 + lax.broadcasted_iota(jnp.int32, (1, TILE), 1)
    allowed = row >= docs.row_start(qpos) - k0
    if q0 is k0:
        allowed = allowed & (row <= lax.broadcasted_iota(jnp.int32, (1, TILE), 1))
    elif near:
        allowed = allowed & (row <= qpos - k0)
    return jnp.where(allowed, s * (SCALE * LOG2E), NEG)


FAR = -(1 << 20)


def diagonal_tiles(z):
    a, b = z * 512, z * 512 + TILE
    return [
        (0, a, [(6, a)]),
        (1, b, [(6, a), (7, b)]),
        (6, a, [(0, a)]),
        (7, b, [(0, a), (1, b)]),
    ]


def near_tiles(docs, z):
    _, lq = docs.case(z * 512)
    rk, _ = docs.case(z * 512 + 512)
    a, b = z * 512, z * 512 + TILE
    fore = jnp.where(jnp.logical_not(rk) & (z < ZN - 1), a, FAR)
    back = jnp.where(jnp.logical_not(lq) & (z > 0), a - 512, FAR)
    tiles = diagonal_tiles(z)
    for i in (2, 3):
        tiles[i][2].extend([(2, back), (3, back + TILE)])
    for i in range(2):
        tiles.append((2 + i, a + 512 + i * TILE, [(6, fore), (7, fore + TILE)]))
    return tiles


def part_stats(docs, q, do, q0, keys, near=False):
    raw = [(masked(docs, raw_scores(k, q), q0, k0, near), raw_scores(v, do)) for k, v, k0 in keys]
    m = jnp.full((1, TILE), LOW, jnp.float32)
    for s, dp in raw:
        m = jnp.maximum(m, jnp.max(s, axis=0, keepdims=True))
    l = jnp.zeros((1, TILE), jnp.float32)
    d = jnp.zeros((1, TILE), jnp.float32)
    for s, dp in raw:
        p = jnp.exp2(s - m)
        l = l + jnp.sum(p, axis=0, keepdims=True)
        d = d + jnp.sum(p * dp, axis=0, keepdims=True)
    return m, l, d


def put_stats(st_ref, qi, values):
    for r, value in enumerate(values):
        st_ref[qi, r : r + 1, :] = value


def add_stats(st_ref, qi, part, use):
    old = [st_ref[qi, r : r + 1, :] for r in range(3)]
    m = jnp.maximum(old[0], jnp.where(use, part[0], LOW))
    a, b = jnp.exp2(old[0] - m), jnp.where(use, jnp.exp2(part[0] - m), 0.0)
    put_stats(st_ref, qi, (m, old[1] * a + part[1] * b, old[2] * a + part[2] * b))


def near_half(docs, z, h, q_ref, do_ref, k_ref, v_ref, st_ref):
    _, lq = docs.case(z * 512)
    rk, _ = docs.case(z * 512 + 512)
    here = z * 512
    fore = jnp.where(jnp.logical_not(rk) & (z < ZN - 1), here, FAR)
    back = jnp.where(jnp.logical_not(lq) & (z > 0), here - 512, FAR)
    k, v = tile_rows(k_ref, 6 + h), tile_rows(v_ref, 6 + h)
    for i in range(4):
        first = (here, fore)[i // 2] + h * TILE
        part = part_stats(docs, tile_rows(q_ref, i), tile_rows(do_ref, i), here + i * TILE, [(k, v, first)], i < 2)
        add_stats(st_ref, i, part, True)
    keys = [(tile_rows(k_ref, j), tile_rows(v_ref, j), (here, back)[j // 2] + j % 2 * TILE) for j in range(4)]
    put_stats(st_ref, 6 + h, part_stats(docs, tile_rows(q_ref, 6 + h), tile_rows(do_ref, 6 + h), here + h * TILE, keys, True))


def late_half(docs, z, h, other, q_ref, do_ref, k_ref, v_ref, st_ref):
    lk, lq = docs.case(z * 512)
    rk, rq = docs.case(z * 512 + 512)
    lm, rm = jnp.logical_not(lk | lq), jnp.logical_not(rk | rq)
    q_ids, k_ids, _ = slots(docs, z)
    here, q2, k2 = z * 512, q_ids[2] * 512, k_ids[2] * 512
    q_ok, k_ok = q_ids[2] < ZN, k_ids[2] >= 0

    def start(use, pos, j):
        return jnp.where(use, pos, FAR) + j * TILE

    def pick(ref, use, one, other):
        return jnp.where(use, tile_rows(ref, one), tile_rows(ref, other))

    own = jnp.logical_not(rk) & q_ok
    both = ((lk & rm) | (rq & lm)) & q_ok & k_ok
    cross = (lk & jnp.logical_not(rk) & (z < ZN - 1) & k_ok) | (rq & jnp.logical_not(lq) & (z > 0) & q_ok)
    halves = [h] if other is None else [h, other]
    keys = [(pick(k_ref, rq, j, 6 + j), pick(v_ref, rq, j, 6 + j), start(own, here, j)) for j in range(2)]
    keys += [(tile_rows(k_ref, 4 + j), tile_rows(v_ref, 4 + j), start(both, k2, j)) for j in halves]
    put_stats(st_ref, 4 + h, part_stats(docs, tile_rows(q_ref, 4 + h), tile_rows(do_ref, 4 + h), q2 + h * TILE, keys))
    if other is not None:
        keys = [(tile_rows(k_ref, 4 + h), tile_rows(v_ref, 4 + h), start(both, k2, h))]
        part = part_stats(docs, tile_rows(q_ref, 4 + other), tile_rows(do_ref, 4 + other), q2 + other * TILE, keys)
        add_stats(st_ref, 4 + other, part, True)
    second = (tile_rows(k_ref, 4 + h), tile_rows(v_ref, 4 + h), start(jnp.logical_not(lq) & k_ok, k2, h))
    for i in range(2):
        part = part_stats(docs, pick(q_ref, lk, i, 6 + i), pick(do_ref, lk, i, 6 + i), here + i * TILE, [second])
        add_stats(st_ref, i, part, lk)
        add_stats(st_ref, 6 + i, part, lm)
    for i in range(2):
        key = (pick(k_ref, lk, 4 + h, 2 + i), pick(v_ref, lk, 4 + h, 2 + i),
               jnp.where(lk, start(cross, k2, h), start(cross, here - 512, i)))
        part = part_stats(docs, pick(q_ref, lk, 2 + i, 4 + h), pick(do_ref, lk, 2 + i, 4 + h),
                          jnp.where(lk, here + 512 + i * TILE, q2 + h * TILE), [key])
        add_stats(st_ref, 2 + i, part, lk)
        add_stats(st_ref, 4 + h, part, jnp.logical_not(lk))


def combine_stats(docs, z, mine, up1, up2, down1, down2):
    lk, lq = docs.case(z * 512)
    rk, rq = docs.case(z * 512 + 512)
    lm = jnp.logical_not(lk | lq)
    rm = jnp.logical_not(rk | rq)
    bk, bq = docs.case(z * 512 - 512)
    bm = jnp.logical_not(bk | bq) & (z >= 2)

    def part(ref, slot, use=None):
        m, l, d = (ref[2 * slot : 2 * slot + 2, r : r + 1, :] for r in range(3))
        if use is not None:
            m = jnp.where(use, m, LOW)
            l = jnp.where(use, l, 0.0)
            d = jnp.where(use, d, 0.0)
        return m, l, d

    groups = (
        (part(mine, 0), part(down1, 1, z >= 1), part(down2, 2, bm)),
        (part(mine, 1), part(up1, 0, z + 1 < ZN), part(down1, 2, lm & (z >= 1))),
        (part(mine, 2), part(up2, 0, rm & (z + 2 < ZN)), part(up1, 1, rm & (z + 1 < ZN)), part(up1, 3, rq & (z + 1 < ZN))),
        (part(mine, 3), part(down1, 2, lq & (z >= 1))),
    )
    out = []
    for parts in groups:
        m = functools.reduce(jnp.maximum, [p[0] for p in parts])
        l = sum(p[1] * jnp.exp2(p[0] - m) for p in parts)
        d = sum(p[2] * jnp.exp2(p[0] - m) for p in parts)
        some = l > 0.0
        l = jnp.where(some, l, 1.0)
        out.append((jnp.where(some, m + jnp.log2(l), -NEG), d / l))
    return out


def tile_grads(docs, tiles, q_ref, do_ref, k_ref, v_ref, stat, kt_ref):
    raw = []
    for qi, ki, q0, k0 in tiles:
        s = raw_scores(tile_rows(k_ref, ki), tile_rows(q_ref, qi))
        raw.append((s, raw_scores(tile_rows(v_ref, ki), tile_rows(do_ref, qi))))
    weights = []
    for (qi, ki, q0, k0), (s, dp) in zip(tiles, raw):
        p = jnp.exp2(masked(docs, s, q0, k0) - stat[qi, 0:1, :])
        weights.append((p.astype(jnp.bfloat16), (p * (dp - stat[qi, 1:2, :])).astype(jnp.bfloat16)))
    terms = []
    for (qi, ki, q0, k0), (p, ds) in zip(tiles, weights):
        terms.append((
            jnp.dot(p, tile_rows(do_ref, qi), preferred_element_type=jnp.float32),
            jnp.dot(ds, tile_rows(q_ref, qi), preferred_element_type=jnp.float32),
            jnp.dot(kt_ref[ki], ds, preferred_element_type=jnp.float32),
        ))
    return terms


def pack_pair(first, second):
    return jnp.concatenate([first[:64], second[:64], first[64:], second[64:]], axis=1)


def pack_query(dqt, q_out, half):
    dq = (dqt * SCALE).T.astype(jnp.bfloat16)
    for i in range(2):
        r = i * 128
        q_out[2 * half + i] = jnp.concatenate([dq[r + 32 * j : r + 32 * j + 32] for j in range(4)], axis=1)


def pack_keys(dk, dv, k_out, half):
    dk = (dk * SCALE).astype(jnp.bfloat16)
    dv = dv.astype(jnp.bfloat16)
    for i in range(2):
        r = i * 128
        k_out[2 * half + i] = pack_pair(dk[r : r + 128], dv[r : r + 128])


def grads_kernel(len_ref, q_ref, do_ref, k_ref, v_ref, stat, qp_ref, kp_ref, dqt, dk_acc, dv_acc, todo, kt_ref):
    z = lax.axis_index("seq") // XN
    docs = Docs(len_ref)
    for i in range(8):
        kt_ref[i] = k_ref[i * TILE : (i + 1) * TILE, :].T
    dqt[...] = jnp.zeros_like(dqt)
    dk_acc[...] = jnp.zeros_like(dk_acc)
    dv_acc[...] = jnp.zeros_like(dv_acc)

    def body(tiles):
        for (qi, ki, q0, k0), (dv, dk, dq) in zip(tiles, tile_grads(docs, tiles, q_ref, do_ref, k_ref, v_ref, stat, kt_ref)):
            dv_acc[ki] += dv
            dk_acc[ki] += dk
            dqt[qi] += dq

    for_groups(list_tiles(docs, z, todo, LATE), todo, body)
    for half in range(2):
        pack_query(dqt[4 + half], qp_ref, half)
        pack_keys(dk_acc[4 + half], dv_acc[4 + half], kp_ref, half)


def copy_to(src, dst, send, recv, device):
    return pltpu.make_async_remote_copy(
        src_ref=src,
        dst_ref=dst,
        send_sem=send,
        recv_sem=recv,
        device_id={"seq": device},
        device_id_type=pl.DeviceIdType.MESH,
    )


def meet(devices):
    for device in devices:
        pl.semaphore_signal(
            pltpu.get_barrier_semaphore(), inc=1, device_id={"seq": device}, device_id_type=pl.DeviceIdType.MESH
        )


def greet(devices):
    meet(devices)
    pl.semaphore_wait(pltpu.get_barrier_semaphore(), len(devices))


def window(ref, off):
    low = off // 128 * 128
    high = -(-(off + HEAD) // 128) * 128
    return ref[:, low:high][:, off - low : off - low + HEAD]


def place():
    me = lax.axis_index("seq")
    z, x = me // XN, me % XN
    up = lax.rem(z + 1, ZN) * XN + x
    down = lax.rem(z + ZN - 1, ZN) * XN + x
    peer = [z * XN + lax.rem(x + d, XN) for d in range(XN)]
    return z, x, up, down, peer


TYPES = (("q", 0), ("k", 1), ("q", 1), ("k", 0))


def gather_kernel(len_ref, raw, q_out, do_out, k_out, v_out, stat,
                  packed, own, q1, k1, qsel, ksel, q2, k2, mine, up1, up2, down1, down2,
                  x_send, x_recv, z_send, z_recv, s_send, s_recv):
    z, x, up, down, peer = place()
    low, top = z > 0, z < ZN - 1
    below, above = z > 1, z < ZN - 2
    upper = lax.rem(z + 2, ZN) * XN + x
    lower = lax.rem(z + ZN - 2, ZN) * XN + x
    meet(peer[1:])
    expected = jnp.int32(3)
    for use, to in ((low, down), (top, up), (below, lower), (above, upper)):
        pl.when(use)(functools.partial(meet, [to]))
        expected = expected + jnp.where(use, 1, 0)

    @pl.when(jnp.logical_not(top))
    def _():
        q1[...] = jnp.zeros_like(q1)
        q2[...] = jnp.zeros_like(q2)

    @pl.when(jnp.logical_not(low))
    def _():
        k1[...] = jnp.zeros_like(k1)
        k2[...] = jnp.zeros_like(k2)

    docs = Docs(len_ref)
    lk, lq = docs.case(z * 512)
    rk, rq = docs.case(z * 512 + 512)

    def pack(t, xp):
        kind, head = TYPES[t]
        i = 0 if kind == "q" else 2
        off = (2 * xp + head) * HEAD
        packed[t, xp] = pack_pair(window(raw.at[i], off), window(raw.at[i + 1], off))

    def x_copy(t, d):
        to = lax.rem(x + d, XN)
        return copy_to(packed.at[t, to], own.at[t, x], x_send.at[t, d - 1], x_recv.at[t, d - 1], peer[d])

    def z_copy(i, c):
        src, dst, to = ((own.at[0, c], q1.at[c], down), (own.at[1, c], k1.at[c], up),
                        (qsel.at[c], q2.at[c], down), (ksel.at[c], k2.at[c], up))[i]
        return copy_to(src, dst, z_send.at[i, c], z_recv.at[i, c], to)

    def z_start(i, c):
        pl.when((low, top)[i % 2])(lambda: z_copy(i, c).start())

    def z_got(i, c):
        pl.when((top, low)[i % 2])(lambda: z_copy(i, c).wait_recv())

    def unpack(value, slot, c, first, second):
        row = slot * 512 + c * 128
        upper = pl.ds(pl.multiple_of(row, 64), 64)
        lower = pl.ds(pl.multiple_of(row + 64, 64), 64)
        first[upper, :] = value[:, 0:HEAD]
        second[upper, :] = value[:, HEAD : 2 * HEAD]
        first[lower, :] = value[:, 2 * HEAD : 3 * HEAD]
        second[lower, :] = value[:, 3 * HEAD : 4 * HEAD]

    def source(d):
        return lax.rem(x + d, XN)

    def got_x(t, d):
        back = XN - d
        copy_to(packed.at[t, x], own.at[t, source(d)], x_send.at[t, back - 1], x_recv.at[t, back - 1], peer[1]).wait_recv()

    def second(i, c):
        z_got(i - 2, c)
        if i == 2:
            qsel[c] = jnp.where(lq, own[2, c], q1[c])
        else:
            ksel[c] = jnp.where(rk, own[3, c], k1[c])
        z_start(i, c)

    def first(t, d):
        got_x(t, d)
        z_start(t, source(d))

    def unpack_own(t, c):
        unpack(own[t, c], *((0, c, q_out, do_out), (0, c, k_out, v_out), (3, c, q_out, do_out), (3, c, k_out, v_out))[t])

    for xp in range(XN):
        pack(0, xp)
    own[0, x] = packed[0, x]
    pl.semaphore_wait(pltpu.get_barrier_semaphore(), expected)
    for d in (1, 3):
        x_copy(0, d).start()
    z_start(0, x)
    for xp in range(XN):
        pack(1, xp)
    own[1, x] = packed[1, x]
    for d in (1, 3):
        x_copy(1, d).start()
    z_start(1, x)
    for t in (0, 1):
        x_copy(t, 2).start()
    for t in (2, 3):
        for xp in range(XN):
            pack(t, xp)
        own[t, x] = packed[t, x]
    second(2, x)
    second(3, x)
    unpack_own(0, x)
    unpack_own(1, x)
    first(0, 1)
    first(0, 3)
    first(1, 1)
    first(1, 3)
    for d in (1, 3):
        x_copy(2, d).start()
        x_copy(3, d).start()
    unpack_own(2, x)
    unpack_own(3, x)
    for t in (0, 1):
        unpack_own(t, source(1))
        unpack_own(t, source(3))
    first(0, 2)
    first(1, 2)
    unpack(q1[x], 1, x, q_out, do_out)
    unpack(k1[x], 1, x, k_out, v_out)
    for t in (0, 1):
        unpack_own(t, source(2))
    def pass_on(i, c):
        if i == 2:
            qsel[c] = jnp.where(lq, own[2, c], q1[c])
        else:
            ksel[c] = jnp.where(rk, own[3, c], k1[c])
        z_start(i, c)

    def unpack_first(c):
        unpack(q1[c], 1, c, q_out, do_out)
        unpack(k1[c], 1, c, k_out, v_out)

    def unpack_second(c):
        z_got(2, c)
        unpack(q2[c], 2, c, q_out, do_out)
        z_got(3, c)
        unpack(k2[c], 2, c, k_out, v_out)

    for i in (0, 1, 2, 3):
        put_stats(mine, i, (jnp.full((1, TILE), LOW, jnp.float32),) + (jnp.zeros((1, TILE), jnp.float32),) * 2)
    arrays = (q_out, do_out, k_out, v_out, mine)
    half = x // 2
    step = 1 + 2 * lax.rem(x, 2)
    steps = (step, XN - step, 2)
    mate = source(step)
    for t in (2, 3):
        got_x(t, step)
        z_got(t - 2, mate)
        pass_on(t, mate)
        x_copy(t, 2).start()
        unpack_own(t, mate)
    unpack_first(mate)
    for d in steps[1:]:
        z_got(0, source(d))
        z_got(1, source(d))
        unpack_first(source(d))
    near_half(docs, z, half, *arrays)
    for d in steps[1:]:
        for t in (2, 3):
            got_x(t, d)
            pass_on(t, source(d))
            unpack_own(t, source(d))
    near_half(docs, z, 1 - half, *arrays)
    unpack_second(x)
    unpack_second(mate)
    late_half(docs, z, half, None, *arrays)
    for d in steps[1:]:
        unpack_second(source(d))
    late_half(docs, z, 1 - half, half, *arrays)
    shares = []
    for i, (ref, tiles, to, sent, got) in enumerate((
        (up1, (0, 8), down, low, top),
        (down1, (2, 4), up, top, low),
        (up2, (0, 2), lower, below, above),
        (down2, (4, 2), upper, above, below),
    )):
        part = pl.ds(*tiles)
        shares.append((copy_to(mine.at[part], ref.at[part], s_send.at[i], s_recv.at[i], to), sent, got))
    for copy, sent, got in shares:
        pl.when(sent)(copy.start)
    for copy, sent, got in shares:
        pl.when(got)(copy.wait_recv)
    for qs, values in enumerate(combine_stats(docs, z, mine, up1, up2, down1, down2)):
        for r, value in enumerate(values):
            stat[2 * qs : 2 * qs + 2, r : r + 1, :] = value
    for copy, sent, got in shares:
        pl.when(sent)(copy.wait_send)
    for t in range(4):
        for d in (1, 2, 3):
            x_copy(t, d).wait_send()
    for t in range(4):
        for c in range(XN):
            pl.when((low, top)[t % 2])(z_copy(t, c).wait_send)


def scatter_kernel(len_ref, q_ref, do_ref, k_ref, v_ref, stat, dqt, dk_acc, dv_acc, qp, kp, qhome, khome,
                   kt_ref, ownq, ownk, q1p, k1p, rq2, rk2, rq1, rk1, qs, ks, qfin, kfin,
                   z_send, z_recv, x_send, x_recv):
    z, x, up, down, peer = place()
    docs = Docs(len_ref)
    lk, lq = docs.case(z * 512)
    rk, rq = docs.case(z * 512 + 512)
    low, top = z >= 1, z < ZN - 1
    lm = jnp.logical_not(lk | lq) & low
    rm = jnp.logical_not(rk | rq) & top
    lq, rk = lq & low, rk & top

    def z_start(i, c):
        pl.when((top, low)[i % 2])(lambda: z_copy(i, c).start())

    def z_got(i, c):
        pl.when((low, top)[i % 2])(lambda: z_copy(i, c).wait_recv())

    def z_copy(i, c):
        src, dst, to = ((qp.at[c], rq2.at[c], up), (kp.at[c], rk2.at[c], down),
                        (qs.at[c], rq1.at[c], up), (ks.at[c], rk1.at[c], down))[i]
        return copy_to(src, dst, z_send.at[i, c], z_recv.at[i, c], to)

    def plus(a, b, use):
        return (a.astype(jnp.float32) + jnp.where(use, b.astype(jnp.float32), 0.0)).astype(jnp.bfloat16)

    def dest(d):
        return lax.rem(x + d, XN)

    def x_copy(kind, head, d):
        src, dst = ((qfin, qhome), (kfin, khome))[kind]
        i = 2 * kind + head
        return copy_to(src.at[head, dest(d)], dst.at[head, x], x_send.at[i, d - 1], x_recv.at[i, d - 1], peer[d])

    def send_home(kind, head, d, value):
        src, dst = ((qfin, qhome), (kfin, khome))[kind]
        if d:
            src[head, dest(d)] = value
            x_copy(kind, head, d).start()
        else:
            dst[head, x] = value

    order = (2, 1, 3, 0)
    meet(peer[1:])
    pl.when(low)(lambda: meet([down]))
    pl.when(top)(lambda: meet([up]))
    pl.semaphore_wait(pltpu.get_barrier_semaphore(), 3 + jnp.where(low, 1, 0) + jnp.where(top, 1, 0))
    def second(d):
        z_start(1, dest(d))
        z_start(0, dest(d))

    for d in order:
        z_start(1, dest(d))
    for d in order:
        z_start(0, dest(d))

    def near_grads(head):
        tiles = [tile for tile in near_tiles(docs, z) if (tile[0] >= 6) == bool(head)]
        for ki in (range(4), (6, 7))[1 - head]:
            kt_ref[ki] = tile_rows(k_ref, ki).T
        pairs = [(qi, ki, q0, k0) for qi, q0, keys in tiles for ki, k0 in keys]
        terms = tile_grads(docs, pairs, q_ref, do_ref, k_ref, v_ref, stat, kt_ref)
        for qi in sorted({p[0] for p in pairs}):
            dq = dqt[qi] + sum(t[2] for p, t in zip(pairs, terms) if p[0] == qi)
            pack_query(dq, (ownq.at[0], q1p, None, ownq.at[1])[qi // 2], qi % 2)
        for ki in sorted({p[1] for p in pairs}):
            dk = dk_acc[ki] + sum(t[1] for p, t in zip(pairs, terms) if p[1] == ki)
            dv = dv_acc[ki] + sum(t[0] for p, t in zip(pairs, terms) if p[1] == ki)
            pack_keys(dk, dv, (ownk.at[1], k1p, None, ownk.at[0])[ki // 2], ki % 2)

    def key_home(d):
        c = dest(d)
        z_got(1, c)
        send_home(1, 0, d, plus(ownk[0, c], rk2[c], rk))

    near_grads(0)
    for d in order:
        c = dest(d)
        z_got(0, c)
        qs[c] = plus(q1p[c], rq2[c], lm)
        z_start(2, c)
    key_home(order[0])
    key_home(order[1])
    near_grads(1)
    for n, d in enumerate(order):
        c = dest(d)
        if n >= 2:
            key_home(d)
        ks[c] = plus(k1p[c], rk2[c], rm)
        z_start(3, c)
        send_home(0, 1, d, plus(ownq[1, c], rq2[c], lq))
    for d in order:
        c = dest(d)
        z_got(2, c)
        send_home(0, 0, d, plus(ownq[0, c], rq1[c], low))
    for d in order:
        c = dest(d)
        z_got(3, c)
        send_home(1, 1, d, plus(ownk[1, c], rk1[c], top))
    for i in range(4):
        for d in (1, 2, 3):
            x_copy(i // 2, i % 2, d).wait_recv()
    for i in range(4):
        for c in range(XN):
            pl.when((top, low)[i % 2])(z_copy(i, c).wait_send)
        for d in (1, 2, 3):
            x_copy(i // 2, i % 2, d).wait_send()


def unpack_kernel(qhome, khome, dq_out, dk_out, dv_out):
    for a, out, n in ((0, dq_out, 4), (0, dk_out, 2), (1, dv_out, 2)):
        home = qhome if n == 4 else khome
        step = 128 // n
        for part in range(n):
            lanes = (part if n == 4 else 2 * part + a) * HEAD
            pieces = []
            for xs in range(XN):
                for head in range(2):
                    pieces.append(home[head, xs][:, lanes : lanes + HEAD])
            out[part * step : (part + 1) * step, :] = jnp.concatenate(pieces, axis=1)


VM = pl.BlockSpec(memory_space=pltpu.VMEM)
SM = pl.BlockSpec(memory_space=pltpu.SMEM)
LIMIT = 26 * 1024 * 1024
BIG = pltpu.CompilerParams(vmem_limit_bytes=LIMIT)
HB = pl.BlockSpec(memory_space=pltpu.HBM)
DMA = pltpu.SemaphoreType.DMA


def remote(number, limit=26):
    return pltpu.CompilerParams(vmem_limit_bytes=limit * 1024 * 1024, collective_id=number, has_side_effects=True)


def buf(*shape, dtype=jnp.bfloat16):
    return pltpu.VMEM(shape, dtype)


def out(*shape, dtype=jnp.bfloat16):
    return jax.ShapeDtypeStruct(shape, dtype)


def shards(queries, key_vectors, value_vectors, out_grad, doc_lengths):
    rows, width = queries.shape[1], queries.shape[2]
    chunk = (XN, 64, 4 * HEAD)
    small = (XN, 32, 4 * HEAD)
    block = out(2048, HEAD)
    stat = out(8, 4, TILE, dtype=jnp.float32)
    todo = pltpu.SMEM((4, 64), jnp.int32)
    qs, dos, ks, vs, stats = pl.pallas_call(
        gather_kernel,
        out_shape=(block,) * 4 + (stat,),
        name="gather",
        in_specs=[SM, VM],
        out_specs=(VM,) * 5,
        scratch_shapes=[buf(4, *chunk), buf(4, *chunk)] + [buf(*chunk)] * 6
        + [buf(8, 4, TILE, dtype=jnp.float32)] * 5
        + [DMA((4, 3)), DMA((4, 3)), DMA((4, 4)), DMA((4, 4)), DMA((4,)), DMA((4,))],
        compiler_params=remote(0),
    )(doc_lengths, jnp.concatenate([queries, out_grad, key_vectors, value_vectors]))
    acc = out(8, TILE, HEAD, dtype=jnp.float32)
    qp, kp, *partial = pl.pallas_call(
        grads_kernel,
        name="grads",
        out_shape=(out(*small), out(*chunk), out(8, HEAD, TILE, dtype=jnp.float32), acc, acc),
        in_specs=[SM] + [VM] * 5,
        out_specs=(VM,) * 5,
        scratch_shapes=[todo, buf(8, HEAD, TILE)],
        compiler_params=BIG,
    )(doc_lengths, qs, dos, ks, vs, stats)
    home = pl.pallas_call(
        scatter_kernel,
        name="scatter",
        out_shape=(out(2, *small), out(2, *chunk)),
        in_specs=[SM] + [VM] * 10,
        out_specs=(VM,) * 2,
        scratch_shapes=[buf(8, HEAD, TILE), buf(2, *small), buf(2, *chunk), buf(*small), buf(*chunk),
                        buf(*small), buf(*chunk), buf(*small), buf(*chunk), buf(*small), buf(*chunk),
                        buf(2, *small), buf(2, *chunk),
                        DMA((4, 4)), DMA((4, 4)), DMA((4, 3)), DMA((4, 3))],
        compiler_params=remote(2),
    )(doc_lengths, qs, dos, ks, vs, stats, *partial, qp, kp)
    full = out(rows, width)
    grads = pl.pallas_call(
        unpack_kernel,
        name="unpack",
        out_shape=(full,) * 3,
        in_specs=[VM, VM],
        out_specs=(VM,) * 3,
        compiler_params=BIG,
    )(*home)
    return tuple(g[None] for g in grads)


def solution(mesh):
    spec = P("section", "seq", "dp")
    return jax.shard_map(
        shards,
        mesh=mesh,
        in_specs=(spec, spec, spec, spec, P()),
        out_specs=(spec, spec, spec),
        check_vma=False,
    )
```

```python
import functools
import math

import jax
import jax.numpy as jnp
from jax import lax
from jax.experimental import pallas as pl
from jax.experimental.pallas import tpu as pltpu
from jax.sharding import PartitionSpec as P

HEAD = 224
ZN, XN = 8, 4
SCALE = HEAD ** (-0.5)
NEG = -1e30
LOG2E = math.log2(math.e)
LOW = -1e20
TILE = 256
GROUP = 4
ITEMS = ((0, 3), (1, 3), (2, 3), (0, 2), (1, 2), (2, 2), (3, 0), (3, 1), (3, 2), (2, 0), (2, 1))

LATE = tuple(item for item in ITEMS if 2 in item)


class Docs:
    def __init__(self, lengths):
        self.bounds = []
        total = jnp.int32(0)
        for d in range(8):
            total = total + lengths[d]
            self.bounds.append(total)

    def start(self, t):
        r = jnp.int32(0)
        for b in self.bounds[:7]:
            r = jnp.where(b <= t, b, r)
        return r

    def end(self, t):
        r = jnp.int32(4096)
        for b in reversed(self.bounds):
            r = jnp.where(b > t, b, r)
        return r

    def row_start(self, pos):
        r = jnp.zeros_like(pos)
        for b in self.bounds[:7]:
            r = jnp.where(pos >= b, b, r)
        return r

    def case(self, t):
        before = t - self.start(t - 1)
        after = self.end(t - 1) - t
        keys = after > 1024
        return keys, (before > 1024) & jnp.logical_not(keys)


def slots(docs, z):
    lk, lq = docs.case(z * 512)
    rk, rq = docs.case(z * 512 + 512)
    lm = jnp.logical_not(lk | lq)
    rm = jnp.logical_not(rk | rq)
    q_ids = (z, z + 1, jnp.where(rq, z + 1, z + 2), z)
    k_ids = (z, z - 1, jnp.where(lk, z - 1, z - 2), z)
    valid = {
        (0, 3): True,
        (1, 3): jnp.logical_not(rk),
        (2, 3): rm,
        (0, 2): lk,
        (1, 2): lk & jnp.logical_not(rk),
        (2, 2): (lk & rm) | (rq & lm),
        (3, 0): True,
        (3, 1): jnp.logical_not(lq),
        (3, 2): lm,
        (2, 0): rq,
        (2, 1): rq & jnp.logical_not(lq),
    }
    return q_ids, k_ids, valid


NT = (((1,), (1,)), ((), ()))


def list_tiles(docs, z, todo, items):
    q_ids, k_ids, valid = slots(docs, z)
    firsts = [[docs.start(q_ids[qs] * 512 + qt * TILE) for qt in range(2)] for qs in range(4)]
    count = jnp.int32(0)
    for qs, ks in items:
        qid, kid, ok = q_ids[qs], k_ids[ks], valid[(qs, ks)]
        use = (qid < ZN) & (kid >= 0) & ok
        for qt in range(2):
            q0 = qid * 512 + qt * TILE
            for kt in range(2):
                k0 = kid * 512 + kt * TILE
                k1 = k0 + TILE - 1
                hit = use & (k0 <= q0 + TILE - 1) & ((k1 >= q0) | (k1 >= firsts[qs][qt]))
                todo[0, count] = 2 * qs + qt
                todo[1, count] = 2 * ks + kt
                todo[2, count] = q0
                todo[3, count] = k0
                count = count + jnp.where(hit, 1, 0)
    for i in range(GROUP - 1):
        todo[0, count + i] = 0
        todo[1, count + i] = 0
        todo[2, count + i] = 0
        todo[3, count + i] = -(1 << 20)
    return count


def for_groups(count, todo, body):
    @pl.loop(0, (count + GROUP - 1) // GROUP)
    def _(g):
        body([tuple(todo[j, g * GROUP + i] for j in range(4)) for i in range(GROUP)])


def tile_rows(ref, i):
    return ref[pl.ds(pl.multiple_of(i * TILE, TILE), TILE), :]


def raw_scores(k, q):
    return lax.dot_general(k, q, NT, preferred_element_type=jnp.float32)


def masked(docs, s, q0, k0, near=False):
    row = lax.broadcasted_iota(jnp.int32, (TILE, TILE), 0)
    qpos = q0 + lax.broadcasted_iota(jnp.int32, (1, TILE), 1)
    allowed = row >= docs.row_start(qpos) - k0
    if q0 is k0:
        allowed = allowed & (row <= lax.broadcasted_iota(jnp.int32, (1, TILE), 1))
    elif near:
        allowed = allowed & (row <= qpos - k0)
    return jnp.where(allowed, s * (SCALE * LOG2E), NEG)


FAR = -(1 << 20)


def diagonal_tiles(z):
    a, b = z * 512, z * 512 + TILE
    return [
        (0, a, [(6, a)]),
        (1, b, [(6, a), (7, b)]),
        (6, a, [(0, a)]),
        (7, b, [(0, a), (1, b)]),
    ]


def near_tiles(docs, z):
    _, lq = docs.case(z * 512)
    rk, _ = docs.case(z * 512 + 512)
    a, b = z * 512, z * 512 + TILE
    fore = jnp.where(jnp.logical_not(rk) & (z < ZN - 1), a, FAR)
    back = jnp.where(jnp.logical_not(lq) & (z > 0), a - 512, FAR)
    tiles = diagonal_tiles(z)
    for i in (2, 3):
        tiles[i][2].extend([(2, back), (3, back + TILE)])
    for i in range(2):
        tiles.append((2 + i, a + 512 + i * TILE, [(6, fore), (7, fore + TILE)]))
    return tiles


def part_stats(docs, q, do, q0, keys, near=False):
    raw = [(masked(docs, raw_scores(k, q), q0, k0, near), raw_scores(v, do)) for k, v, k0 in keys]
    m = jnp.full((1, TILE), LOW, jnp.float32)
    for s, dp in raw:
        m = jnp.maximum(m, jnp.max(s, axis=0, keepdims=True))
    l = jnp.zeros((1, TILE), jnp.float32)
    d = jnp.zeros((1, TILE), jnp.float32)
    for s, dp in raw:
        p = jnp.exp2(s - m)
        l = l + jnp.sum(p, axis=0, keepdims=True)
        d = d + jnp.sum(p * dp, axis=0, keepdims=True)
    return m, l, d


def put_stats(st_ref, qi, values):
    for r, value in enumerate(values):
        st_ref[qi, r : r + 1, :] = value


def add_stats(st_ref, qi, part, use):
    old = [st_ref[qi, r : r + 1, :] for r in range(3)]
    m = jnp.maximum(old[0], jnp.where(use, part[0], LOW))
    a, b = jnp.exp2(old[0] - m), jnp.where(use, jnp.exp2(part[0] - m), 0.0)
    put_stats(st_ref, qi, (m, old[1] * a + part[1] * b, old[2] * a + part[2] * b))


def near_half(docs, z, h, q_ref, do_ref, k_ref, v_ref, st_ref):
    _, lq = docs.case(z * 512)
    rk, _ = docs.case(z * 512 + 512)
    here = z * 512
    fore = jnp.where(jnp.logical_not(rk) & (z < ZN - 1), here, FAR)
    back = jnp.where(jnp.logical_not(lq) & (z > 0), here - 512, FAR)
    k, v = tile_rows(k_ref, 6 + h), tile_rows(v_ref, 6 + h)
    for i in range(4):
        first = (here, fore)[i // 2] + h * TILE
        part = part_stats(docs, tile_rows(q_ref, i), tile_rows(do_ref, i), here + i * TILE, [(k, v, first)], i < 2)
        add_stats(st_ref, i, part, True)
    keys = [(tile_rows(k_ref, j), tile_rows(v_ref, j), (here, back)[j // 2] + j % 2 * TILE) for j in range(4)]
    put_stats(st_ref, 6 + h, part_stats(docs, tile_rows(q_ref, 6 + h), tile_rows(do_ref, 6 + h), here + h * TILE, keys, True))


def late_half(docs, z, h, other, q_ref, do_ref, k_ref, v_ref, st_ref):
    lk, lq = docs.case(z * 512)
    rk, rq = docs.case(z * 512 + 512)
    lm, rm = jnp.logical_not(lk | lq), jnp.logical_not(rk | rq)
    q_ids, k_ids, _ = slots(docs, z)
    here, q2, k2 = z * 512, q_ids[2] * 512, k_ids[2] * 512
    q_ok, k_ok = q_ids[2] < ZN, k_ids[2] >= 0

    def start(use, pos, j):
        return jnp.where(use, pos, FAR) + j * TILE

    def pick(ref, use, one, other):
        return jnp.where(use, tile_rows(ref, one), tile_rows(ref, other))

    own = jnp.logical_not(rk) & q_ok
    both = ((lk & rm) | (rq & lm)) & q_ok & k_ok
    cross = (lk & jnp.logical_not(rk) & (z < ZN - 1) & k_ok) | (rq & jnp.logical_not(lq) & (z > 0) & q_ok)
    halves = [h] if other is None else [h, other]
    keys = [(pick(k_ref, rq, j, 6 + j), pick(v_ref, rq, j, 6 + j), start(own, here, j)) for j in range(2)]
    keys += [(tile_rows(k_ref, 4 + j), tile_rows(v_ref, 4 + j), start(both, k2, j)) for j in halves]
    put_stats(st_ref, 4 + h, part_stats(docs, tile_rows(q_ref, 4 + h), tile_rows(do_ref, 4 + h), q2 + h * TILE, keys))
    if other is not None:
        keys = [(tile_rows(k_ref, 4 + h), tile_rows(v_ref, 4 + h), start(both, k2, h))]
        part = part_stats(docs, tile_rows(q_ref, 4 + other), tile_rows(do_ref, 4 + other), q2 + other * TILE, keys)
        add_stats(st_ref, 4 + other, part, True)
    second = (tile_rows(k_ref, 4 + h), tile_rows(v_ref, 4 + h), start(jnp.logical_not(lq) & k_ok, k2, h))
    for i in range(2):
        part = part_stats(docs, pick(q_ref, lk, i, 6 + i), pick(do_ref, lk, i, 6 + i), here + i * TILE, [second])
        add_stats(st_ref, i, part, lk)
        add_stats(st_ref, 6 + i, part, lm)
    for i in range(2):
        key = (pick(k_ref, lk, 4 + h, 2 + i), pick(v_ref, lk, 4 + h, 2 + i),
               jnp.where(lk, start(cross, k2, h), start(cross, here - 512, i)))
        part = part_stats(docs, pick(q_ref, lk, 2 + i, 4 + h), pick(do_ref, lk, 2 + i, 4 + h),
                          jnp.where(lk, here + 512 + i * TILE, q2 + h * TILE), [key])
        add_stats(st_ref, 2 + i, part, lk)
        add_stats(st_ref, 4 + h, part, jnp.logical_not(lk))


def combine_stats(docs, z, mine, up1, up2, down1, down2):
    lk, lq = docs.case(z * 512)
    rk, rq = docs.case(z * 512 + 512)
    lm = jnp.logical_not(lk | lq)
    rm = jnp.logical_not(rk | rq)
    bk, bq = docs.case(z * 512 - 512)
    bm = jnp.logical_not(bk | bq) & (z >= 2)

    def part(ref, slot, use=None):
        m, l, d = (ref[2 * slot : 2 * slot + 2, r : r + 1, :] for r in range(3))
        if use is not None:
            m = jnp.where(use, m, LOW)
            l = jnp.where(use, l, 0.0)
            d = jnp.where(use, d, 0.0)
        return m, l, d

    groups = (
        (part(mine, 0), part(down1, 1, z >= 1), part(down2, 2, bm)),
        (part(mine, 1), part(up1, 0, z + 1 < ZN), part(down1, 2, lm & (z >= 1))),
        (part(mine, 2), part(up2, 0, rm & (z + 2 < ZN)), part(up1, 1, rm & (z + 1 < ZN)), part(up1, 3, rq & (z + 1 < ZN))),
        (part(mine, 3), part(down1, 2, lq & (z >= 1))),
    )
    out = []
    for parts in groups:
        m = functools.reduce(jnp.maximum, [p[0] for p in parts])
        l = sum(p[1] * jnp.exp2(p[0] - m) for p in parts)
        d = sum(p[2] * jnp.exp2(p[0] - m) for p in parts)
        some = l > 0.0
        l = jnp.where(some, l, 1.0)
        out.append((jnp.where(some, m + jnp.log2(l), -NEG), d / l))
    return out


def tile_grads(docs, tiles, q_ref, do_ref, k_ref, v_ref, stat, kt_ref):
    raw = []
    for qi, ki, q0, k0 in tiles:
        s = raw_scores(tile_rows(k_ref, ki), tile_rows(q_ref, qi))
        raw.append((s, raw_scores(tile_rows(v_ref, ki), tile_rows(do_ref, qi))))
    weights = []
    for (qi, ki, q0, k0), (s, dp) in zip(tiles, raw):
        p = jnp.exp2(masked(docs, s, q0, k0) - stat[qi, 0:1, :])
        weights.append((p.astype(jnp.bfloat16), (p * (dp - stat[qi, 1:2, :])).astype(jnp.bfloat16)))
    terms = []
    for (qi, ki, q0, k0), (p, ds) in zip(tiles, weights):
        terms.append((
            jnp.dot(p, tile_rows(do_ref, qi), preferred_element_type=jnp.float32),
            jnp.dot(ds, tile_rows(q_ref, qi), preferred_element_type=jnp.float32),
            jnp.dot(kt_ref[ki], ds, preferred_element_type=jnp.float32),
        ))
    return terms


def pack_pair(first, second):
    return jnp.concatenate([first[:64], second[:64], first[64:], second[64:]], axis=1)


def pack_query(dqt, q_out, half):
    dq = (dqt * SCALE).T.astype(jnp.bfloat16)
    for i in range(2):
        r = i * 128
        q_out[2 * half + i] = jnp.concatenate([dq[r + 32 * j : r + 32 * j + 32] for j in range(4)], axis=1)


def pack_keys(dk, dv, k_out, half):
    dk = (dk * SCALE).astype(jnp.bfloat16)
    dv = dv.astype(jnp.bfloat16)
    for i in range(2):
        r = i * 128
        k_out[2 * half + i] = pack_pair(dk[r : r + 128], dv[r : r + 128])


def grads_kernel(len_ref, q_ref, do_ref, k_ref, v_ref, stat, qp_ref, kp_ref, dqt, dk_acc, dv_acc, todo, kt_ref):
    z = lax.axis_index("seq") // XN
    docs = Docs(len_ref)
    for i in range(8):
        kt_ref[i] = k_ref[i * TILE : (i + 1) * TILE, :].T
    dqt[...] = jnp.zeros_like(dqt)
    dk_acc[...] = jnp.zeros_like(dk_acc)
    dv_acc[...] = jnp.zeros_like(dv_acc)

    def body(tiles):
        for (qi, ki, q0, k0), (dv, dk, dq) in zip(tiles, tile_grads(docs, tiles, q_ref, do_ref, k_ref, v_ref, stat, kt_ref)):
            dv_acc[ki] += dv
            dk_acc[ki] += dk
            dqt[qi] += dq

    for_groups(list_tiles(docs, z, todo, LATE), todo, body)
    for half in range(2):
        pack_query(dqt[4 + half], qp_ref, half)
        pack_keys(dk_acc[4 + half], dv_acc[4 + half], kp_ref, half)


def copy_to(src, dst, send, recv, device):
    return pltpu.make_async_remote_copy(
        src_ref=src,
        dst_ref=dst,
        send_sem=send,
        recv_sem=recv,
        device_id={"seq": device},
        device_id_type=pl.DeviceIdType.MESH,
    )


def meet(devices):
    for device in devices:
        pl.semaphore_signal(
            pltpu.get_barrier_semaphore(), inc=1, device_id={"seq": device}, device_id_type=pl.DeviceIdType.MESH
        )


def greet(devices):
    meet(devices)
    pl.semaphore_wait(pltpu.get_barrier_semaphore(), len(devices))


def window(ref, off):
    low = off // 128 * 128
    high = -(-(off + HEAD) // 128) * 128
    return ref[:, low:high][:, off - low : off - low + HEAD]


def place():
    me = lax.axis_index("seq")
    z, x = me // XN, me % XN
    up = lax.rem(z + 1, ZN) * XN + x
    down = lax.rem(z + ZN - 1, ZN) * XN + x
    peer = [z * XN + lax.rem(x + d, XN) for d in range(XN)]
    return z, x, up, down, peer


TYPES = (("q", 0), ("k", 1), ("q", 1), ("k", 0))


def gather_kernel(len_ref, raw, q_out, do_out, k_out, v_out, stat,
                  packed, own, q1, k1, qsel, ksel, q2, k2, mine, up1, up2, down1, down2,
                  x_send, x_recv, z_send, z_recv, s_send, s_recv):
    z, x, up, down, peer = place()
    low, top = z > 0, z < ZN - 1
    below, above = z > 1, z < ZN - 2
    upper = lax.rem(z + 2, ZN) * XN + x
    lower = lax.rem(z + ZN - 2, ZN) * XN + x
    meet(peer[1:])
    expected = jnp.int32(3)
    for use, to in ((low, down), (top, up), (below, lower), (above, upper)):
        pl.when(use)(functools.partial(meet, [to]))
        expected = expected + jnp.where(use, 1, 0)

    @pl.when(jnp.logical_not(top))
    def _():
        q1[...] = jnp.zeros_like(q1)
        q2[...] = jnp.zeros_like(q2)

    @pl.when(jnp.logical_not(low))
    def _():
        k1[...] = jnp.zeros_like(k1)
        k2[...] = jnp.zeros_like(k2)

    docs = Docs(len_ref)
    lk, lq = docs.case(z * 512)
    rk, rq = docs.case(z * 512 + 512)

    def pack(t, xp):
        kind, head = TYPES[t]
        i = 0 if kind == "q" else 2
        off = (2 * xp + head) * HEAD
        packed[t, xp] = pack_pair(window(raw.at[i], off), window(raw.at[i + 1], off))

    def x_copy(t, d):
        to = lax.rem(x + d, XN)
        return copy_to(packed.at[t, to], own.at[t, x], x_send.at[t, d - 1], x_recv.at[t, d - 1], peer[d])

    def z_copy(i, c):
        src, dst, to = ((own.at[0, c], q1.at[c], down), (own.at[1, c], k1.at[c], up),
                        (qsel.at[c], q2.at[c], down), (ksel.at[c], k2.at[c], up))[i]
        return copy_to(src, dst, z_send.at[i, c], z_recv.at[i, c], to)

    def z_start(i, c):
        pl.when((low, top)[i % 2])(lambda: z_copy(i, c).start())

    def z_got(i, c):
        pl.when((top, low)[i % 2])(lambda: z_copy(i, c).wait_recv())

    def unpack(value, slot, c, first, second):
        row = slot * 512 + c * 128
        upper = pl.ds(pl.multiple_of(row, 64), 64)
        lower = pl.ds(pl.multiple_of(row + 64, 64), 64)
        first[upper, :] = value[:, 0:HEAD]
        second[upper, :] = value[:, HEAD : 2 * HEAD]
        first[lower, :] = value[:, 2 * HEAD : 3 * HEAD]
        second[lower, :] = value[:, 3 * HEAD : 4 * HEAD]

    def source(d):
        return lax.rem(x + d, XN)

    def got_x(t, d):
        back = XN - d
        copy_to(packed.at[t, x], own.at[t, source(d)], x_send.at[t, back - 1], x_recv.at[t, back - 1], peer[1]).wait_recv()

    def second(i, c):
        z_got(i - 2, c)
        if i == 2:
            qsel[c] = jnp.where(lq, own[2, c], q1[c])
        else:
            ksel[c] = jnp.where(rk, own[3, c], k1[c])
        z_start(i, c)

    def first(t, d):
        got_x(t, d)
        z_start(t, source(d))

    def unpack_own(t, c):
        unpack(own[t, c], *((0, c, q_out, do_out), (0, c, k_out, v_out), (3, c, q_out, do_out), (3, c, k_out, v_out))[t])

    for xp in range(XN):
        pack(0, xp)
    own[0, x] = packed[0, x]
    pl.semaphore_wait(pltpu.get_barrier_semaphore(), expected)
    for d in (1, 3):
        x_copy(0, d).start()
    z_start(0, x)
    for xp in range(XN):
        pack(1, xp)
    own[1, x] = packed[1, x]
    for d in (1, 3):
        x_copy(1, d).start()
    z_start(1, x)
    for t in (0, 1):
        x_copy(t, 2).start()
    for t in (2, 3):
        for xp in range(XN):
            pack(t, xp)
        own[t, x] = packed[t, x]
    second(2, x)
    second(3, x)
    unpack_own(0, x)
    unpack_own(1, x)
    first(0, 1)
    first(0, 3)
    first(1, 1)
    first(1, 3)
    for d in (1, 3):
        x_copy(2, d).start()
        x_copy(3, d).start()
    unpack_own(2, x)
    unpack_own(3, x)
    for t in (0, 1):
        unpack_own(t, source(1))
        unpack_own(t, source(3))
    first(0, 2)
    first(1, 2)
    unpack(q1[x], 1, x, q_out, do_out)
    unpack(k1[x], 1, x, k_out, v_out)
    for t in (0, 1):
        unpack_own(t, source(2))
    def pass_on(i, c):
        if i == 2:
            qsel[c] = jnp.where(lq, own[2, c], q1[c])
        else:
            ksel[c] = jnp.where(rk, own[3, c], k1[c])
        z_start(i, c)

    def unpack_first(c):
        unpack(q1[c], 1, c, q_out, do_out)
        unpack(k1[c], 1, c, k_out, v_out)

    def unpack_second(c):
        z_got(2, c)
        unpack(q2[c], 2, c, q_out, do_out)
        z_got(3, c)
        unpack(k2[c], 2, c, k_out, v_out)

    for i in (0, 1, 2, 3):
        put_stats(mine, i, (jnp.full((1, TILE), LOW, jnp.float32),) + (jnp.zeros((1, TILE), jnp.float32),) * 2)
    arrays = (q_out, do_out, k_out, v_out, mine)
    half = x // 2
    step = 1 + 2 * lax.rem(x, 2)
    steps = (step, XN - step, 2)
    mate = source(step)
    for t in (2, 3):
        got_x(t, step)
        z_got(t - 2, mate)
        pass_on(t, mate)
        x_copy(t, 2).start()
        unpack_own(t, mate)
    unpack_first(mate)
    for d in steps[1:]:
        z_got(0, source(d))
        z_got(1, source(d))
        unpack_first(source(d))
    near_half(docs, z, half, *arrays)
    for d in steps[1:]:
        for t in (2, 3):
            got_x(t, d)
            pass_on(t, source(d))
            unpack_own(t, source(d))
    near_half(docs, z, 1 - half, *arrays)
    unpack_second(x)
    unpack_second(mate)
    late_half(docs, z, half, None, *arrays)
    for d in steps[1:]:
        unpack_second(source(d))
    late_half(docs, z, 1 - half, half, *arrays)
    shares = []
    for i, (ref, tiles, to, sent, got) in enumerate((
        (up1, (0, 8), down, low, top),
        (down1, (2, 4), up, top, low),
        (up2, (0, 2), lower, below, above),
        (down2, (4, 2), upper, above, below),
    )):
        part = pl.ds(*tiles)
        shares.append((copy_to(mine.at[part], ref.at[part], s_send.at[i], s_recv.at[i], to), sent, got))
    for copy, sent, got in shares:
        pl.when(sent)(copy.start)
    for copy, sent, got in shares:
        pl.when(got)(copy.wait_recv)
    for qs, values in enumerate(combine_stats(docs, z, mine, up1, up2, down1, down2)):
        for r, value in enumerate(values):
            stat[2 * qs : 2 * qs + 2, r : r + 1, :] = value
    for copy, sent, got in shares:
        pl.when(sent)(copy.wait_send)
    for t in range(4):
        for d in (1, 2, 3):
            x_copy(t, d).wait_send()
    for t in range(4):
        for c in range(XN):
            pl.when((low, top)[t % 2])(z_copy(t, c).wait_send)


def scatter_kernel(len_ref, q_ref, do_ref, k_ref, v_ref, stat, dqt, dk_acc, dv_acc, qp, kp, qhome, khome,
                   kt_ref, ownq, ownk, q1p, k1p, rq2, rk2, rq1, rk1, qs, ks, qfin, kfin,
                   z_send, z_recv, x_send, x_recv):
    z, x, up, down, peer = place()
    docs = Docs(len_ref)
    lk, lq = docs.case(z * 512)
    rk, rq = docs.case(z * 512 + 512)
    low, top = z >= 1, z < ZN - 1
    lm = jnp.logical_not(lk | lq) & low
    rm = jnp.logical_not(rk | rq) & top
    lq, rk = lq & low, rk & top

    def z_start(i, c):
        pl.when((top, low)[i % 2])(lambda: z_copy(i, c).start())

    def z_got(i, c):
        pl.when((low, top)[i % 2])(lambda: z_copy(i, c).wait_recv())

    def z_copy(i, c):
        src, dst, to = ((qp.at[c], rq2.at[c], up), (kp.at[c], rk2.at[c], down),
                        (qs.at[c], rq1.at[c], up), (ks.at[c], rk1.at[c], down))[i]
        return copy_to(src, dst, z_send.at[i, c], z_recv.at[i, c], to)

    def plus(a, b, use):
        return (a.astype(jnp.float32) + jnp.where(use, b.astype(jnp.float32), 0.0)).astype(jnp.bfloat16)

    def dest(d):
        return lax.rem(x + d, XN)

    def x_copy(kind, head, d):
        src, dst = ((qfin, qhome), (kfin, khome))[kind]
        i = 2 * kind + head
        return copy_to(src.at[head, dest(d)], dst.at[head, x], x_send.at[i, d - 1], x_recv.at[i, d - 1], peer[d])

    def send_home(kind, head, d, value):
        src, dst = ((qfin, qhome), (kfin, khome))[kind]
        if d:
            src[head, dest(d)] = value
            x_copy(kind, head, d).start()
        else:
            dst[head, x] = value

    order = (2, 1, 3, 0)
    meet(peer[1:])
    pl.when(low)(lambda: meet([down]))
    pl.when(top)(lambda: meet([up]))
    pl.semaphore_wait(pltpu.get_barrier_semaphore(), 3 + jnp.where(low, 1, 0) + jnp.where(top, 1, 0))
    def second(d):
        z_start(1, dest(d))
        z_start(0, dest(d))

    for d in order:
        z_start(1, dest(d))
    for d in order:
        z_start(0, dest(d))

    def near_grads(head):
        tiles = [tile for tile in near_tiles(docs, z) if (tile[0] >= 6) == bool(head)]
        for ki in (range(4), (6, 7))[1 - head]:
            kt_ref[ki] = tile_rows(k_ref, ki).T
        pairs = [(qi, ki, q0, k0) for qi, q0, keys in tiles for ki, k0 in keys]
        terms = tile_grads(docs, pairs, q_ref, do_ref, k_ref, v_ref, stat, kt_ref)
        for qi in sorted({p[0] for p in pairs}):
            dq = dqt[qi] + sum(t[2] for p, t in zip(pairs, terms) if p[0] == qi)
            pack_query(dq, (ownq.at[0], q1p, None, ownq.at[1])[qi // 2], qi % 2)
        for ki in sorted({p[1] for p in pairs}):
            dk = dk_acc[ki] + sum(t[1] for p, t in zip(pairs, terms) if p[1] == ki)
            dv = dv_acc[ki] + sum(t[0] for p, t in zip(pairs, terms) if p[1] == ki)
            pack_keys(dk, dv, (ownk.at[1], k1p, None, ownk.at[0])[ki // 2], ki % 2)

    def key_home(d):
        c = dest(d)
        z_got(1, c)
        send_home(1, 0, d, plus(ownk[0, c], rk2[c], rk))

    near_grads(0)
    for d in order:
        c = dest(d)
        z_got(0, c)
        qs[c] = plus(q1p[c], rq2[c], lm)
        z_start(2, c)
    key_home(order[0])
    key_home(order[1])
    near_grads(1)
    for n, d in enumerate(order):
        c = dest(d)
        if n >= 2:
            key_home(d)
        ks[c] = plus(k1p[c], rk2[c], rm)
        z_start(3, c)
        send_home(0, 1, d, plus(ownq[1, c], rq2[c], lq))
    for d in order:
        c = dest(d)
        z_got(2, c)
        send_home(0, 0, d, plus(ownq[0, c], rq1[c], low))
    for d in order:
        c = dest(d)
        z_got(3, c)
        send_home(1, 1, d, plus(ownk[1, c], rk1[c], top))
    for i in range(4):
        for d in (1, 2, 3):
            x_copy(i // 2, i % 2, d).wait_recv()
    for i in range(4):
        for c in range(XN):
            pl.when((top, low)[i % 2])(z_copy(i, c).wait_send)
        for d in (1, 2, 3):
            x_copy(i // 2, i % 2, d).wait_send()


def unpack_kernel(qhome, khome, dq_out, dk_out, dv_out, stage, sem):
    copies = []
    for i, (a, out, n) in enumerate(((0, dq_out, 4), (0, dk_out, 2), (1, dv_out, 2))):
        home = qhome if n == 4 else khome
        step = 128 // n
        for part in range(n):
            lanes = (part if n == 4 else 2 * part + a) * HEAD
            pieces = []
            for xs in range(XN):
                for head in range(2):
                    pieces.append(home[head, xs][:, lanes : lanes + HEAD])
            stage[i, part * step : (part + 1) * step, :] = jnp.concatenate(pieces, axis=1)
        copies.append(pltpu.make_async_copy(stage.at[i], out, sem.at[i]))
        copies[-1].start()
    for copy in copies:
        copy.wait()


VM = pl.BlockSpec(memory_space=pltpu.VMEM)
SM = pl.BlockSpec(memory_space=pltpu.SMEM)
LIMIT = 26 * 1024 * 1024
BIG = pltpu.CompilerParams(vmem_limit_bytes=LIMIT)
HB = pl.BlockSpec(memory_space=pltpu.HBM)
DMA = pltpu.SemaphoreType.DMA


def remote(number, limit=26):
    return pltpu.CompilerParams(vmem_limit_bytes=limit * 1024 * 1024, collective_id=number, has_side_effects=True)


def buf(*shape, dtype=jnp.bfloat16):
    return pltpu.VMEM(shape, dtype)


def out(*shape, dtype=jnp.bfloat16):
    return jax.ShapeDtypeStruct(shape, dtype)


def shards(queries, key_vectors, value_vectors, out_grad, doc_lengths):
    rows, width = queries.shape[1], queries.shape[2]
    chunk = (XN, 64, 4 * HEAD)
    small = (XN, 32, 4 * HEAD)
    block = out(2048, HEAD)
    stat = out(8, 4, TILE, dtype=jnp.float32)
    todo = pltpu.SMEM((4, 64), jnp.int32)
    qs, dos, ks, vs, stats = pl.pallas_call(
        gather_kernel,
        out_shape=(block,) * 4 + (stat,),
        name="gather",
        in_specs=[SM, VM],
        out_specs=(VM,) * 5,
        scratch_shapes=[buf(4, *chunk), buf(4, *chunk)] + [buf(*chunk)] * 6
        + [buf(8, 4, TILE, dtype=jnp.float32)] * 5
        + [DMA((4, 3)), DMA((4, 3)), DMA((4, 4)), DMA((4, 4)), DMA((4,)), DMA((4,))],
        compiler_params=remote(0),
    )(doc_lengths, jnp.concatenate([queries, out_grad, key_vectors, value_vectors]))
    acc = out(8, TILE, HEAD, dtype=jnp.float32)
    qp, kp, *partial = pl.pallas_call(
        grads_kernel,
        name="grads",
        out_shape=(out(*small), out(*chunk), out(8, HEAD, TILE, dtype=jnp.float32), acc, acc),
        in_specs=[SM] + [VM] * 5,
        out_specs=(VM,) * 5,
        scratch_shapes=[todo, buf(8, HEAD, TILE)],
        compiler_params=BIG,
    )(doc_lengths, qs, dos, ks, vs, stats)
    home = pl.pallas_call(
        scatter_kernel,
        name="scatter",
        out_shape=(out(2, *small), out(2, *chunk)),
        in_specs=[SM] + [VM] * 10,
        out_specs=(VM,) * 2,
        scratch_shapes=[buf(8, HEAD, TILE), buf(2, *small), buf(2, *chunk), buf(*small), buf(*chunk),
                        buf(*small), buf(*chunk), buf(*small), buf(*chunk), buf(*small), buf(*chunk),
                        buf(2, *small), buf(2, *chunk),
                        DMA((4, 4)), DMA((4, 4)), DMA((4, 3)), DMA((4, 3))],
        compiler_params=remote(2),
    )(doc_lengths, qs, dos, ks, vs, stats, *partial, qp, kp)
    full = out(rows, width)
    grads = pl.pallas_call(
        unpack_kernel,
        name="unpack",
        out_shape=(full,) * 3,
        in_specs=[VM, VM],
        out_specs=(HB,) * 3,
        scratch_shapes=[buf(3, rows, width), DMA((3,))],
        compiler_params=BIG,
    )(*home)
    return tuple(g[None] for g in grads)


def solution(mesh):
    spec = P("section", "seq", "dp")
    return jax.shard_map(
        shards,
        mesh=mesh,
        in_specs=(spec, spec, spec, spec, P()),
        out_specs=(spec, spec, spec),
        check_vma=False,
    )
```
